128 devices in a mesh: dp: 8 (over y_lo, z), gene: 16 (over x, y_hi, core).
Axes of the slice: x: 4, y: 4 (y_hi: 2, y_lo: 2; y = y_hi * 2 + y_lo), z: 4, core: 2. Of those that a mesh axis runs over, the one named last changes fastest.
Arguments:
- y_pool: bfloat16 [8192, 16384], P('dp', 'gene'), may hold values from -40 to 40
- cell_index: int32 [2048], P('dp'), may hold values from 0 to 8191, as said below
- latent_mean: float32 [32, 2048], P(None, 'dp'), may hold values from -4 to 4
- latent_logvar: float32 [32, 2048], P(None, 'dp'), may hold values from -3 to 0.5
- inducing: float32 [32, 1024], replicated, may hold values from -4 to 4
- length_sq: float32 [32], replicated, may hold values from 8 to 64
- log_var: float32 [1], replicated, may hold values from -0.5 to 0.5
- log_beta: float32 [1], replicated, may hold values from -0.5 to 0.5
- proj_mean: float32 [1024, 16384], P(None, 'gene'), may hold values from -0.0625 to 0.0625
- second_moment: float32 [1024, 1024], P('gene'), may hold values from -0.3 to 0.3
Outputs:
- grad_latent: float32 [2, 32, 2048], P(None, None, 'dp')
- grad_proj: float32 [1024, 16384], P('dp', 'gene')
- grad_logbeta: float32 [1], replicated
The draws below stay inside these ranges and needn't reach their ends.
Inputs may be any that keep to these rules, and one draw needn't show every extreme that they name: The 256 entries of each aligned block of cell_index are distinct rows of the matching aligned block of 1024 rows of y_pool; each block names that block's first and last row.
All inputs are finite; a program needn't handle non-finite values.
Results may differ from the reference program's by a relative error of at most 0.0049.
Values may be sent and summed in bfloat16 or wider, within the bound.
A program may use at most 64 MiB of HBM per device.

```python
import math
import jax
import jax.numpy as jnp
from jax import lax

LATENT = 32
INDUCING = 1024
GENES = 16384
CELL_DEV = 256
CELL_BLOCK = 32
BATCH = 2048
POOL = 8192


def draw_y_pool(key, part):
    key = jax.random.fold_in(key, 11)
    key_cell, key_gene, key_noise = jax.random.split(key, 3)
    cell_scale = jnp.exp(jax.random.uniform(key_cell, (POOL, 1), jnp.float32, math.log(0.4), math.log(4.0)))
    gene_place = jnp.arange(GENES, dtype=jnp.float32) / GENES
    gene_scale = jnp.exp(jax.random.uniform(key_gene, (1, GENES), jnp.float32, math.log(0.4), math.log(4.0))) * jnp.sqrt(1.0 + 2.0 * gene_place)[None, :]
    noise_part = jnp.clip(jax.random.normal(key_noise, (POOL, GENES), jnp.float32), -3.0, 3.0)
    return jnp.clip(cell_scale * gene_scale * noise_part, -40.0, 40.0).astype(jnp.bfloat16)


def draw_cell_index(key, part):
    key = jax.random.fold_in(key, 23)
    blocks = BATCH // CELL_DEV
    pool_block = POOL // blocks

    def draw_block(block_id):
        block_key = jax.random.fold_in(key, block_id)
        key_pick, key_shuffle = jax.random.split(block_key)
        middle = jax.random.permutation(key_pick, pool_block - 2)[:CELL_DEV - 2].astype(jnp.int32) + 1
        picked = jnp.concatenate([jnp.array([0, pool_block - 1], jnp.int32), middle])
        shuffle = jax.random.permutation(key_shuffle, CELL_DEV)
        return picked[shuffle] + block_id * pool_block
    return jax.vmap(draw_block)(jnp.arange(blocks, dtype=jnp.int32)).reshape(BATCH).astype(jnp.int32)


def raised(drawn, own_key, source, target, blocks, factor):
    def block_of(position):
        return (jnp.arange(drawn.shape[position]) // (drawn.shape[position] // blocks)).reshape((-1,) + (1,) * (drawn.ndim - 1 - position))

    one_side = jax.random.permutation(own_key, blocks)[block_of(target)]
    other_side = (block_of(target) + blocks // 2) % blocks
    return jnp.where((block_of(source) == one_side) | (block_of(source) == other_side), factor * drawn, drawn)


def block_scale(stream_key, dims, cuts, smallest, high):
    factor_of = 1.0
    for dim, shards_of in cuts:
        heights = jax.random.uniform(jax.random.fold_in(jax.random.fold_in(stream_key, 6), dim), (shards_of,), jnp.float32, smallest / len(cuts), high / len(cuts))
        factor_of = factor_of * jnp.repeat(jnp.exp(heights), dims[dim] // shards_of).reshape((-1,) + (1,) * (len(dims) - 1 - dim))
    return factor_of


def bell_draw(rng, shape, width, bound, cuts=(), kind=jnp.bfloat16):
    values = jax.random.normal(rng, shape, jnp.float32) * width
    if len(cuts) > 0:
        values = block_scale(rng, shape, cuts, -0.22, 0.18) * values
    return jnp.clip(values, min=-bound, max=bound).astype(kind)


def noise_with(stream_key, dims, scale, limit, pieces, heavy, held_as=jnp.bfloat16):
    values = scale * jax.random.normal(stream_key, dims, jnp.float32)
    if pieces:
        values = values * block_scale(stream_key, dims, pieces, -0.22, 0.18)
    return jnp.clip(raised(values, jax.random.fold_in(stream_key, 3), *heavy), -limit, limit).astype(held_as)


def setup_inputs(seed: int = 0) -> dict:
    key_of = jax.random.split(jax.random.key(seed), 11)
    return {
        "y_pool": draw_y_pool(jax.random.fold_in(key_of[10], 71), 0),
        "cell_index": draw_cell_index(jax.random.fold_in(key_of[10], 71), 0),
        "latent_mean": bell_draw(key_of[2], (LATENT, BATCH), 1.0, 4.0, ((1, 8),), jnp.float32),
        "latent_logvar": jnp.clip(-3.0 + 3.5 * jax.random.uniform(key_of[3], (LATENT, BATCH), jnp.float32) ** block_scale(key_of[3], (LATENT, BATCH), ((1, 8),), -0.2, 0.2), -3.0, 0.5),
        "inducing": bell_draw(key_of[4], (LATENT, INDUCING), 1.0, 4.0, (), jnp.float32),
        "length_sq": jnp.clip(jnp.exp(jax.random.uniform(key_of[5], (LATENT,), jnp.float32, math.log(8.0), math.log(64.0))), 8.0, 64.0),
        "log_var": jnp.clip(jax.random.uniform(key_of[6], (1,), jnp.float32, -0.5, 0.5), -0.5, 0.5),
        "log_beta": jnp.clip(jax.random.uniform(key_of[7], (1,), jnp.float32, -0.5, 0.5), -0.5, 0.5),
        "proj_mean": noise_with(key_of[8], (INDUCING, GENES), GENES ** -0.5, 0.0625, ((1, 16),), (1, 0, 16, 2.0), jnp.float32),
        "second_moment": bell_draw(key_of[9], (INDUCING, INDUCING), 0.05, 0.3, ((0, 16),), jnp.float32),
    }


def psi_first(mean_arg, logvar_arg, inducing, length_sq, kernel_log):
    spread = length_sq[:, None] + jnp.exp(logvar_arg)
    inverse = 1.0 / spread
    quad_first = jnp.dot((inducing * inducing).T, inverse, precision=lax.Precision.HIGHEST)
    quad_cross = jnp.dot(inducing.T, mean_arg * inverse, precision=lax.Precision.HIGHEST)
    quad_last = lax.optimization_barrier(jnp.sum(mean_arg * mean_arg * inverse, axis=0))
    prefix = kernel_log + 0.5 * lax.optimization_barrier(jnp.sum(jnp.log(length_sq[:, None] * inverse), axis=0))
    return jnp.exp(prefix[None, :] - 0.5 * (quad_first - 2.0 * quad_cross + quad_last[None, :]))

def pair_log(rows_z, inducing, length_sq):
    factor = 0.5 / jnp.sqrt(length_sq)
    left_side = rows_z * factor[:, None]
    right_side = inducing * factor[:, None]
    cross_prod = jnp.dot(left_side.T, right_side, precision=lax.Precision.HIGHEST)
    return 2.0 * cross_prod - lax.optimization_barrier(jnp.sum(left_side * left_side, axis=0))[:, None] - lax.optimization_barrier(jnp.sum(right_side * right_side, axis=0))[None, :]

def cell_block_value(mean_slice, logvar_slice, rows_z, inducing, length_sq, kernel_log, pair_term, weight):
    cell_width = length_sq[:, None] + 2.0 * jnp.exp(logvar_slice)
    root_width = jnp.sqrt(2.0 * cell_width)
    left_side = (rows_z[None, :, :] - mean_slice.T[:, :, None]) / root_width.T[:, :, None]
    right_side = (inducing[None, :, :] - mean_slice.T[:, :, None]) / root_width.T[:, :, None]
    inner_prod = jnp.einsum('bqr,bqm->brm', left_side, right_side, precision=lax.Precision.HIGHEST)
    exponent = -(0.5 * lax.optimization_barrier(jnp.sum(left_side * left_side, axis=1))[:, :, None] + 0.5 * lax.optimization_barrier(jnp.sum(right_side * right_side, axis=1))[:, None, :] + inner_prod)
    prefix = 2.0 * kernel_log + 0.5 * lax.optimization_barrier(jnp.sum(jnp.log(length_sq[:, None] / cell_width), axis=0))
    cells_psi = jnp.exp(prefix[:, None, None] + pair_term[None, :, :] + exponent)
    block_value = jnp.sum(cells_psi * weight[None, :, :])
    return (block_value, lax.optimization_barrier(jnp.sum(cells_psi, axis=0)))

def cell_scan(latent_mean, latent_logvar, rows_z, inducing, length_sq, kernel_log, pair_term, weight, block_size):
    latent_dims, cell_count = latent_mean.shape
    step_count = cell_count // block_size
    mean_blocks = latent_mean.reshape(latent_dims, step_count, block_size).transpose(1, 0, 2)
    logvar_blocks = latent_logvar.reshape(latent_dims, step_count, block_size).transpose(1, 0, 2)
    value_grad = jax.value_and_grad(cell_block_value, argnums=(0, 1), has_aux=True)

    def scan_step(running, slices):
        (block_value, psi_sum), grad_pair = value_grad(slices[0], slices[1], rows_z, inducing, length_sq, kernel_log, pair_term, weight)
        return ((running[0] + psi_sum, running[1] + block_value), grad_pair)
    start_state = (jnp.zeros((rows_z.shape[1], inducing.shape[1]), jnp.float32), jnp.zeros((), jnp.float32))
    (psi_sum, trace_sum), (grad_mean, grad_logvar) = lax.scan(scan_step, start_state, (mean_blocks, logvar_blocks))
    grad_mean = grad_mean.transpose(1, 0, 2).reshape(latent_dims, cell_count)
    grad_logvar = grad_logvar.transpose(1, 0, 2).reshape(latent_dims, cell_count)
    return (psi_sum, grad_mean, grad_logvar, trace_sum)

def reference(y_pool, cell_index, latent_mean, latent_logvar, inducing, length_sq, log_var, log_beta, proj_mean, second_moment):
    cell_rows = jnp.take(y_pool, cell_index, axis=0)
    noise_prec = jnp.exp(log_beta[0])
    kernel_log = log_var[0]

    def first_stat(mean_arg, logvar_arg):
        return psi_first(mean_arg, logvar_arg, inducing, length_sq, kernel_log)
    psi_one, pull_back = jax.vjp(first_stat, latent_mean, latent_logvar)
    proj_low = proj_mean.astype(jnp.bfloat16)
    cross_term = jnp.dot(proj_low, cell_rows.T, preferred_element_type=jnp.float32)
    second = jnp.dot(proj_low, proj_low.T, preferred_element_type=jnp.float32) + second_moment
    pair_term = pair_log(inducing, inducing, length_sq)
    group_count = BATCH // CELL_DEV
    stat_part = jnp.zeros((INDUCING, GENES), jnp.float32)
    trace_sum = jnp.zeros((), jnp.float32)
    mean_pieces = []
    logvar_pieces = []
    for group in range(group_count):
        mean_group = latent_mean[:, group * CELL_DEV:(group + 1) * CELL_DEV]
        logvar_group = latent_logvar[:, group * CELL_DEV:(group + 1) * CELL_DEV]
        psi_group, grad_mean_group, grad_logvar_group, trace_group = cell_scan(mean_group, logvar_group, inducing, inducing, length_sq, kernel_log, pair_term, second, CELL_BLOCK)
        psi_part = psi_group.astype(jnp.bfloat16)
        stat_part = stat_part + jnp.dot(psi_part, proj_low, preferred_element_type=jnp.float32)
        trace_sum = trace_sum + trace_group
        mean_pieces.append(grad_mean_group)
        logvar_pieces.append(grad_logvar_group)
    grad_mean_two = jnp.concatenate(mean_pieces, axis=1)
    grad_logvar_two = jnp.concatenate(logvar_pieces, axis=1)
    grad_mean_one, grad_logvar_one = pull_back(noise_prec * cross_term)
    variance = jnp.exp(latent_logvar)
    grad_latent = jnp.stack([noise_prec * grad_mean_one - 0.5 * noise_prec * grad_mean_two - latent_mean, noise_prec * grad_logvar_one - 0.5 * noise_prec * grad_logvar_two - 0.5 * (variance - 1.0)])
    psi_low = psi_one.astype(jnp.bfloat16)
    data_part = jnp.dot(psi_low, cell_rows, preferred_element_type=jnp.float32)
    grad_proj = noise_prec / BATCH * (data_part - stat_part)
    total_cross = jnp.sum(psi_one * cross_term)
    total_square = jnp.sum(jnp.square(cell_rows.astype(jnp.float32)))
    grad_logbeta = noise_prec / (BATCH * GENES) * (total_cross - 0.5 * total_square - 0.5 * trace_sum) - 0.5 * noise_prec * jnp.exp(kernel_log) + 0.5
    return (grad_latent, grad_proj, grad_logbeta.reshape(1))
```

```python
import functools

import jax
import jax.numpy as jnp
from jax import lax
from jax.experimental import pallas as pl
from jax.experimental.pallas import tpu as pltpu
from jax.sharding import PartitionSpec as P

F32 = jnp.float32
BF16 = jnp.bfloat16
LOG2E = 1.4426950408889634
MESH = pl.DeviceIdType.MESH

DP = 8
GENE = 16
CELLS = 256
LAT = 32
IND = 1024
GENES = 1024
BLOCK = IND // DP
ROWS = BLOCK // GENE
SPAN = 5
WIDTH = SPAN * BLOCK
STEPS = 4
PAIRS = ROWS * WIDTH // STEPS
DEPTH = 256
USED = 208
BLOCK_WEIGHT = (1.0, 2.0, 2.0, 2.0, 1.0)


def each(count, body):
    def step(k, carry):
        body(k)
        return carry

    lax.fori_loop(0, count, step, 0)


def split_two(value):
    high = value.astype(BF16).astype(F32)
    return high, (value - high).astype(BF16).astype(F32)


def split_three(value):
    high = value.astype(BF16).astype(F32)
    rest = value - high
    mid = rest.astype(BF16).astype(F32)
    return high, mid, (rest - mid).astype(BF16).astype(F32)


def special(rows, width):
    place = lax.broadcasted_iota(jnp.int32, (64, width), 0)
    total = jnp.zeros((64, width), F32)
    for at, row in enumerate(rows):
        total = jnp.where(place == at, jnp.broadcast_to(row, (64, width)), total)
    return total


def point_features(value, extra):
    width = value.shape[1]
    high, low = split_two(value)
    square_high, square_low = split_two(value * value)
    ones = jnp.ones((1, width), F32)
    rows = [ones, ones, ones] + list(extra)
    return jnp.concatenate(
        [high, square_high, low, square_low, high, square_high, special(rows, width)], axis=0
    )


def cell_coefficients(linear, square, constant, extra):
    width = linear.shape[1]
    high, low = split_two(linear)
    square_high, square_low = split_two(square)
    rows = list(split_three(constant)) + [jnp.ones((1, width), F32)] * extra
    return jnp.concatenate(
        [high, square_high, high, square_high, low, square_low, special(rows, width)], axis=0
    )


def moments(table):
    return table[192:193], table[0:32] + table[64:96], table[32:64] + table[96:128]


def dot(left, right, left_dim, right_dim):
    return lax.dot_general(
        left, right, (((left_dim,), (right_dim,)), ((), ())), preferred_element_type=F32
    )


def kernel(
    y_hbm,
    index_ref,
    mean_ref,
    logvar_ref,
    inducing_ref,
    length_ref,
    log_var_ref,
    log_beta_ref,
    proj_hbm,
    moment_ref,
    latent_out,
    proj_out,
    total_out,
    proj_f32,
    proj_low,
    y_ref,
    cell_ref,
    psi_low_ref,
    lat_all,
    gram_send,
    gram_recv,
    data_send,
    data_recv,
    data_own,
    pair_feat,
    cell_coef,
    inv_width,
    weight_ref,
    psi_acc,
    first_ref,
    trace_ref,
    grad_send,
    grad_recv,
    psi_send,
    psi_recv,
    part_send,
    part_recv,
    sum_all,
    block_send,
    block_recv,
    total_recv,
    local_sem,
    dp_sems,
    gene_sems,
):
    d = lax.axis_index("dp")
    g = lax.axis_index("gene")

    def remote(src, dst, axis, send_sem, recv_sem, peer):
        return pltpu.make_async_remote_copy(
            src_ref=src,
            dst_ref=dst,
            send_sem=send_sem,
            recv_sem=recv_sem,
            device_id={axis: peer},
            device_id_type=MESH,
        )

    def dp_peer(k):
        return lax.rem(d + 1 + k, DP)

    def gene_peer(k):
        return lax.rem(g + 1 + k, GENE)

    def dp_copy(kind, src, dst, peer, slot):
        return remote(src, dst, "dp", dp_sems.at[kind, 0, peer], dp_sems.at[kind, 1, slot], peer)

    def gene_copy(kind, src, dst, peer, slot):
        return remote(
            src, dst, "gene", gene_sems.at[kind, 0, peer], gene_sems.at[kind, 1, slot], peer
        )

    quarter = IND // 4
    proj_copies = [
        pltpu.make_async_copy(
            proj_hbm.at[pl.ds(quarter * k, quarter)],
            proj_f32.at[pl.ds(quarter * k, quarter)],
            local_sem.at[k],
        )
        for k in range(4)
    ]
    y_copy = pltpu.make_async_copy(y_hbm, y_ref, local_sem.at[4])
    for copy in proj_copies:
        copy.start()
    y_copy.start()

    barrier = pltpu.get_barrier_semaphore()
    each(
        DP - 1,
        lambda k: pl.semaphore_signal(
            barrier, inc=1, device_id={"dp": dp_peer(k)}, device_id_type=MESH
        ),
    )
    each(
        GENE - 1,
        lambda k: pl.semaphore_signal(
            barrier, inc=1, device_id={"gene": gene_peer(k)}, device_id_type=MESH
        ),
    )
    lat_all[d, 0:LAT] = mean_ref[...]
    lat_all[d, LAT : 2 * LAT] = logvar_ref[...]
    pl.semaphore_wait(barrier, DP + GENE - 2)

    def latent_copy(peer, slot):
        return dp_copy(0, lat_all.at[d], lat_all.at[slot], peer, slot)

    each(DP - 1, lambda k: latent_copy(dp_peer(k), d).start())

    for k in range(4):
        proj_copies[k].wait()
        proj_low[quarter * k : quarter * (k + 1)] = proj_f32[
            quarter * k : quarter * (k + 1)
        ].astype(BF16)

    own_rows = proj_low[pl.ds(pl.multiple_of(BLOCK * d, BLOCK), BLOCK)]
    row_of = lax.broadcasted_iota(jnp.int32, (BLOCK, 64), 0) + BLOCK * d
    col_of = lax.broadcasted_iota(jnp.int32, (BLOCK, 64), 1) + 64 * g
    pick_rows = jnp.where(row_of == col_of, 1.0, 0.0).astype(BF16)
    moment_cols = moment_ref[:, pl.ds(pl.multiple_of(BLOCK * d, BLOCK), BLOCK)].astype(BF16)
    for o in range(SPAN):
        at = lax.rem(d + o, DP)
        start = pl.multiple_of(BLOCK * at, BLOCK)
        gram = dot(own_rows, proj_low[pl.ds(start, BLOCK)], 1, 1)
        moment_rows = dot(pick_rows, moment_ref[:, pl.ds(start, BLOCK)].astype(BF16), 1, 0)
        place_row = lax.broadcasted_iota(jnp.int32, (64, BLOCK), 0) + 64 * g
        place_col = lax.broadcasted_iota(jnp.int32, (64, BLOCK), 1) + BLOCK * at
        place = jnp.where(place_row == place_col, 1.0, 0.0).astype(BF16)
        moment_part = moment_rows + dot(moment_cols, place, 0, 0)
        block = BLOCK_WEIGHT[o] * (gram + 0.5 * moment_part)
        gram_send[:, :, BLOCK * o : BLOCK * (o + 1)] = block.reshape(GENE, ROWS, BLOCK)

    def gram_copy(peer, slot):
        return gene_copy(0, gram_send.at[peer], gram_recv.at[slot], peer, slot)

    each(GENE - 1, lambda k: gram_copy(gene_peer(k), g).start())
    gram_recv[g] = gram_send[g]

    kernel_log = log_var_ref[0]
    eye = lax.broadcasted_iota(jnp.int32, (LAT, LAT), 0) == lax.broadcasted_iota(
        jnp.int32, (LAT, LAT), 1
    )
    length = jnp.sum(
        jnp.where(eye, jnp.broadcast_to(length_ref[...], (LAT, LAT)), 0.0), axis=1, keepdims=True
    )
    mean = mean_ref[...]
    variance = jnp.exp(logvar_ref[...])
    inverse = 1.0 / (length + variance)
    constant = kernel_log + 0.5 * jnp.sum(
        jnp.log(length * inverse) - mean * mean * inverse, axis=0, keepdims=True
    )
    coef = cell_coefficients(
        LOG2E * mean * inverse, (-0.5 * LOG2E) * inverse, LOG2E * constant, 0
    ).astype(BF16)
    features = point_features(inducing_ref[...], []).astype(BF16)
    psi_one = jnp.exp2(dot(features, coef, 0, 0))
    psi_low_ref[...] = psi_one.astype(BF16)

    eye_cells = lax.broadcasted_iota(jnp.int32, (CELLS, CELLS), 0) == lax.broadcasted_iota(
        jnp.int32, (CELLS, CELLS), 1
    )
    local_index = (index_ref[...] - d * IND).astype(F32)
    index_col = jnp.sum(
        jnp.where(eye_cells, jnp.broadcast_to(local_index, (CELLS, CELLS)), 0.0),
        axis=1,
        keepdims=True,
    )
    row_number = lax.broadcasted_iota(jnp.int32, (CELLS, IND), 1).astype(F32)
    one_hot = jnp.where(row_number == index_col, 1.0, 0.0).astype(BF16)
    y_copy.wait()
    cell_rows = dot(one_hot, y_ref[...], 1, 0)
    cell_ref[...] = cell_rows.astype(BF16)
    squares = jnp.sum((cell_rows * cell_rows).reshape(CELLS // 8, 8, GENES), axis=0)
    square_tile = functools.reduce(
        jnp.add, [squares[:, 128 * k : 128 * (k + 1)] for k in range(GENES // 128)]
    )

    def data_copy(peer, slot):
        return dp_copy(1, data_send.at[peer], data_recv.at[slot], peer, slot)

    def data_step(k):
        peer = dp_peer(k)
        rows = psi_low_ref[pl.ds(pl.multiple_of(BLOCK * peer, BLOCK), BLOCK)]
        data_send[peer] = dot(rows, cell_ref[...], 1, 0).astype(BF16)
        data_copy(peer, d).start()

    each(DP - 1, data_step)
    data_own[...] = dot(
        psi_low_ref[pl.ds(pl.multiple_of(BLOCK * d, BLOCK), BLOCK)], cell_ref[...], 1, 0
    )

    cross = dot(proj_low[...], cell_ref[...], 1, 1)
    product = psi_one * cross
    sum_0, sum_1, sum_2 = moments(dot(features, product.astype(BF16), 1, 0))
    beta = jnp.exp(jnp.full((1, CELLS), log_beta_ref[0], F32))
    beta_sq = beta * beta
    first_ref[0:LAT] = beta_sq * inverse * (sum_1 - mean * sum_0)
    first_ref[LAT : 2 * LAT] = (
        beta_sq
        * 0.5
        * variance
        * inverse
        * (inverse * (sum_2 - 2.0 * mean * sum_1 + mean * mean * sum_0) - sum_0)
    )

    base = inducing_ref[:, pl.ds(pl.multiple_of(BLOCK * d, BLOCK), BLOCK)]
    lane = lax.broadcasted_iota(jnp.int32, (LAT, BLOCK), 1)
    quarter_inv = (-0.25 * LOG2E) / length

    def feature_step(i):
        column = jnp.sum(jnp.where(lane == ROWS * g + i, base, 0.0), axis=1, keepdims=True)
        for o in range(SPAN):
            at = lax.rem(d + o, DP)
            points = inducing_ref[:, pl.ds(pl.multiple_of(BLOCK * at, BLOCK), BLOCK)]
            gap = points - column
            pair = jnp.sum(gap * gap * quarter_inv, axis=0, keepdims=True)
            block = point_features(0.5 * (points + column), split_three(pair))
            offset = pl.multiple_of(lax.rem(i, 2) * WIDTH + BLOCK * o, BLOCK)
            pair_feat[lax.div(i, 2), :, pl.ds(offset, BLOCK)] = block.astype(BF16)

    each(ROWS, feature_step)

    def coefficient_step(k):
        at = dp_peer(k)

        @pl.when(k < DP - 1)
        def _():
            latent_copy(at, at).wait_recv()

        cell_mean = lat_all[at, 0:LAT]
        cell_var = jnp.exp(lat_all[at, LAT : 2 * LAT])
        inverse_w = 1.0 / (length + 2.0 * cell_var)
        inv_width[at] = inverse_w
        const = 2.0 * kernel_log + jnp.sum(
            0.5 * jnp.log(length * inverse_w) - cell_mean * cell_mean * inverse_w,
            axis=0,
            keepdims=True,
        )
        block = cell_coefficients(
            (2.0 * LOG2E) * cell_mean * inverse_w, -LOG2E * inverse_w, LOG2E * const, 3
        )
        cell_coef[at] = block.T.astype(BF16)

    each(DP, coefficient_step)

    each(GENE - 1, lambda k: gram_copy(gene_peer(k), gene_peer(k)).wait_recv())
    weight = jnp.sum(gram_recv[...], axis=0)
    for i in range(ROWS):
        weight_ref[i // 2, :, WIDTH * (i % 2) : WIDTH * (i % 2 + 1)] = jnp.broadcast_to(
            weight[i : i + 1], (8, WIDTH)
        )

    psi_acc[...] = jnp.zeros_like(psi_acc)
    trace_ref[...] = jnp.zeros_like(trace_ref)

    def grad_copy(peer, slot):
        return dp_copy(2, grad_send.at[peer], grad_recv.at[slot], peer, slot)

    def cell_step(k):
        at = dp_peer(k)
        table = jnp.zeros((USED, CELLS), F32)
        for s in range(STEPS):
            psi = jnp.exp2(dot(cell_coef[at], pair_feat[s], 1, 0))
            psi = psi.reshape(CELLS // 8, 8, PAIRS)
            psi_acc[s] += jnp.sum(psi, axis=0)
            weighted = (psi * weight_ref[s][None]).reshape(CELLS, PAIRS).astype(BF16)
            table = table + dot(pair_feat[s, 0:USED], weighted, 1, 1)
        mom_0, mom_1, mom_2 = moments(table)
        cell_mean = lat_all[at, 0:LAT]
        cell_var = jnp.exp(lat_all[at, LAT : 2 * LAT])
        inverse_w = inv_width[at]
        trace_ref[...] += mom_0
        grad_send[at, 0:LAT] = -beta * inverse_w * (mom_1 - cell_mean * mom_0)
        grad_send[at, LAT : 2 * LAT] = (
            -beta
            * cell_var
            * inverse_w
            * (
                inverse_w * (mom_2 - 2.0 * cell_mean * mom_1 + cell_mean * cell_mean * mom_0)
                - 0.5 * mom_0
            )
        )

        @pl.when(k < DP - 1)
        def _():
            grad_copy(at, d).start()

    each(DP, cell_step)

    total_row = sum_0 - 0.5 * trace_ref[...]
    total_row = total_row[:, 0:128] + total_row[:, 128:256]
    first_row = lax.broadcasted_iota(jnp.int32, (8, 128), 0) == 0
    total_tile = jnp.where(first_row, jnp.broadcast_to(total_row, (8, 128)), 0.0) - (
        0.5 * square_tile
    )
    for i in range(ROWS):
        row = jnp.sum(
            psi_acc[i // 2, :, WIDTH * (i % 2) : WIDTH * (i % 2 + 1)], axis=0, keepdims=True
        )
        psi_send[i : i + 1, 0:WIDTH] = row
    psi_send[:, WIDTH : WIDTH + 128] = total_tile

    def psi_copy(peer, slot):
        return gene_copy(1, psi_send, psi_recv.at[slot], peer, slot)

    each(GENE - 1, lambda k: psi_copy(gene_peer(k), g).start())
    psi_recv[g] = psi_send[...]

    each(DP - 1, lambda k: grad_copy(dp_peer(k), dp_peer(k)).wait_recv())
    grad_recv[d] = grad_send[d]
    own_grad = first_ref[...] + jnp.sum(grad_recv[...], axis=0)
    for p in range(GENE):
        part_send[p] = own_grad[
            8 * (p // 2) : 8 * (p // 2 + 1), 128 * (p % 2) : 128 * (p % 2 + 1)
        ]

    def part_copy(peer, slot):
        return gene_copy(2, part_send.at[peer], part_recv.at[slot], peer, slot)

    each(GENE - 1, lambda k: part_copy(gene_peer(k), g).start())
    part_recv[g] = part_send[g]

    each(GENE - 1, lambda k: psi_copy(gene_peer(k), gene_peer(k)).wait_recv())
    total_recv[d] = jnp.sum(psi_recv[:, :, WIDTH : WIDTH + 128], axis=0)
    psi_rows = [
        psi_recv[:, :, BLOCK * o : BLOCK * (o + 1)].reshape(BLOCK, BLOCK).astype(BF16)
        for o in range(SPAN)
    ]
    for o in range(1, 4):
        block_send[o - 1] = psi_rows[o]

    def block_copy(o, slot):
        return dp_copy(
            3, block_send.at[o - 1], block_recv.at[slot], lax.rem(d + o, DP), slot
        )

    def total_copy(peer, slot):
        return dp_copy(4, total_recv.at[d], total_recv.at[slot], peer, slot)

    for o in range(1, 4):
        block_copy(o, o - 1).start()
    each(DP - 1, lambda k: total_copy(dp_peer(k), d).start())

    each(GENE - 1, lambda k: part_copy(gene_peer(k), gene_peer(k)).wait_recv())
    sum_all[g] = jnp.sum(part_recv[...], axis=0)

    def sum_copy(peer, slot):
        return gene_copy(3, sum_all.at[g], sum_all.at[slot], peer, slot)

    each(GENE - 1, lambda k: sum_copy(gene_peer(k), g).start())

    stat = jnp.zeros((BLOCK, GENES), F32)
    for o in range(SPAN):
        at = lax.rem(d + o, DP)
        stat = stat + dot(
            psi_rows[o], proj_low[pl.ds(pl.multiple_of(BLOCK * at, BLOCK), BLOCK)], 1, 0
        )
    each(DP - 1, lambda k: data_copy(dp_peer(k), dp_peer(k)).wait_recv())
    data_recv[d] = jnp.zeros((BLOCK, GENES), BF16)
    data = data_own[...]
    for p in range(DP):
        data = data + data_recv[p].astype(F32)
    for o in range(1, 4):
        block_copy(o, o - 1).wait_recv()
        at = lax.rem(d + (DP - o), DP)
        stat = stat + dot(
            block_recv[o - 1],
            proj_low[pl.ds(pl.multiple_of(BLOCK * at, BLOCK), BLOCK)],
            0,
            0,
        )
    proj_out[...] = data - stat

    each(GENE - 1, lambda k: sum_copy(gene_peer(k), gene_peer(k)).wait_recv())
    for p in range(GENE):
        latent_out[8 * (p // 2) : 8 * (p // 2 + 1), 128 * (p % 2) : 128 * (p % 2 + 1)] = sum_all[p]
    each(DP - 1, lambda k: total_copy(dp_peer(k), dp_peer(k)).wait_recv())
    total_out[...] = jnp.sum(total_recv[...], axis=0)

    def sent_dp(k):
        peer = dp_peer(k)
        latent_copy(peer, d).wait_send()
        data_copy(peer, d).wait_send()
        grad_copy(peer, d).wait_send()
        total_copy(peer, d).wait_send()

    def sent_gene(k):
        peer = gene_peer(k)
        gram_copy(peer, g).wait_send()
        psi_copy(peer, g).wait_send()
        part_copy(peer, g).wait_send()
        sum_copy(peer, g).wait_send()

    each(DP - 1, sent_dp)
    each(GENE - 1, sent_gene)
    for o in range(1, 4):
        block_copy(o, o - 1).wait_send()


def on_device(
    y_pool,
    cell_index,
    latent_mean,
    latent_logvar,
    inducing,
    length_sq,
    log_var,
    log_beta,
    proj_mean,
    second_moment,
):
    vmem = pl.BlockSpec(memory_space=pltpu.VMEM)
    smem = pl.BlockSpec(memory_space=pltpu.SMEM)
    hbm = pl.BlockSpec(memory_space=pl.ANY)
    scratch = [
        pltpu.VMEM((IND, GENES), F32),
        pltpu.VMEM((IND, GENES), BF16),
        pltpu.VMEM((IND, GENES), BF16),
        pltpu.VMEM((CELLS, GENES), BF16),
        pltpu.VMEM((IND, CELLS), BF16),
        pltpu.VMEM((DP, 2 * LAT, CELLS), F32),
        pltpu.VMEM((GENE, ROWS, WIDTH), F32),
        pltpu.VMEM((GENE, ROWS, WIDTH), F32),
        pltpu.VMEM((DP, BLOCK, GENES), BF16),
        pltpu.VMEM((DP, BLOCK, GENES), BF16),
        pltpu.VMEM((BLOCK, GENES), F32),
        pltpu.VMEM((STEPS, DEPTH, PAIRS), BF16),
        pltpu.VMEM((DP, CELLS, DEPTH), BF16),
        pltpu.VMEM((DP, LAT, CELLS), F32),
        pltpu.VMEM((STEPS, 8, PAIRS), F32),
        pltpu.VMEM((STEPS, 8, PAIRS), F32),
        pltpu.VMEM((2 * LAT, CELLS), F32),
        pltpu.VMEM((1, CELLS), F32),
        pltpu.VMEM((DP, 2 * LAT, CELLS), F32),
        pltpu.VMEM((DP, 2 * LAT, CELLS), F32),
        pltpu.VMEM((ROWS, WIDTH + 128), F32),
        pltpu.VMEM((GENE, ROWS, WIDTH + 128), F32),
        pltpu.VMEM((GENE, 8, 128), F32),
        pltpu.VMEM((GENE, 8, 128), F32),
        pltpu.VMEM((GENE, 8, 128), F32),
        pltpu.VMEM((3, BLOCK, BLOCK), BF16),
        pltpu.VMEM((3, BLOCK, BLOCK), BF16),
        pltpu.VMEM((DP, 8, 128), F32),
        pltpu.SemaphoreType.DMA((5,)),
        pltpu.SemaphoreType.DMA((5, 2, DP)),
        pltpu.SemaphoreType.DMA((4, 2, GENE)),
    ]
    latent, proj, total = pl.pallas_call(
        kernel,
        out_shape=(
            jax.ShapeDtypeStruct((2 * LAT, CELLS), F32),
            jax.ShapeDtypeStruct((BLOCK, GENES), F32),
            jax.ShapeDtypeStruct((8, 128), F32),
        ),
        in_specs=[hbm, vmem, vmem, vmem, vmem, vmem, smem, smem, hbm, vmem],
        out_specs=(vmem, vmem, vmem),
        scratch_shapes=scratch,
        compiler_params=pltpu.CompilerParams(
            collective_id=0, has_side_effects=True, vmem_limit_bytes=56 * 1024 * 1024
        ),
        name="bound_gradients",
    )(
        y_pool,
        cell_index.reshape(1, CELLS),
        latent_mean,
        latent_logvar,
        inducing,
        length_sq.reshape(1, LAT),
        log_var,
        log_beta,
        proj_mean,
        second_moment,
    )
    noise_prec = jnp.exp(log_beta[0])
    batch_size = CELLS * DP
    gene_count = GENES * GENE
    variance = jnp.exp(latent_logvar)
    grad_latent = latent.reshape(2, LAT, CELLS) + jnp.stack(
        [-latent_mean, -0.5 * (variance - 1.0)]
    )
    grad_proj = (noise_prec / batch_size) * proj
    grad_logbeta = (
        noise_prec / (batch_size * gene_count) * jnp.sum(total)
        - 0.5 * noise_prec * jnp.exp(log_var[0])
        + 0.5
    )
    return (grad_latent, grad_proj, grad_logbeta.reshape(1))


def solution(mesh):
    in_specs = (
        P("dp", "gene"),
        P("dp"),
        P(None, "dp"),
        P(None, "dp"),
        P(),
        P(),
        P(),
        P(),
        P(None, "gene"),
        P("gene", None),
    )
    out_specs = (P(None, None, "dp"), P("dp", "gene"), P())
    return jax.shard_map(
        on_device, mesh=mesh, in_specs=in_specs, out_specs=out_specs, check_vma=False
    )
```

```python
import functools

import jax
import jax.numpy as jnp
from jax import lax
from jax.experimental import pallas as pl
from jax.experimental.pallas import tpu as pltpu
from jax.sharding import PartitionSpec as P

F32 = jnp.float32
BF16 = jnp.bfloat16
LOG2E = 1.4426950408889634
MESH = pl.DeviceIdType.MESH

DP = 8
DP_Z = 4
GENE = 16
CELLS = 256
LAT = 32
IND = 1024
GENES = 1024
BLOCK = IND // DP
ROWS = BLOCK // GENE
SPAN = 5
WIDTH = SPAN * BLOCK
STEPS = 4
PAIRS = ROWS * WIDTH // STEPS
DEPTH = 256
HALF = 384
SPLIT = 4
BLOCK_WEIGHT = (1.0, 2.0, 2.0, 2.0, 1.0)


def each(count, body):
    def step(k, carry):
        body(k)
        return carry

    lax.fori_loop(0, count, step, 0)


def split_two(value):
    high = value.astype(BF16).astype(F32)
    return high, (value - high).astype(BF16).astype(F32)


def split_three(value):
    high = value.astype(BF16).astype(F32)
    rest = value - high
    mid = rest.astype(BF16).astype(F32)
    return high, mid, (rest - mid).astype(BF16).astype(F32)


def special(rows, width):
    place = lax.broadcasted_iota(jnp.int32, (64, width), 0)
    total = jnp.zeros((64, width), F32)
    for at, row in enumerate(rows):
        total = jnp.where(place == at, jnp.broadcast_to(row, (64, width)), total)
    return total


def point_features(value, extra):
    width = value.shape[1]
    high, low = split_two(value)
    square_high, square_low = split_two(value * value)
    ones = jnp.ones((1, width), F32)
    rows = [ones, ones, ones] + list(extra)
    return jnp.concatenate(
        [high, square_high, low, square_low, high, square_high, special(rows, width)], axis=0
    )


def cell_coefficients(linear, square, constant, extra):
    width = linear.shape[1]
    high, low = split_two(linear)
    square_high, square_low = split_two(square)
    rows = list(split_three(constant)) + [jnp.ones((1, width), F32)] * extra
    return jnp.concatenate(
        [high, square_high, high, square_high, low, square_low, special(rows, width)], axis=0
    )


def moments(table):
    return table[192:193], table[0:32] + table[64:96], table[32:64] + table[96:128]


def dot(left, right, left_dim, right_dim):
    return lax.dot_general(
        left, right, (((left_dim,), (right_dim,)), ((), ())), preferred_element_type=F32
    )


def kernel(
    y_hbm,
    index_ref,
    mean_ref,
    logvar_ref,
    inducing_ref,
    length_ref,
    log_var_ref,
    log_beta_ref,
    proj_hbm,
    moment_ref,
    latent_out,
    proj_out,
    total_out,
    proj_f32,
    proj_low,
    y_ref,
    cell_all,
    psi_low_ref,
    psi_side,
    lat_all,
    gram_send,
    gram_recv,
    data_send,
    data_recv,
    data_own,
    pair_feat,
    pair_cols,
    cell_coef,
    inv_width,
    weight_ref,
    psi_acc,
    first_ref,
    trace_ref,
    grad_send,
    grad_recv,
    psi_all,
    part_send,
    part_recv,
    sum_all,
    block_send,
    block_recv,
    total_recv,
    local_sem,
    dp_sems,
    gene_sems,
    pair_sems,
):
    d = lax.axis_index("dp")
    g = lax.axis_index("gene")
    z = lax.rem(d, DP_Z)
    side = d - z
    core = lax.rem(g, 2)
    place = lax.div(g, 2)
    group = GENE // 2 * core + place
    sibling = g + 1 - 2 * core

    def remote(src, dst, axis, send_sem, recv_sem, peer):
        return pltpu.make_async_remote_copy(
            src_ref=src,
            dst_ref=dst,
            send_sem=send_sem,
            recv_sem=recv_sem,
            device_id={axis: peer},
            device_id_type=MESH,
        )

    def dp_peer(k):
        return lax.rem(d + 1 + k, DP)

    def gene_peer(k):
        return lax.rem(g + 1 + k, GENE)

    def chip_peer(k):
        return lax.rem(place + 1 + k, GENE // 2)

    def z_peer(k):
        return side + lax.rem(z + 1 + k, DP_Z)

    def cell_order(k):
        return lax.rem(side + DP_Z * (1 - lax.div(k, DP_Z)), DP) + lax.rem(z + 1 + k, DP_Z)

    def dp_copy(kind, src, dst, peer, slot):
        return remote(src, dst, "dp", dp_sems.at[kind, 0, peer], dp_sems.at[kind, 1, slot], peer)

    def gene_copy(kind, src, dst, peer, slot):
        return remote(
            src, dst, "gene", gene_sems.at[kind, 0, peer], gene_sems.at[kind, 1, slot], peer
        )

    def pair_copy(kind, src, dst):
        return remote(src, dst, "gene", pair_sems.at[kind, 0], pair_sems.at[kind, 1], sibling)

    quarter = IND // 4
    proj_copies = [
        pltpu.make_async_copy(
            proj_hbm.at[pl.ds(quarter * k, quarter)],
            proj_f32.at[pl.ds(quarter * k, quarter)],
            local_sem.at[k],
        )
        for k in range(4)
    ]
    y_copy = pltpu.make_async_copy(y_hbm, y_ref, local_sem.at[4])
    for copy in proj_copies:
        copy.start()
    y_copy.start()

    barrier = pltpu.get_barrier_semaphore()
    each(
        DP - 1,
        lambda k: pl.semaphore_signal(
            barrier, inc=1, device_id={"dp": dp_peer(k)}, device_id_type=MESH
        ),
    )
    each(
        GENE - 1,
        lambda k: pl.semaphore_signal(
            barrier, inc=1, device_id={"gene": gene_peer(k)}, device_id_type=MESH
        ),
    )
    lat_all[core, d] = jnp.where(core == 0, mean_ref[...], logvar_ref[...])
    pl.semaphore_wait(barrier, DP + GENE - 2)

    def latent_copy(peer, slot):
        return dp_copy(0, lat_all.at[core, d], lat_all.at[core, slot], peer, slot)

    each(DP - 1, lambda k: latent_copy(dp_peer(k), d).start())

    for k in range(4):
        proj_copies[k].wait()
        proj_low[quarter * k : quarter * (k + 1)] = proj_f32[
            quarter * k : quarter * (k + 1)
        ].astype(BF16)

    own_rows = proj_low[pl.ds(pl.multiple_of(BLOCK * d, BLOCK), BLOCK)]
    row_of = lax.broadcasted_iota(jnp.int32, (BLOCK, 64), 0) + BLOCK * d
    col_of = lax.broadcasted_iota(jnp.int32, (BLOCK, 64), 1) + 64 * g
    pick_rows = jnp.where(row_of == col_of, 1.0, 0.0).astype(BF16)
    moment_cols = moment_ref[:, pl.ds(pl.multiple_of(BLOCK * d, BLOCK), BLOCK)].astype(BF16)
    for o in range(SPAN):
        at = lax.rem(d + o, DP)
        start = pl.multiple_of(BLOCK * at, BLOCK)
        gram = dot(own_rows, proj_low[pl.ds(start, BLOCK)], 1, 1)
        moment_rows = dot(pick_rows, moment_ref[:, pl.ds(start, BLOCK)].astype(BF16), 1, 0)
        to_row = lax.broadcasted_iota(jnp.int32, (64, BLOCK), 0) + 64 * g
        to_col = lax.broadcasted_iota(jnp.int32, (64, BLOCK), 1) + BLOCK * at
        to_place = jnp.where(to_row == to_col, 1.0, 0.0).astype(BF16)
        moment_part = moment_rows + dot(moment_cols, to_place, 0, 0)
        block = BLOCK_WEIGHT[o] * (gram + 0.5 * moment_part)
        gram_send[:, :, BLOCK * o : BLOCK * (o + 1)] = block.reshape(GENE, ROWS, BLOCK)

    def group_of(device):
        return GENE // 2 * lax.rem(device, 2) + lax.div(device, 2)

    def gram_copy(peer, slot):
        return gene_copy(0, gram_send.at[group_of(peer)], gram_recv.at[slot], peer, slot)

    each(GENE - 1, lambda k: gram_copy(gene_peer(k), g).start())
    gram_recv[g] = gram_send[group]

    eye_cells = lax.broadcasted_iota(jnp.int32, (CELLS, CELLS), 0) == lax.broadcasted_iota(
        jnp.int32, (CELLS, CELLS), 1
    )
    local_index = (index_ref[...] - d * IND).astype(F32)
    index_col = jnp.sum(
        jnp.where(eye_cells, jnp.broadcast_to(local_index, (CELLS, CELLS)), 0.0),
        axis=1,
        keepdims=True,
    )
    row_number = lax.broadcasted_iota(jnp.int32, (CELLS, IND), 1).astype(F32)
    one_hot = jnp.where(row_number == index_col, 1.0, 0.0).astype(BF16)
    y_copy.wait()
    cell_rows = dot(one_hot, y_ref[...], 1, 0)
    cell_all[0] = cell_rows.astype(BF16)
    across = lax.rem(d + DP_Z, DP)

    def cell_copy():
        return dp_copy(3, cell_all.at[0], cell_all.at[1], across, 7)

    cell_copy().start()
    squares = jnp.sum((cell_rows * cell_rows).reshape(CELLS // 8, 8, GENES), axis=0)
    square_tile = functools.reduce(
        jnp.add, [squares[:, 128 * k : 128 * (k + 1)] for k in range(GENES // 128)]
    )

    kernel_log = log_var_ref[0]
    eye = lax.broadcasted_iota(jnp.int32, (LAT, LAT), 0) == lax.broadcasted_iota(
        jnp.int32, (LAT, LAT), 1
    )
    length = jnp.sum(
        jnp.where(eye, jnp.broadcast_to(length_ref[...], (LAT, LAT)), 0.0), axis=1, keepdims=True
    )

    def first_coefficients(cell_mean, inverse):
        constant = kernel_log + 0.5 * jnp.sum(
            jnp.log(length * inverse) - cell_mean * cell_mean * inverse, axis=0, keepdims=True
        )
        return cell_coefficients(
            LOG2E * cell_mean * inverse, (-0.5 * LOG2E) * inverse, LOG2E * constant, 0
        ).astype(BF16)

    mean = mean_ref[...]
    variance = jnp.exp(logvar_ref[...])
    inverse = 1.0 / (length + variance)
    features = point_features(inducing_ref[...], []).astype(BF16)
    psi_one = jnp.exp2(dot(features, first_coefficients(mean, inverse), 0, 0))
    psi_low_ref[...] = psi_one.astype(BF16)

    cross = dot(proj_low[...], cell_all[0], 1, 1)
    product = psi_one * cross
    sum_0, sum_1, sum_2 = moments(dot(features, product.astype(BF16), 1, 0))
    beta = jnp.exp(jnp.full((1, CELLS), log_beta_ref[0], F32))
    beta_sq = beta * beta
    first_ref[0:LAT] = beta_sq * inverse * (sum_1 - mean * sum_0)
    first_ref[LAT : 2 * LAT] = (
        beta_sq
        * 0.5
        * variance
        * inverse
        * (inverse * (sum_2 - 2.0 * mean * sum_1 + mean * mean * sum_0) - sum_0)
    )

    base = inducing_ref[:, pl.ds(pl.multiple_of(BLOCK * d, BLOCK), BLOCK)]
    lane = lax.broadcasted_iota(jnp.int32, (LAT, BLOCK), 1)
    quarter_inv = (-0.25 * LOG2E) / length

    def feature_step(i):
        column = jnp.sum(jnp.where(lane == ROWS * group + i, base, 0.0), axis=1, keepdims=True)
        for o in range(SPAN):
            at = lax.rem(d + o, DP)
            points = inducing_ref[:, pl.ds(pl.multiple_of(BLOCK * at, BLOCK), BLOCK)]
            gap = points - column
            pair = jnp.sum(gap * gap * quarter_inv, axis=0, keepdims=True)
            block = point_features(0.5 * (points + column), split_three(pair))
            offset = pl.multiple_of(lax.rem(i, 2) * WIDTH + BLOCK * o, BLOCK)
            pair_feat[lax.div(i, 2), :, pl.ds(offset, BLOCK)] = block.astype(BF16)
            columns = jnp.concatenate([block[0:96], block[192:224]], axis=0)
            pair_cols[lax.div(i, 2), pl.ds(offset, BLOCK)] = columns.T.astype(BF16)

    each(ROWS, feature_step)

    def pair_latent_copy():
        return pair_copy(0, lat_all.at[core], lat_all.at[core])

    def pair_latent_arrival():
        return pair_copy(0, lat_all.at[core], lat_all.at[1 - core])

    each(DP - 1, lambda k: latent_copy(dp_peer(k), dp_peer(k)).wait_recv())
    pair_latent_copy().start()
    pair_latent_arrival().wait_recv()

    def coefficient_step(at):
        cell_mean = lat_all[0, at]
        inverse_w = 1.0 / (length + 2.0 * jnp.exp(lat_all[1, at]))
        inv_width[at] = inverse_w
        const = 2.0 * kernel_log + jnp.sum(
            0.5 * jnp.log(length * inverse_w) - cell_mean * cell_mean * inverse_w,
            axis=0,
            keepdims=True,
        )
        block = cell_coefficients(
            (2.0 * LOG2E) * cell_mean * inverse_w, -LOG2E * inverse_w, LOG2E * const, 3
        )
        cell_coef[at] = block.T.astype(BF16)

    each(DP, coefficient_step)

    each(GENE - 1, lambda k: gram_copy(gene_peer(k), gene_peer(k)).wait_recv())
    weight = jnp.sum(gram_recv[...], axis=0)
    for i in range(ROWS):
        weight_ref[i // 2, :, WIDTH * (i % 2) : WIDTH * (i % 2 + 1)] = jnp.broadcast_to(
            weight[i : i + 1], (8, WIDTH)
        )
    psi_acc[...] = jnp.zeros_like(psi_acc)
    trace_ref[...] = jnp.zeros_like(trace_ref)

    def grad_copy(peer, slot):
        return dp_copy(2, grad_send.at[peer], grad_recv.at[slot], peer, slot)

    def cell_gradients(at):
        table = jnp.zeros((CELLS, 128), F32)
        for s in range(STEPS):
            psi = jnp.exp2(dot(cell_coef[at], pair_feat[s], 1, 0))
            psi = psi.reshape(CELLS // 8, 8, PAIRS)
            psi_acc[s] += jnp.sum(psi, axis=0)
            weighted = (psi * weight_ref[s][None]).reshape(CELLS, PAIRS).astype(BF16)
            table = table + dot(weighted, pair_cols[s], 1, 0)
        table = table.T
        mom_0 = table[96:97]
        mom_1 = table[0:32] + table[64:96]
        mom_2 = table[32:64]
        cell_mean = lat_all[0, at]
        cell_var = jnp.exp(lat_all[1, at])
        inverse_w = inv_width[at]
        trace_ref[...] += mom_0
        by_mean = -beta * inverse_w * (mom_1 - cell_mean * mom_0)
        by_logvar = (
            -beta
            * cell_var
            * inverse_w
            * (
                inverse_w * (mom_2 - 2.0 * cell_mean * mom_1 + cell_mean * cell_mean * mom_0)
                - 0.5 * mom_0
            )
        )
        return by_mean, by_logvar

    def cell_step(k):
        at = cell_order(k)
        by_mean, by_logvar = cell_gradients(at)
        grad_send[at, 0:LAT] = by_mean.astype(BF16)
        grad_send[at, LAT : 2 * LAT] = by_logvar.astype(BF16)
        grad_copy(at, d).start()

    each(SPLIT, cell_step)

    def data_copy(peer, slot):
        return dp_copy(
            1,
            data_send.at[lax.rem(peer, DP_Z)],
            data_recv.at[lax.rem(slot, DP_Z)],
            peer,
            slot,
        )

    dp_copy(3, cell_all.at[0], cell_all.at[1], across, 7).wait_recv()
    side_points = inducing_ref[:, pl.ds(pl.multiple_of(BLOCK * side, BLOCK), BLOCK * DP_Z)]
    across_mean = lat_all[0, across]
    across_inverse = 1.0 / (length + jnp.exp(lat_all[1, across]))
    psi_across = jnp.exp2(
        dot(
            point_features(side_points, []).astype(BF16),
            first_coefficients(across_mean, across_inverse),
            0,
            0,
        )
    )
    psi_side[...] = psi_across.astype(BF16)

    def data_rows(at):
        near = psi_low_ref[pl.ds(pl.multiple_of(BLOCK * (side + at), BLOCK), BLOCK)]
        far = psi_side[pl.ds(pl.multiple_of(BLOCK * at, BLOCK), BLOCK)]
        return dot(near, cell_all[0], 1, 0) + dot(far, cell_all[1], 1, 0)

    def data_step(k):
        at = lax.rem(z + 1 + k, DP_Z)
        data_send[at] = data_rows(at).astype(BF16)
        data_copy(z_peer(k), d).start()

    each(DP_Z - 1, data_step)

    each(DP - 1 - SPLIT, lambda k: cell_step(k + SPLIT))
    by_mean, by_logvar = cell_gradients(d)
    first_ref[0:LAT] += by_mean
    first_ref[LAT : 2 * LAT] += by_logvar

    total_row = sum_0 - 0.5 * trace_ref[...]
    total_row = total_row[:, 0:128] + total_row[:, 128:256]
    first_row = lax.broadcasted_iota(jnp.int32, (8, 128), 0) == 0
    total_tile = jnp.where(first_row, jnp.broadcast_to(total_row, (8, 128)), 0.0) - (
        0.5 * square_tile
    )
    rows = jnp.concatenate(
        [
            jnp.sum(
                psi_acc[i // 2, :, WIDTH * (i % 2) : WIDTH * (i % 2 + 1)], axis=0, keepdims=True
            )
            for i in range(ROWS)
        ],
        axis=0,
    )
    wide = jnp.concatenate([rows, jnp.zeros((ROWS, 128), F32)], axis=1)
    psi_all[core, place] = jnp.concatenate([wide[:, 0:HALF], wide[:, HALF:]], axis=0).astype(BF16)

    def psi_copy(chip, slot):
        return remote(
            psi_all.at[core, place],
            psi_all.at[core, slot],
            "gene",
            gene_sems.at[1, 0, chip],
            gene_sems.at[1, 1, slot],
            2 * chip + core,
        )

    each(GENE // 2 - 1, lambda k: psi_copy(chip_peer(k), place).start())

    grad_recv[d] = jnp.zeros((2 * LAT, CELLS), BF16)
    each(DP - 1, lambda k: grad_copy(dp_peer(k), dp_peer(k)).wait_recv())
    own_grad = first_ref[...]
    for p in range(DP):
        own_grad = own_grad + grad_recv[p].astype(F32)
    for p in range(GENE):
        part_send[p, 0:8] = own_grad[
            8 * (p // 2) : 8 * (p // 2 + 1), 128 * (p % 2) : 128 * (p % 2 + 1)
        ]
        part_send[p, 8:16] = total_tile

    def part_copy(peer, slot):
        return gene_copy(2, part_send.at[peer], part_recv.at[slot], peer, slot)

    each(GENE - 1, lambda k: part_copy(gene_peer(k), g).start())
    part_recv[g] = part_send[g]

    def pair_psi_copy():
        return pair_copy(1, psi_all.at[core], psi_all.at[core])

    def pair_psi_arrival():
        return pair_copy(1, psi_all.at[core], psi_all.at[1 - core])

    each(GENE // 2 - 1, lambda k: psi_copy(chip_peer(k), chip_peer(k)).wait_recv())
    pair_psi_copy().start()

    data_own[...] = data_rows(z)

    pair_psi_arrival().wait_recv()
    gathered = psi_all[...].astype(F32).reshape(GENE, 2 * ROWS, HALF)
    left = gathered[:, 0:ROWS].reshape(BLOCK, HALF)
    right = gathered[:, ROWS : 2 * ROWS].reshape(BLOCK, HALF)
    psi_rows = [
        (left if o < 3 else right)[:, BLOCK * (o % 3) : BLOCK * (o % 3 + 1)].astype(BF16)
        for o in range(SPAN)
    ]
    for o in range(1, 4):
        block_send[o - 1] = psi_rows[o]

    def block_copy(o, slot):
        return dp_copy(3, block_send.at[o - 1], block_recv.at[slot], lax.rem(d + o, DP), slot)

    for o in range(1, 4):
        block_copy(o, o - 1).start()

    each(GENE - 1, lambda k: part_copy(gene_peer(k), gene_peer(k)).wait_recv())
    part_sum = jnp.sum(part_recv[...], axis=0)
    sum_all[g] = part_sum[0:8]
    total_recv[d] = part_sum[8:16]

    def sum_copy(peer, slot):
        return gene_copy(3, sum_all.at[g], sum_all.at[slot], peer, slot)

    def total_copy(peer, slot):
        return dp_copy(4, total_recv.at[d], total_recv.at[slot], peer, slot)

    each(GENE - 1, lambda k: sum_copy(gene_peer(k), g).start())
    each(DP - 1, lambda k: total_copy(dp_peer(k), d).start())

    stat = data_own[...]
    for o in range(SPAN):
        at = lax.rem(d + o, DP)
        stat = stat - dot(
            psi_rows[o], proj_low[pl.ds(pl.multiple_of(BLOCK * at, BLOCK), BLOCK)], 1, 0
        )
    each(DP_Z - 1, lambda k: data_copy(z_peer(k), z_peer(k)).wait_recv())
    for k in range(DP_Z - 1):
        stat = stat + data_recv[lax.rem(z + 1 + k, DP_Z)].astype(F32)
    for o in range(1, 4):
        block_copy(o, o - 1).wait_recv()
        at = lax.rem(d + (DP - o), DP)
        stat = stat - dot(
            block_recv[o - 1],
            proj_low[pl.ds(pl.multiple_of(BLOCK * at, BLOCK), BLOCK)],
            0,
            0,
        )
    proj_out[...] = stat

    each(GENE - 1, lambda k: sum_copy(gene_peer(k), gene_peer(k)).wait_recv())
    for p in range(GENE):
        latent_out[8 * (p // 2) : 8 * (p // 2 + 1), 128 * (p % 2) : 128 * (p % 2 + 1)] = sum_all[p]
    each(DP - 1, lambda k: total_copy(dp_peer(k), dp_peer(k)).wait_recv())
    total_out[...] = jnp.sum(total_recv[...], axis=0)

    def sent_dp(k):
        peer = dp_peer(k)
        latent_copy(peer, d).wait_send()
        grad_copy(peer, d).wait_send()
        total_copy(peer, d).wait_send()

    def sent_gene(k):
        peer = gene_peer(k)
        gram_copy(peer, g).wait_send()
        part_copy(peer, g).wait_send()
        sum_copy(peer, g).wait_send()

    each(DP - 1, sent_dp)
    each(DP_Z - 1, lambda k: data_copy(z_peer(k), d).wait_send())
    each(GENE - 1, sent_gene)
    each(GENE // 2 - 1, lambda k: psi_copy(chip_peer(k), place).wait_send())
    for o in range(1, 4):
        block_copy(o, o - 1).wait_send()
    cell_copy().wait_send()
    pair_latent_copy().wait_send()
    pair_psi_copy().wait_send()


def finish(
    latent_ref,
    proj_ref,
    total_ref,
    mean_ref,
    logvar_ref,
    log_var_ref,
    log_beta_ref,
    latent_out,
    proj_out,
    scalar_out,
):
    beta = jnp.exp(jnp.full((8, 128), log_beta_ref[0], F32))
    amplitude = jnp.exp(jnp.full((8, 128), log_var_ref[0], F32))
    proj_out[...] = proj_ref[...] * (beta[0:1, 0:1] / (CELLS * DP))

    @pl.when(pl.program_id(0) == 0)
    def _():
        latent_out[0] = latent_ref[0:LAT] - mean_ref[...]
        latent_out[1] = latent_ref[LAT : 2 * LAT] - 0.5 * (jnp.exp(logvar_ref[...]) - 1.0)
        entries = CELLS * DP * GENES * GENE
        scalar_out[0] = jnp.sum(
            beta * total_ref[...] / entries - (0.5 / 1024) * beta * amplitude + 0.5 / 1024
        )


def on_device(
    y_pool,
    cell_index,
    latent_mean,
    latent_logvar,
    inducing,
    length_sq,
    log_var,
    log_beta,
    proj_mean,
    second_moment,
):
    vmem = pl.BlockSpec(memory_space=pltpu.VMEM)
    smem = pl.BlockSpec(memory_space=pltpu.SMEM)
    hbm = pl.BlockSpec(memory_space=pl.ANY)
    scratch = [
        pltpu.VMEM((IND, GENES), F32),
        pltpu.VMEM((IND, GENES), BF16),
        pltpu.VMEM((IND, GENES), BF16),
        pltpu.VMEM((2, CELLS, GENES), BF16),
        pltpu.VMEM((IND, CELLS), BF16),
        pltpu.VMEM((DP_Z * BLOCK, CELLS), BF16),
        pltpu.VMEM((2, DP, LAT, CELLS), F32),
        pltpu.VMEM((GENE, ROWS, WIDTH), F32),
        pltpu.VMEM((GENE, ROWS, WIDTH), F32),
        pltpu.VMEM((DP_Z, BLOCK, GENES), BF16),
        pltpu.VMEM((DP_Z, BLOCK, GENES), BF16),
        pltpu.VMEM((BLOCK, GENES), F32),
        pltpu.VMEM((STEPS, DEPTH, PAIRS), BF16),
        pltpu.VMEM((STEPS, PAIRS, 128), BF16),
        pltpu.VMEM((DP, CELLS, DEPTH), BF16),
        pltpu.VMEM((DP, LAT, CELLS), F32),
        pltpu.VMEM((STEPS, 8, PAIRS), F32),
        pltpu.VMEM((STEPS, 8, PAIRS), F32),
        pltpu.VMEM((2 * LAT, CELLS), F32),
        pltpu.VMEM((1, CELLS), F32),
        pltpu.VMEM((DP, 2 * LAT, CELLS), BF16),
        pltpu.VMEM((DP, 2 * LAT, CELLS), BF16),
        pltpu.VMEM((2, GENE // 2, 2 * ROWS, HALF), BF16),
        pltpu.VMEM((GENE, 16, 128), F32),
        pltpu.VMEM((GENE, 16, 128), F32),
        pltpu.VMEM((GENE, 8, 128), F32),
        pltpu.VMEM((3, BLOCK, BLOCK), BF16),
        pltpu.VMEM((3, BLOCK, BLOCK), BF16),
        pltpu.VMEM((DP, 8, 128), F32),
        pltpu.SemaphoreType.DMA((5,)),
        pltpu.SemaphoreType.DMA((5, 2, DP)),
        pltpu.SemaphoreType.DMA((4, 2, GENE)),
        pltpu.SemaphoreType.DMA((2, 2)),
    ]
    latent, proj, total = pl.pallas_call(
        kernel,
        out_shape=(
            jax.ShapeDtypeStruct((2 * LAT, CELLS), F32),
            jax.ShapeDtypeStruct((BLOCK, GENES), F32),
            jax.ShapeDtypeStruct((8, 128), F32),
        ),
        in_specs=[hbm, vmem, vmem, vmem, vmem, vmem, smem, smem, hbm, vmem],
        out_specs=(vmem, vmem, vmem),
        scratch_shapes=scratch,
        compiler_params=pltpu.CompilerParams(
            collective_id=0, has_side_effects=True, vmem_limit_bytes=56 * 1024 * 1024
        ),
        name="bound_gradients",
    )(
        y_pool,
        cell_index.reshape(1, CELLS),
        latent_mean,
        latent_logvar,
        inducing,
        length_sq.reshape(1, LAT),
        log_var,
        log_beta,
        proj_mean,
        second_moment,
    )
    steps = 4
    grad_latent, grad_proj, grad_logbeta = pl.pallas_call(
        finish,
        grid=(steps,),
        out_shape=(
            jax.ShapeDtypeStruct((2, LAT, CELLS), F32),
            jax.ShapeDtypeStruct((BLOCK, GENES), F32),
            jax.ShapeDtypeStruct((1,), F32),
        ),
        in_specs=[
            pl.BlockSpec((2 * LAT, CELLS), lambda i: (0, 0)),
            pl.BlockSpec((BLOCK // steps, GENES), lambda i: (i, 0)),
            pl.BlockSpec((8, 128), lambda i: (0, 0)),
            pl.BlockSpec((LAT, CELLS), lambda i: (0, 0)),
            pl.BlockSpec((LAT, CELLS), lambda i: (0, 0)),
            smem,
            smem,
        ],
        out_specs=(
            pl.BlockSpec((2, LAT, CELLS), lambda i: (0, 0, 0)),
            pl.BlockSpec((BLOCK // steps, GENES), lambda i: (i, 0)),
            smem,
        ),
        name="finish",
    )(latent, proj, total, latent_mean, latent_logvar, log_var, log_beta)
    return (grad_latent, grad_proj, grad_logbeta)


def solution(mesh):
    in_specs = (
        P("dp", "gene"),
        P("dp"),
        P(None, "dp"),
        P(None, "dp"),
        P(),
        P(),
        P(),
        P(),
        P(None, "gene"),
        P("gene", None),
    )
    out_specs = (P(None, None, "dp"), P("dp", "gene"), P())
    return jax.shard_map(
        on_device, mesh=mesh, in_specs=in_specs, out_specs=out_specs, check_vma=False
    )
```

```python
import functools

import jax
import jax.numpy as jnp
from jax import lax
from jax.experimental import pallas as pl
from jax.experimental.pallas import tpu as pltpu
from jax.sharding import PartitionSpec as P

F32 = jnp.float32
BF16 = jnp.bfloat16
LOG2E = 1.4426950408889634
MESH = pl.DeviceIdType.MESH

DP = 8
DP_Z = 4
GENE = 16
CELLS = 256
LAT = 32
IND = 1024
GENES = 1024
BLOCK = IND // DP
ROWS = BLOCK // GENE
SPAN = 5
WIDTH = SPAN * BLOCK
STEPS = 4
PAIRS = ROWS * WIDTH // STEPS
DEPTH = 256
HALF = 384
SPLIT = 4
(
    ACROSS,
    LATENT,
    PAIR_LATENT,
    PAIR_GRAM,
    GRAM,
    CELL,
    GRAD,
    DATA,
    PSI,
    PAIR_PSI,
    PART,
    TURNED,
    SUM,
    TOTAL,
    KINDS,
) = range(15)
BLOCK_WEIGHT = (1.0, 2.0, 2.0, 2.0, 1.0)


def each(count, body):
    def step(k, carry):
        body(k)
        return carry

    lax.fori_loop(0, count, step, 0)


def split_two(value):
    high = value.astype(BF16).astype(F32)
    return high, (value - high).astype(BF16).astype(F32)


def split_three(value):
    high = value.astype(BF16).astype(F32)
    rest = value - high
    mid = rest.astype(BF16).astype(F32)
    return high, mid, (rest - mid).astype(BF16).astype(F32)


def special(rows, width):
    place = lax.broadcasted_iota(jnp.int32, (64, width), 0)
    total = jnp.zeros((64, width), F32)
    for at, row in enumerate(rows):
        total = jnp.where(place == at, jnp.broadcast_to(row, (64, width)), total)
    return total


def point_features(value, extra):
    width = value.shape[1]
    high, low = split_two(value)
    square_high, square_low = split_two(value * value)
    ones = jnp.ones((1, width), F32)
    rows = [ones, ones, ones] + list(extra)
    return jnp.concatenate(
        [high, square_high, low, square_low, high, square_high, special(rows, width)], axis=0
    )


def cell_coefficients(linear, square, constant, extra):
    width = linear.shape[1]
    high, low = split_two(linear)
    square_high, square_low = split_two(square)
    rows = list(split_three(constant)) + [jnp.ones((1, width), F32)] * extra
    return jnp.concatenate(
        [high, square_high, high, square_high, low, square_low, special(rows, width)], axis=0
    )


def moments(table):
    return table[192:193], table[0:32] + table[64:96], table[32:64] + table[96:128]


def dot(left, right, left_dim, right_dim):
    return lax.dot_general(
        left, right, (((left_dim,), (right_dim,)), ((), ())), preferred_element_type=F32
    )


def kernel(
    y_hbm,
    index_ref,
    mean_ref,
    logvar_ref,
    inducing_ref,
    length_ref,
    log_var_ref,
    log_beta_ref,
    proj_hbm,
    moment_ref,
    latent_out,
    proj_out,
    total_out,
    proj_f32,
    proj_low,
    y_ref,
    cell_all,
    psi_low_ref,
    psi_side,
    lat_all,
    gram_send,
    gram_pair,
    gram_out,
    gram_recv,
    data_send,
    data_recv,
    data_own,
    pair_feat,
    pair_cols,
    cell_coef,
    inv_width,
    weight_ref,
    psi_acc,
    first_ref,
    trace_ref,
    grad_send,
    grad_recv,
    psi_all,
    part_send,
    part_recv,
    sum_all,
    block_send,
    block_recv,
    total_recv,
    local_sem,
    sems,
):
    d = lax.axis_index("dp")
    g = lax.axis_index("gene")
    z = lax.rem(d, DP_Z)
    half = lax.div(d, DP_Z)
    side = d - z
    across = lax.rem(d + DP_Z, DP)
    core = lax.rem(g, 2)
    place = lax.div(g, 2)
    group = GENE // 2 * core + place
    sibling = g + 1 - 2 * core

    def remote(src, dst, axis, send_sem, recv_sem, peer):
        return pltpu.make_async_remote_copy(
            src_ref=src,
            dst_ref=dst,
            send_sem=send_sem,
            recv_sem=recv_sem,
            device_id={axis: peer},
            device_id_type=MESH,
        )

    def dp_peer(k):
        return lax.rem(d + 1 + k, DP)

    def gene_peer(k):
        return lax.rem(g + 1 + k, GENE)

    def chip_peer(k):
        return lax.rem(place + 1 + k, GENE // 2)

    def z_peer(k):
        return side + lax.rem(z + 1 + k, DP_Z)

    def cell_order(k):
        return lax.rem(side + DP_Z * (1 - lax.div(k, DP_Z)), DP) + lax.rem(z + 1 + k, DP_Z)

    def dp_copy(kind, src, dst, peer):
        return remote(src, dst, "dp", sems.at[kind, 0], sems.at[kind, 1], peer)

    def gene_copy(kind, src, dst, peer):
        return remote(src, dst, "gene", sems.at[kind, 0], sems.at[kind, 1], peer)

    def pair_copy(kind, src, dst):
        return gene_copy(kind, src, dst, sibling)

    def wait_all(kind, side_of, buffer):
        pltpu.make_async_copy(buffer, buffer, sems.at[kind, side_of]).wait()

    quarter = IND // 4
    proj_copies = [
        pltpu.make_async_copy(
            proj_hbm.at[pl.ds(quarter * k, quarter)],
            proj_f32.at[pl.ds(quarter * k, quarter)],
            local_sem.at[k],
        )
        for k in range(4)
    ]
    y_copy = pltpu.make_async_copy(y_hbm, y_ref, local_sem.at[4])
    for copy in proj_copies:
        copy.start()
    y_copy.start()

    barrier = pltpu.get_barrier_semaphore()
    each(
        DP - 1,
        lambda k: pl.semaphore_signal(
            barrier, inc=1, device_id={"dp": dp_peer(k)}, device_id_type=MESH
        ),
    )
    each(
        GENE - 1,
        lambda k: pl.semaphore_signal(
            barrier, inc=1, device_id={"gene": gene_peer(k)}, device_id_type=MESH
        ),
    )
    lat_all[core, z, half] = jnp.where(core == 0, mean_ref[...], logvar_ref[...])
    pl.semaphore_wait(barrier, DP + GENE - 2)

    def latent_across():
        mine = lat_all.at[core, z, half]
        return dp_copy(ACROSS, mine, mine, across)

    latent_across().start()

    for k in range(4):
        proj_copies[k].wait()
        proj_low[quarter * k : quarter * (k + 1)] = proj_f32[
            quarter * k : quarter * (k + 1)
        ].astype(BF16)

    own_rows = proj_low[pl.ds(pl.multiple_of(BLOCK * d, BLOCK), BLOCK)]
    row_of = lax.broadcasted_iota(jnp.int32, (BLOCK, 64), 0) + BLOCK * d
    col_of = lax.broadcasted_iota(jnp.int32, (BLOCK, 64), 1) + 64 * g
    pick_rows = jnp.where(row_of == col_of, 1.0, 0.0).astype(BF16)
    moment_cols = moment_ref[:, pl.ds(pl.multiple_of(BLOCK * d, BLOCK), BLOCK)].astype(BF16)
    for o in range(SPAN):
        at = lax.rem(d + o, DP)
        start = pl.multiple_of(BLOCK * at, BLOCK)
        gram = dot(own_rows, proj_low[pl.ds(start, BLOCK)], 1, 1)
        moment_rows = dot(pick_rows, moment_ref[:, pl.ds(start, BLOCK)].astype(BF16), 1, 0)
        to_row = lax.broadcasted_iota(jnp.int32, (64, BLOCK), 0) + 64 * g
        to_col = lax.broadcasted_iota(jnp.int32, (64, BLOCK), 1) + BLOCK * at
        to_place = jnp.where(to_row == to_col, 1.0, 0.0).astype(BF16)
        moment_part = moment_rows + dot(moment_cols, to_place, 0, 0)
        block = BLOCK_WEIGHT[o] * (gram + 0.5 * moment_part)
        gram_send[:, :, BLOCK * o : BLOCK * (o + 1)] = block.reshape(GENE, ROWS, BLOCK)

    chips = GENE // 2

    def pair_gram_copy():
        return pair_copy(PAIR_GRAM, gram_send.at[pl.ds(chips * (1 - core), chips)], gram_pair)

    pair_gram_copy().start()

    latent_across().wait_recv()
    each(
        DP_Z - 1,
        lambda k: dp_copy(LATENT, lat_all.at[core, z], lat_all.at[core, z], z_peer(k)).start(),
    )

    eye_cells = lax.broadcasted_iota(jnp.int32, (CELLS, CELLS), 0) == lax.broadcasted_iota(
        jnp.int32, (CELLS, CELLS), 1
    )
    local_index = (index_ref[...] - d * IND).astype(F32)
    index_col = jnp.sum(
        jnp.where(eye_cells, jnp.broadcast_to(local_index, (CELLS, CELLS)), 0.0),
        axis=1,
        keepdims=True,
    )
    row_number = lax.broadcasted_iota(jnp.int32, (CELLS, IND), 1).astype(F32)
    one_hot = jnp.where(row_number == index_col, 1.0, 0.0).astype(BF16)
    y_copy.wait()
    cell_rows = dot(one_hot, y_ref[...], 1, 0)
    cell_all[0] = cell_rows.astype(BF16)

    pair_gram_copy().wait_recv()
    gram_sum = gram_send[pl.ds(chips * core, chips)] + gram_pair[...]
    gram_sum = jnp.concatenate([gram_sum, jnp.zeros((chips, ROWS, 128), F32)], axis=2)
    gram_out[...] = jnp.concatenate(
        [gram_sum[:, :, 0:HALF], gram_sum[:, :, HALF:]], axis=1
    ).astype(BF16)

    def gram_step(k):
        chip = chip_peer(k)
        gene_copy(GRAM, gram_out.at[chip], gram_recv.at[place], 2 * chip + core).start()

    each(chips - 1, gram_step)
    gram_recv[place] = gram_out[place]

    def cell_copy():
        return dp_copy(CELL, cell_all.at[0], cell_all.at[1], across)

    cell_copy().start()
    squares = jnp.sum((cell_rows * cell_rows).reshape(CELLS // 8, 8, GENES), axis=0)
    square_tile = functools.reduce(
        jnp.add, [squares[:, 128 * k : 128 * (k + 1)] for k in range(GENES // 128)]
    )

    kernel_log = log_var_ref[0]
    eye = lax.broadcasted_iota(jnp.int32, (LAT, LAT), 0) == lax.broadcasted_iota(
        jnp.int32, (LAT, LAT), 1
    )
    length = jnp.sum(
        jnp.where(eye, jnp.broadcast_to(length_ref[...], (LAT, LAT)), 0.0), axis=1, keepdims=True
    )

    def first_coefficients(cell_mean, inverse):
        constant = kernel_log + 0.5 * jnp.sum(
            jnp.log(length * inverse) - cell_mean * cell_mean * inverse, axis=0, keepdims=True
        )
        return cell_coefficients(
            LOG2E * cell_mean * inverse, (-0.5 * LOG2E) * inverse, LOG2E * constant, 0
        ).astype(BF16)

    mean = mean_ref[...]
    variance = jnp.exp(logvar_ref[...])
    inverse = 1.0 / (length + variance)
    features = point_features(inducing_ref[...], []).astype(BF16)
    psi_one = jnp.exp2(dot(features, first_coefficients(mean, inverse), 0, 0))
    psi_low_ref[...] = psi_one.astype(BF16)

    cross = dot(proj_low[...], cell_all[0], 1, 1)
    product = psi_one * cross
    sum_0, sum_1, sum_2 = moments(dot(features, product.astype(BF16), 1, 0))
    beta = jnp.exp(jnp.full((1, CELLS), log_beta_ref[0], F32))
    beta_sq = beta * beta
    first_ref[0:LAT] = beta_sq * inverse * (sum_1 - mean * sum_0)
    first_ref[LAT : 2 * LAT] = (
        beta_sq
        * 0.5
        * variance
        * inverse
        * (inverse * (sum_2 - 2.0 * mean * sum_1 + mean * mean * sum_0) - sum_0)
    )

    base = inducing_ref[:, pl.ds(pl.multiple_of(BLOCK * d, BLOCK), BLOCK)]
    lane = lax.broadcasted_iota(jnp.int32, (LAT, BLOCK), 1)
    quarter_inv = (-0.25 * LOG2E) / length

    def feature_step(i):
        column = jnp.sum(jnp.where(lane == ROWS * group + i, base, 0.0), axis=1, keepdims=True)
        for o in range(SPAN):
            at = lax.rem(d + o, DP)
            points = inducing_ref[:, pl.ds(pl.multiple_of(BLOCK * at, BLOCK), BLOCK)]
            gap = points - column
            pair = jnp.sum(gap * gap * quarter_inv, axis=0, keepdims=True)
            block = point_features(0.5 * (points + column), split_three(pair))
            offset = pl.multiple_of(lax.rem(i, 2) * WIDTH + BLOCK * o, BLOCK)
            pair_feat[lax.div(i, 2), :, pl.ds(offset, BLOCK)] = block.astype(BF16)
            columns = jnp.concatenate([block[0:96], block[192:224]], axis=0)
            pair_cols[lax.div(i, 2), pl.ds(offset, BLOCK)] = columns.T.astype(BF16)

    each(ROWS, feature_step)

    def latents(kind, at):
        return lat_all[kind, lax.rem(at, DP_Z), lax.div(at, DP_Z)]

    def pair_latent_copy():
        return pair_copy(PAIR_LATENT, lat_all.at[core], lat_all.at[core])

    wait_all(LATENT, 1, lat_all.at[core, pl.ds(0, DP_Z - 1)])
    pair_latent_copy().start()
    pair_latent_copy().wait_recv()

    def coefficient_step(at):
        cell_mean = latents(0, at)
        inverse_w = 1.0 / (length + 2.0 * jnp.exp(latents(1, at)))
        inv_width[at] = inverse_w
        const = 2.0 * kernel_log + jnp.sum(
            0.5 * jnp.log(length * inverse_w) - cell_mean * cell_mean * inverse_w,
            axis=0,
            keepdims=True,
        )
        block = cell_coefficients(
            (2.0 * LOG2E) * cell_mean * inverse_w, -LOG2E * inverse_w, LOG2E * const, 3
        )
        cell_coef[at] = block.T.astype(BF16)

    each(DP, coefficient_step)

    wait_all(GRAM, 1, gram_recv.at[pl.ds(0, chips - 1)])
    weight = jnp.sum(gram_recv[...].astype(F32), axis=0)
    weight = jnp.concatenate([weight[0:ROWS], weight[ROWS:, 0 : WIDTH - HALF]], axis=1)
    for i in range(ROWS):
        weight_ref[i // 2, :, WIDTH * (i % 2) : WIDTH * (i % 2 + 1)] = jnp.broadcast_to(
            weight[i : i + 1], (8, WIDTH)
        )
    psi_acc[...] = jnp.zeros_like(psi_acc)
    trace_ref[...] = jnp.zeros_like(trace_ref)

    def cell_gradients(at):
        table = jnp.zeros((CELLS, 128), F32)
        for s in range(STEPS):
            psi = jnp.exp2(dot(cell_coef[at], pair_feat[s], 1, 0))
            psi = psi.reshape(CELLS // 8, 8, PAIRS)
            psi_acc[s] += jnp.sum(psi, axis=0)
            weighted = (psi * weight_ref[s][None]).reshape(CELLS, PAIRS).astype(BF16)
            table = table + dot(weighted, pair_cols[s], 1, 0)
        table = table.T
        mom_0 = table[96:97]
        mom_1 = table[0:32] + table[64:96]
        mom_2 = table[32:64]
        cell_mean = latents(0, at)
        cell_var = jnp.exp(latents(1, at))
        inverse_w = inv_width[at]
        trace_ref[...] += mom_0
        by_mean = -beta * inverse_w * (mom_1 - cell_mean * mom_0)
        by_logvar = (
            -beta
            * cell_var
            * inverse_w
            * (
                inverse_w * (mom_2 - 2.0 * cell_mean * mom_1 + cell_mean * cell_mean * mom_0)
                - 0.5 * mom_0
            )
        )
        return by_mean, by_logvar

    def cell_step(k):
        at = cell_order(k)
        by_mean, by_logvar = cell_gradients(at)
        grad_send[at, 0:LAT] = by_mean.astype(BF16)
        grad_send[at, LAT : 2 * LAT] = by_logvar.astype(BF16)
        dp_copy(GRAD, grad_send.at[at], grad_recv.at[d], at).start()

    each(SPLIT, cell_step)

    cell_copy().wait_recv()
    side_points = inducing_ref[:, pl.ds(pl.multiple_of(BLOCK * side, BLOCK), BLOCK * DP_Z)]
    across_mean = latents(0, across)
    across_inverse = 1.0 / (length + jnp.exp(latents(1, across)))
    psi_across = jnp.exp2(
        dot(
            point_features(side_points, []).astype(BF16),
            first_coefficients(across_mean, across_inverse),
            0,
            0,
        )
    )
    psi_side[...] = psi_across.astype(BF16)

    def data_rows(at):
        near = psi_low_ref[pl.ds(pl.multiple_of(BLOCK * (side + at), BLOCK), BLOCK)]
        far = psi_side[pl.ds(pl.multiple_of(BLOCK * at, BLOCK), BLOCK)]
        return dot(near, cell_all[0], 1, 0) + dot(far, cell_all[1], 1, 0)

    def data_step(k):
        at = lax.rem(z + 1 + k, DP_Z)
        data_send[at] = data_rows(at).astype(BF16)
        dp_copy(DATA, data_send.at[at], data_recv.at[z], z_peer(k)).start()

    data_step(1)
    each(DP - 1 - SPLIT, lambda k: cell_step(k + SPLIT))
    data_step(0)
    data_step(2)
    by_mean, by_logvar = cell_gradients(d)
    first_ref[0:LAT] += by_mean
    first_ref[LAT : 2 * LAT] += by_logvar

    total_row = sum_0 - 0.5 * trace_ref[...]
    total_row = total_row[:, 0:128] + total_row[:, 128:256]
    first_row = lax.broadcasted_iota(jnp.int32, (8, 128), 0) == 0
    total_tile = jnp.where(first_row, jnp.broadcast_to(total_row, (8, 128)), 0.0) - (
        0.5 * square_tile
    )
    rows = jnp.concatenate(
        [
            jnp.sum(
                psi_acc[i // 2, :, WIDTH * (i % 2) : WIDTH * (i % 2 + 1)], axis=0, keepdims=True
            )
            for i in range(ROWS)
        ],
        axis=0,
    )
    wide = jnp.concatenate([rows, jnp.zeros((ROWS, 128), F32)], axis=1)
    psi_all[core, place] = jnp.concatenate([wide[:, 0:HALF], wide[:, HALF:]], axis=0).astype(BF16)

    own_psi = psi_all.at[core, place]
    each(
        chips - 1,
        lambda k: gene_copy(PSI, own_psi, own_psi, 2 * chip_peer(k) + core).start(),
    )

    grad_recv[d] = jnp.zeros((2 * LAT, CELLS), BF16)
    wait_all(GRAD, 1, grad_recv.at[pl.ds(0, DP - 1)])
    own_grad = first_ref[...]
    for p in range(DP):
        own_grad = own_grad + grad_recv[p].astype(F32)
    for p in range(GENE):
        part_send[p, 0:8] = own_grad[
            8 * (p // 2) : 8 * (p // 2 + 1), 128 * (p % 2) : 128 * (p % 2 + 1)
        ]
        part_send[p, 8:16] = total_tile

    def part_step(k):
        peer = gene_peer(k)
        gene_copy(PART, part_send.at[peer], part_recv.at[g], peer).start()

    each(GENE - 1, part_step)
    part_recv[g] = part_send[g]

    def pair_psi_copy():
        return pair_copy(PAIR_PSI, psi_all.at[core], psi_all.at[core])

    wait_all(PSI, 1, psi_all.at[core, pl.ds(0, chips - 1)])
    pair_psi_copy().start()

    data_own[...] = data_rows(z)

    pair_psi_copy().wait_recv()
    gathered = psi_all[...].astype(F32).reshape(GENE, 2 * ROWS, HALF)
    left = gathered[:, 0:ROWS].reshape(BLOCK, HALF)
    right = gathered[:, ROWS : 2 * ROWS].reshape(BLOCK, HALF)
    psi_rows = [
        (left if o < 3 else right)[:, BLOCK * (o % 3) : BLOCK * (o % 3 + 1)].astype(BF16)
        for o in range(SPAN)
    ]
    for o in range(1, 4):
        block_send[o - 1] = psi_rows[o]

    for o in range(1, 4):
        dp_copy(
            TURNED, block_send.at[o - 1], block_recv.at[o - 1], lax.rem(d + o, DP)
        ).start()

    wait_all(PART, 1, part_recv.at[pl.ds(0, GENE - 1)])
    part_sum = jnp.sum(part_recv[...], axis=0)
    sum_all[g] = part_sum[0:8]
    total_recv[d] = part_sum[8:16]

    own_sum = sum_all.at[g]
    own_total = total_recv.at[d]
    each(GENE - 1, lambda k: gene_copy(SUM, own_sum, own_sum, gene_peer(k)).start())
    each(DP - 1, lambda k: dp_copy(TOTAL, own_total, own_total, dp_peer(k)).start())

    stat = data_own[...]
    for o in range(SPAN):
        at = lax.rem(d + o, DP)
        stat = stat - dot(
            psi_rows[o], proj_low[pl.ds(pl.multiple_of(BLOCK * at, BLOCK), BLOCK)], 1, 0
        )
    wait_all(DATA, 1, data_recv.at[pl.ds(0, DP_Z - 1)])
    for k in range(DP_Z - 1):
        stat = stat + data_recv[lax.rem(z + 1 + k, DP_Z)].astype(F32)
    wait_all(TURNED, 1, block_recv)
    for o in range(1, 4):
        at = lax.rem(d + (DP - o), DP)
        stat = stat - dot(
            block_recv[o - 1],
            proj_low[pl.ds(pl.multiple_of(BLOCK * at, BLOCK), BLOCK)],
            0,
            0,
        )
    data_own[...] = stat * (beta[0:1, 0:1] / (CELLS * DP))
    proj_copy = pltpu.make_async_copy(data_own, proj_out, local_sem.at[0])
    proj_copy.start()

    wait_all(SUM, 1, sum_all.at[pl.ds(0, GENE - 1)])
    for p in range(GENE):
        first_ref[8 * (p // 2) : 8 * (p // 2 + 1), 128 * (p % 2) : 128 * (p % 2 + 1)] = sum_all[p]
    first_ref[0:LAT] -= mean
    first_ref[LAT : 2 * LAT] -= 0.5 * (variance - 1.0)
    out_copy = pltpu.make_async_copy(first_ref, latent_out, local_sem.at[1])
    out_copy.start()
    wait_all(TOTAL, 1, total_recv.at[pl.ds(0, DP - 1)])
    factor = beta[:, 0:128] / (CELLS * DP * GENES * GENE)
    amplitude = jnp.exp(jnp.full((1, 128), kernel_log, F32))
    rest = (0.5 - 0.5 * beta[:, 0:128] * amplitude) / 1024
    total_out[0] = jnp.sum(jnp.sum(total_recv[...], axis=0) * factor + rest)

    latent_across().wait_send()
    pair_gram_copy().wait_send()
    cell_copy().wait_send()
    pair_latent_copy().wait_send()
    pair_psi_copy().wait_send()
    wait_all(LATENT, 0, lat_all.at[core, pl.ds(0, DP_Z - 1)])
    wait_all(GRAM, 0, gram_recv.at[pl.ds(0, chips - 1)])
    wait_all(GRAD, 0, grad_recv.at[pl.ds(0, DP - 1)])
    wait_all(DATA, 0, data_recv.at[pl.ds(0, DP_Z - 1)])
    wait_all(PSI, 0, psi_all.at[core, pl.ds(0, chips - 1)])
    wait_all(PART, 0, part_recv.at[pl.ds(0, GENE - 1)])
    wait_all(TURNED, 0, block_recv)
    wait_all(SUM, 0, sum_all.at[pl.ds(0, GENE - 1)])
    wait_all(TOTAL, 0, total_recv.at[pl.ds(0, DP - 1)])
    proj_copy.wait()
    out_copy.wait()


def on_device(
    y_pool,
    cell_index,
    latent_mean,
    latent_logvar,
    inducing,
    length_sq,
    log_var,
    log_beta,
    proj_mean,
    second_moment,
):
    vmem = pl.BlockSpec(memory_space=pltpu.VMEM)
    smem = pl.BlockSpec(memory_space=pltpu.SMEM)
    hbm = pl.BlockSpec(memory_space=pl.ANY)
    scratch = [
        pltpu.VMEM((IND, GENES), F32),
        pltpu.VMEM((IND, GENES), BF16),
        pltpu.VMEM((IND, GENES), BF16),
        pltpu.VMEM((2, CELLS, GENES), BF16),
        pltpu.VMEM((IND, CELLS), BF16),
        pltpu.VMEM((DP_Z * BLOCK, CELLS), BF16),
        pltpu.VMEM((2, DP_Z, DP // DP_Z, LAT, CELLS), F32),
        pltpu.VMEM((GENE, ROWS, WIDTH), F32),
        pltpu.VMEM((GENE // 2, ROWS, WIDTH), F32),
        pltpu.VMEM((GENE // 2, 2 * ROWS, HALF), BF16),
        pltpu.VMEM((GENE // 2, 2 * ROWS, HALF), BF16),
        pltpu.VMEM((DP_Z, BLOCK, GENES), BF16),
        pltpu.VMEM((DP_Z, BLOCK, GENES), BF16),
        pltpu.VMEM((BLOCK, GENES), F32),
        pltpu.VMEM((STEPS, DEPTH, PAIRS), BF16),
        pltpu.VMEM((STEPS, PAIRS, 128), BF16),
        pltpu.VMEM((DP, CELLS, DEPTH), BF16),
        pltpu.VMEM((DP, LAT, CELLS), F32),
        pltpu.VMEM((STEPS, 8, PAIRS), F32),
        pltpu.VMEM((STEPS, 8, PAIRS), F32),
        pltpu.VMEM((2 * LAT, CELLS), F32),
        pltpu.VMEM((1, CELLS), F32),
        pltpu.VMEM((DP, 2 * LAT, CELLS), BF16),
        pltpu.VMEM((DP, 2 * LAT, CELLS), BF16),
        pltpu.VMEM((2, GENE // 2, 2 * ROWS, HALF), BF16),
        pltpu.VMEM((GENE, 16, 128), F32),
        pltpu.VMEM((GENE, 16, 128), F32),
        pltpu.VMEM((GENE, 8, 128), F32),
        pltpu.VMEM((3, BLOCK, BLOCK), BF16),
        pltpu.VMEM((3, BLOCK, BLOCK), BF16),
        pltpu.VMEM((DP, 8, 128), F32),
        pltpu.SemaphoreType.DMA((5,)),
        pltpu.SemaphoreType.DMA((KINDS, 2)),
    ]
    latent, proj, scalar = pl.pallas_call(
        kernel,
        out_shape=(
            jax.ShapeDtypeStruct((2 * LAT, CELLS), F32),
            jax.ShapeDtypeStruct((BLOCK, GENES), F32),
            jax.ShapeDtypeStruct((1,), F32),
        ),
        in_specs=[hbm, vmem, vmem, vmem, vmem, vmem, smem, smem, hbm, vmem],
        out_specs=(hbm, hbm, smem),
        scratch_shapes=scratch,
        compiler_params=pltpu.CompilerParams(
            collective_id=0, has_side_effects=True, vmem_limit_bytes=56 * 1024 * 1024
        ),
        name="bound_gradients",
    )(
        y_pool,
        cell_index.reshape(1, CELLS),
        latent_mean,
        latent_logvar,
        inducing,
        length_sq.reshape(1, LAT),
        log_var,
        log_beta,
        proj_mean,
        second_moment,
    )
    return (latent.reshape(2, LAT, CELLS), proj, scalar)


def solution(mesh):
    in_specs = (
        P("dp", "gene"),
        P("dp"),
        P(None, "dp"),
        P(None, "dp"),
        P(),
        P(),
        P(),
        P(),
        P(None, "gene"),
        P("gene", None),
    )
    out_specs = (P(None, None, "dp"), P("dp", "gene"), P())
    return jax.shard_map(
        on_device, mesh=mesh, in_specs=in_specs, out_specs=out_specs, check_vma=False
    )
```

```python
import functools

import jax
import jax.numpy as jnp
from jax import lax
from jax.experimental import pallas as pl
from jax.experimental.pallas import tpu as pltpu
from jax.sharding import PartitionSpec as P

F32 = jnp.float32
BF16 = jnp.bfloat16
LOG2E = 1.4426950408889634
MESH = pl.DeviceIdType.MESH

DP = 8
DP_Z = 4
GENE = 16
CELLS = 256
LAT = 32
IND = 1024
GENES = 1024
BLOCK = IND // DP
ROWS = BLOCK // GENE
SPAN = 5
WIDTH = SPAN * BLOCK
STEPS = 4
PAIRS = ROWS * WIDTH // STEPS
DEPTH = 256
HALF = 384
CLOSING = 4
SPLIT = 4
(
    ACROSS,
    LATENT,
    PAIR_LATENT,
    PAIR_GRAM,
    GRAM,
    CELL,
    GRAD,
    DATA,
    PSI,
    PAIR_PSI,
    PART,
    TURNED,
    PAIR_TURNED,
    PAIR_GRAD,
    PAIR_SUM,
    TOTAL,
    GRAND,
    KINDS,
) = range(18)
BLOCK_WEIGHT = (1.0, 2.0, 2.0, 2.0, 1.0)


def each(count, body):
    def step(k, carry):
        body(k)
        return carry

    lax.fori_loop(0, count, step, 0)


def split_two(value):
    high = value.astype(BF16).astype(F32)
    return high, (value - high).astype(BF16).astype(F32)


def split_three(value):
    high = value.astype(BF16).astype(F32)
    rest = value - high
    mid = rest.astype(BF16).astype(F32)
    return high, mid, (rest - mid).astype(BF16).astype(F32)


def special(rows, width):
    place = lax.broadcasted_iota(jnp.int32, (64, width), 0)
    total = jnp.zeros((64, width), F32)
    for at, row in enumerate(rows):
        total = jnp.where(place == at, jnp.broadcast_to(row, (64, width)), total)
    return total


def point_features(value, extra):
    width = value.shape[1]
    high, low = split_two(value)
    square_high, square_low = split_two(value * value)
    ones = jnp.ones((1, width), F32)
    rows = [ones, ones, ones] + list(extra)
    return jnp.concatenate(
        [high, square_high, low, square_low, high, square_high, special(rows, width)], axis=0
    )


def cell_coefficients(linear, square, constant, extra):
    width = linear.shape[1]
    high, low = split_two(linear)
    square_high, square_low = split_two(square)
    rows = list(split_three(constant)) + [jnp.ones((1, width), F32)] * extra
    return jnp.concatenate(
        [high, square_high, high, square_high, low, square_low, special(rows, width)], axis=0
    )


def moments(table):
    return table[192:193], table[0:32] + table[64:96], table[32:64] + table[96:128]


def dot(left, right, left_dim, right_dim):
    return lax.dot_general(
        left, right, (((left_dim,), (right_dim,)), ((), ())), preferred_element_type=F32
    )


def kernel(
    y_hbm,
    index_hbm,
    mean_hbm,
    logvar_hbm,
    inducing_hbm,
    length_hbm,
    log_var_ref,
    log_beta_ref,
    proj_hbm,
    moment_hbm,
    latent_out,
    proj_out,
    total_out,
    index_ref,
    mean_ref,
    logvar_ref,
    inducing_ref,
    length_ref,
    moment_ref,
    proj_f32,
    proj_low,
    y_ref,
    cell_all,
    point_feat,
    psi_one_ref,
    psi_low_ref,
    psi_side,
    lat_all,
    gram_send,
    gram_pair,
    gram_out,
    gram_recv,
    data_send,
    data_recv,
    data_own,
    base_ref,
    norm_ref,
    row_ref,
    pair_feat,
    pair_cols,
    cell_coef,
    inv_width,
    weight_ref,
    psi_acc,
    first_ref,
    trace_ref,
    grad_send,
    grad_recv,
    psi_all,
    turned_all,
    half_send,
    half_recv,
    part_all,
    sum_all,
    total_recv,
    grand_recv,
    local_sem,
    sems,
):
    d = lax.axis_index("dp")
    g = lax.axis_index("gene")
    z = lax.rem(d, DP_Z)
    half = lax.div(d, DP_Z)
    side = d - z
    across = lax.rem(d + DP_Z, DP)
    core = lax.rem(g, 2)
    place = lax.div(g, 2)
    group = GENE // 2 * core + place
    sibling = g + 1 - 2 * core
    chips = GENE // 2

    def remote(src, dst, axis, send_sem, recv_sem, peer):
        return pltpu.make_async_remote_copy(
            src_ref=src,
            dst_ref=dst,
            send_sem=send_sem,
            recv_sem=recv_sem,
            device_id={axis: peer},
            device_id_type=MESH,
        )

    def dp_peer(k):
        return lax.rem(d + 1 + k, DP)

    def gene_peer(k):
        return lax.rem(g + 1 + k, GENE)

    def chip_peer(k):
        return lax.rem(place + 1 + k, GENE // 2)

    def z_peer(k):
        return side + lax.rem(z + 1 + k, DP_Z)

    def cell_order(k):
        return lax.rem(side + DP_Z * (1 - lax.div(k, DP_Z)), DP) + lax.rem(z + 1 + k, DP_Z)

    def dp_copy(kind, src, dst, peer):
        return remote(src, dst, "dp", sems.at[kind, 0], sems.at[kind, 1], peer)

    def gene_copy(kind, src, dst, peer):
        return remote(src, dst, "gene", sems.at[kind, 0], sems.at[kind, 1], peer)

    def pair_copy(kind, src, dst):
        return gene_copy(kind, src, dst, sibling)

    def wait_all(kind, side_of, buffer):
        pltpu.make_async_copy(buffer, buffer, sems.at[kind, side_of]).wait()

    quarter = IND // 4
    proj_copies = [
        pltpu.make_async_copy(
            proj_hbm.at[pl.ds(quarter * k, quarter)],
            proj_f32.at[pl.ds(quarter * k, quarter)],
            local_sem.at[k],
        )
        for k in range(4)
    ]
    y_copy = pltpu.make_async_copy(y_hbm, y_ref, local_sem.at[4])
    small = [
        (mean_hbm, mean_ref),
        (logvar_hbm, logvar_ref),
        (moment_hbm, moment_ref),
        (inducing_hbm, inducing_ref),
        (index_hbm, index_ref),
        (length_hbm, length_ref),
    ]
    small_copies = [
        pltpu.make_async_copy(src, dst, local_sem.at[5 + k]) for k, (src, dst) in enumerate(small)
    ]
    for copy in small_copies[0:2] + proj_copies + small_copies[2:] + [y_copy]:
        copy.start()

    barrier = pltpu.get_barrier_semaphore()
    each(
        DP - 1,
        lambda k: pl.semaphore_signal(
            barrier, inc=1, device_id={"dp": dp_peer(k)}, device_id_type=MESH
        ),
    )
    each(
        GENE - 1,
        lambda k: pl.semaphore_signal(
            barrier, inc=1, device_id={"gene": gene_peer(k)}, device_id_type=MESH
        ),
    )
    def greet_step(k):
        pl.semaphore_signal(
            barrier,
            inc=1,
            device_id={
                "dp": lax.rem(d + DP - 1 - lax.div(k, chips - 1), DP),
                "gene": 2 * chip_peer(lax.rem(k, chips - 1)) + core,
            },
            device_id_type=MESH,
        )

    each(3 * (chips - 1), greet_step)
    for copy in small_copies[0:2]:
        copy.wait()
    lat_all[core, z, half] = jnp.where(core == 0, mean_ref[...], logvar_ref[...])
    pl.semaphore_wait(barrier, DP + GENE - 2 + 3 * (chips - 1))

    def latent_across():
        mine = lat_all.at[core, z, half]
        return dp_copy(ACROSS, mine, mine, across)

    latent_across().start()

    for k in range(4):
        proj_copies[k].wait()
        proj_low[quarter * k : quarter * (k + 1)] = proj_f32[
            quarter * k : quarter * (k + 1)
        ].astype(BF16)

    for copy in small_copies[2:]:
        copy.wait()
    own_rows = proj_low[pl.ds(pl.multiple_of(BLOCK * d, BLOCK), BLOCK)]
    row_of = lax.broadcasted_iota(jnp.int32, (BLOCK, 64), 0) + BLOCK * d
    col_of = lax.broadcasted_iota(jnp.int32, (BLOCK, 64), 1) + 64 * g
    pick_rows = jnp.where(row_of == col_of, 1.0, 0.0).astype(BF16)
    moment_cols = moment_ref[:, pl.ds(pl.multiple_of(BLOCK * d, BLOCK), BLOCK)].astype(BF16)
    for o in range(SPAN):
        at = lax.rem(d + o, DP)
        start = pl.multiple_of(BLOCK * at, BLOCK)
        gram = dot(own_rows, proj_low[pl.ds(start, BLOCK)], 1, 1)
        moment_rows = dot(pick_rows, moment_ref[:, pl.ds(start, BLOCK)].astype(BF16), 1, 0)
        to_row = lax.broadcasted_iota(jnp.int32, (64, BLOCK), 0) + 64 * g
        to_col = lax.broadcasted_iota(jnp.int32, (64, BLOCK), 1) + BLOCK * at
        to_place = jnp.where(to_row == to_col, 1.0, 0.0).astype(BF16)
        moment_part = moment_rows + dot(moment_cols, to_place, 0, 0)
        block = BLOCK_WEIGHT[o] * (gram + 0.5 * moment_part)
        gram_send[:, :, BLOCK * o : BLOCK * (o + 1)] = block.reshape(GENE, ROWS, BLOCK)

    def pair_gram_copy():
        return pair_copy(PAIR_GRAM, gram_send.at[pl.ds(chips * (1 - core), chips)], gram_pair)

    pair_gram_copy().start()

    eye_cells = lax.broadcasted_iota(jnp.int32, (CELLS, CELLS), 0) == lax.broadcasted_iota(
        jnp.int32, (CELLS, CELLS), 1
    )
    local_index = (index_ref[...] - d * IND).astype(F32)
    index_col = jnp.sum(
        jnp.where(eye_cells, jnp.broadcast_to(local_index, (CELLS, CELLS)), 0.0),
        axis=1,
        keepdims=True,
    )
    row_number = lax.broadcasted_iota(jnp.int32, (CELLS, IND), 1).astype(F32)
    one_hot = jnp.where(row_number == index_col, 1.0, 0.0).astype(BF16)
    y_copy.wait()
    cell_rows = dot(one_hot, y_ref[...], 1, 0)
    cell_all[0] = cell_rows.astype(BF16)

    pair_gram_copy().wait_recv()
    gram_sum = gram_send[pl.ds(chips * core, chips)] + gram_pair[...]
    gram_sum = jnp.concatenate([gram_sum, jnp.zeros((chips, ROWS, 128), F32)], axis=2)
    gram_out[...] = jnp.concatenate(
        [gram_sum[:, :, 0:HALF], gram_sum[:, :, HALF:]], axis=1
    ).astype(BF16)

    def gram_step(k):
        chip = chip_peer(k)
        gene_copy(GRAM, gram_out.at[chip], gram_recv.at[place], 2 * chip + core).start()

    each(chips - 1, gram_step)
    gram_recv[place] = gram_out[place]

    def cell_copy():
        return dp_copy(CELL, cell_all.at[0], cell_all.at[1], across)

    cell_copy().start()
    squares = jnp.sum((cell_rows * cell_rows).reshape(CELLS // 8, 8, GENES), axis=0)
    square_tile = functools.reduce(
        jnp.add, [squares[:, 128 * k : 128 * (k + 1)] for k in range(GENES // 128)]
    )

    latent_across().wait_recv()
    each(
        DP_Z - 1,
        lambda k: dp_copy(LATENT, lat_all.at[core, z], lat_all.at[core, z], z_peer(k)).start(),
    )

    kernel_log = log_var_ref[0]
    eye = lax.broadcasted_iota(jnp.int32, (LAT, LAT), 0) == lax.broadcasted_iota(
        jnp.int32, (LAT, LAT), 1
    )
    length = jnp.sum(
        jnp.where(eye, jnp.broadcast_to(length_ref[...], (LAT, LAT)), 0.0), axis=1, keepdims=True
    )

    def first_coefficients(cell_mean, inverse):
        constant = kernel_log + 0.5 * jnp.sum(
            jnp.log(length * inverse) - cell_mean * cell_mean * inverse, axis=0, keepdims=True
        )
        return cell_coefficients(
            LOG2E * cell_mean * inverse, (-0.5 * LOG2E) * inverse, LOG2E * constant, 0
        ).astype(BF16)

    mean = mean_ref[...]
    variance = jnp.exp(logvar_ref[...])
    inverse = 1.0 / (length + variance)
    point_feat[...] = point_features(inducing_ref[...], []).astype(BF16)
    psi_one_ref[...] = jnp.exp2(dot(point_feat[...], first_coefficients(mean, inverse), 0, 0))
    psi_low_ref[...] = psi_one_ref[...].astype(BF16)
    beta = jnp.exp(jnp.full((1, CELLS), log_beta_ref[0], F32))

    lane = lax.broadcasted_iota(jnp.int32, (BLOCK, BLOCK), 1)
    squared = lax.rem(lane, 2 * LAT) >= LAT
    high_part = lane < 2 * LAT
    ones = jnp.where((lane >= 64) & (lane < 67), 1.0, 0.0)
    half_inv = (-0.5 * LOG2E) / length

    def window(o):
        at = lax.rem(d + o, DP)
        return inducing_ref[:, pl.ds(pl.multiple_of(BLOCK * at, BLOCK), BLOCK)]

    for o in range(SPAN):
        points = window(o)
        norm = jnp.sum(points * points * half_inv, axis=0, keepdims=True)
        base_ref[o] = jnp.concatenate([points] * 4, axis=0).T
        norm_ref[o] = jnp.broadcast_to(norm, (BLOCK, BLOCK)).T
    own_point = base_ref[0, pl.ds(pl.multiple_of(ROWS * group, ROWS), ROWS)]
    own_norm = norm_ref[0, pl.ds(pl.multiple_of(ROWS * group, ROWS), ROWS)]
    row_ref[0] = own_point
    row_ref[1] = own_norm

    def feature_step(i):
        row = row_ref[0, pl.ds(i, 1)]
        row_norm = row_ref[1, pl.ds(i, 1)]
        for o in range(SPAN):
            middle = 0.5 * (base_ref[o] + row)
            value = jnp.where(squared, middle * middle, middle)
            high = value.astype(BF16).astype(F32)
            pair = split_three(norm_ref[o] + row_norm)
            extra = ones
            for k in range(3):
                extra = jnp.where(lane == 67 + k, pair[k], extra)
            offset = pl.multiple_of(lax.rem(i, 2) * WIDTH + BLOCK * o, BLOCK)
            at = pl.ds(offset, BLOCK)
            step = lax.div(i, 2)
            pair_feat[step, at, 0:128] = jnp.where(high_part, high, value - high).astype(BF16)
            pair_feat[step, at, 128:256] = jnp.where(high_part, high, extra).astype(BF16)

    each(ROWS, feature_step)

    cross = dot(proj_low[...], cell_all[0], 1, 1)
    product = psi_one_ref[...] * cross
    sum_0, sum_1, sum_2 = moments(dot(point_feat[...], product.astype(BF16), 1, 0))
    beta_sq = beta * beta
    first_ref[0:LAT] = beta_sq * inverse * (sum_1 - mean * sum_0)
    first_ref[LAT : 2 * LAT] = (
        beta_sq
        * 0.5
        * variance
        * inverse
        * (inverse * (sum_2 - 2.0 * mean * sum_1 + mean * mean * sum_0) - sum_0)
    )

    def latents(kind, at):
        return lat_all[kind, lax.rem(at, DP_Z), lax.div(at, DP_Z)]

    def pair_latent_copy():
        return pair_copy(PAIR_LATENT, lat_all.at[core], lat_all.at[core])

    wait_all(LATENT, 1, lat_all.at[core, pl.ds(0, DP_Z - 1)])
    pair_latent_copy().start()
    wait_all(GRAM, 1, gram_recv.at[pl.ds(0, chips - 1)])
    weight = jnp.sum(gram_recv[...].astype(F32), axis=0)
    weight = jnp.concatenate([weight[0:ROWS], weight[ROWS:, 0 : WIDTH - HALF]], axis=1)
    weight_ref[...] = weight
    base = window(0)
    own_lane = lax.broadcasted_iota(jnp.int32, (LAT, BLOCK), 1) - ROWS * group

    def weight_step(i):
        column = jnp.sum(jnp.where(own_lane == i, base, 0.0), axis=1, keepdims=True)
        row = weight_ref[pl.ds(i, 1)]
        for o in range(SPAN):
            weight_row = row[:, BLOCK * o : BLOCK * (o + 1)]
            middle = 0.5 * (window(o) + column)
            linear = middle * weight_row
            high, low = split_two(linear)
            block = jnp.concatenate(
                [high, middle * linear, low, special(split_two(weight_row), BLOCK)[0:32]], axis=0
            )
            offset = pl.multiple_of(lax.rem(i, 2) * WIDTH + BLOCK * o, BLOCK)
            pair_cols[lax.div(i, 2), :, pl.ds(offset, BLOCK)] = block.astype(BF16)

    each(ROWS, weight_step)
    psi_acc[...] = jnp.zeros_like(psi_acc)
    trace_ref[...] = jnp.zeros_like(trace_ref)

    pair_latent_copy().wait_recv()

    def coefficient_step(at):
        cell_mean = latents(0, at)
        cell_var = jnp.exp(latents(1, at))
        inverse_w = 1.0 / (length + 2.0 * cell_var)
        inv_width[at] = inverse_w
        const = 2.0 * kernel_log + jnp.sum(
            0.5 * jnp.log(length * inverse_w) - cell_mean * cell_mean * inverse_w,
            axis=0,
            keepdims=True,
        )
        block = cell_coefficients(
            (2.0 * LOG2E) * cell_mean * inverse_w,
            (2.0 * LOG2E) * cell_var * inverse_w / length,
            LOG2E * const,
            3,
        )
        cell_coef[at] = block.astype(BF16)

    each(DP, coefficient_step)

    def cell_gradients(at):
        table = jnp.zeros((128, CELLS), F32)
        for s in range(STEPS):
            psi = jnp.exp2(dot(pair_feat[s], cell_coef[at], 1, 0))
            psi_acc[s] += psi[:, 0:128] + psi[:, 128:256]
            table = table + dot(pair_cols[s], psi.astype(BF16), 1, 0)
        mom_0 = table[96:97] + table[97:98]
        mom_1 = table[0:32] + table[64:96]
        mom_2 = table[32:64]
        cell_mean = latents(0, at)
        cell_var = jnp.exp(latents(1, at))
        inverse_w = inv_width[at]
        trace_ref[...] += mom_0
        by_mean = -beta * inverse_w * (mom_1 - cell_mean * mom_0)
        by_logvar = (
            -beta
            * cell_var
            * inverse_w
            * (
                inverse_w * (mom_2 - 2.0 * cell_mean * mom_1 + cell_mean * cell_mean * mom_0)
                - 0.5 * mom_0
            )
        )
        return by_mean, by_logvar

    def cell_step(k):
        at = cell_order(k)
        by_mean, by_logvar = cell_gradients(at)
        grad_send[at, 0:LAT] = by_mean.astype(BF16)
        grad_send[at, LAT : 2 * LAT] = by_logvar.astype(BF16)
        dp_copy(GRAD, grad_send.at[at], grad_recv.at[d], at).start()

    each(SPLIT, cell_step)

    cell_copy().wait_recv()
    side_points = inducing_ref[:, pl.ds(pl.multiple_of(BLOCK * side, BLOCK), BLOCK * DP_Z)]
    across_mean = latents(0, across)
    across_inverse = 1.0 / (length + jnp.exp(latents(1, across)))
    psi_across = jnp.exp2(
        dot(
            point_features(side_points, []).astype(BF16),
            first_coefficients(across_mean, across_inverse),
            0,
            0,
        )
    )
    psi_side[...] = psi_across.astype(BF16)

    def data_rows(at):
        near = psi_low_ref[pl.ds(pl.multiple_of(BLOCK * (side + at), BLOCK), BLOCK)]
        far = psi_side[pl.ds(pl.multiple_of(BLOCK * at, BLOCK), BLOCK)]
        return dot(near, cell_all[0], 1, 0) + dot(far, cell_all[1], 1, 0)

    def data_step(k):
        at = lax.rem(z + 1 + k, DP_Z)
        data_send[at] = data_rows(at).astype(BF16)
        dp_copy(DATA, data_send.at[at], data_recv.at[z], z_peer(k)).start()

    data_step(1)
    each(DP - 1 - SPLIT, lambda k: cell_step(k + SPLIT))
    by_mean, by_logvar = cell_gradients(d)
    first_ref[0:LAT] += by_mean
    first_ref[LAT : 2 * LAT] += by_logvar

    add_lanes = jnp.ones((16, 128), BF16)
    sums = [dot(add_lanes, psi_acc[s].astype(BF16), 1, 1)[0:1] for s in range(STEPS)]
    rows = jnp.concatenate(
        [sums[i // 2][:, WIDTH * (i % 2) : WIDTH * (i % 2 + 1)] for i in range(ROWS)], axis=0
    )
    psi_all[core, place] = rows
    own_psi = psi_all.at[core, place]

    def turned_step(k):
        chip = chip_peer(k)
        for o in range(1, 4):
            pltpu.make_async_remote_copy(
                src_ref=psi_all.at[core, place, :, pl.ds(BLOCK * o, BLOCK)],
                dst_ref=turned_all.at[core, o - 1, place],
                send_sem=sems.at[TURNED, 0],
                recv_sem=sems.at[TURNED, 1],
                device_id={"dp": lax.rem(d + o, DP), "gene": 2 * chip + core},
                device_id_type=MESH,
            ).start()

    each(chips, turned_step)
    each(
        chips - 1,
        lambda k: gene_copy(PSI, own_psi, own_psi, 2 * chip_peer(k) + core).start(),
    )

    total_row = sum_0 - 0.5 * trace_ref[...]
    total_row = total_row[:, 0:128] + total_row[:, 128:256]
    total_row = total_row - 0.5 * jnp.sum(square_tile, axis=0, keepdims=True)
    first_row = lax.broadcasted_iota(jnp.int32, (8, 128), 0) == 0
    total_recv[d] = jnp.where(first_row, jnp.broadcast_to(total_row, (8, 128)), 0.0)
    own_total = total_recv.at[d]
    each(DP - 1, lambda k: dp_copy(TOTAL, own_total, own_total, dp_peer(k)).start())

    data_step(0)
    data_step(2)

    grad_recv[d] = jnp.zeros((2 * LAT, CELLS), BF16)
    wait_all(GRAD, 1, grad_recv.at[pl.ds(0, DP - 1)])
    own_grad = first_ref[...]
    for p in range(DP):
        own_grad = own_grad + grad_recv[p].astype(F32)
    first_ref[...] = own_grad
    give = jnp.where(core == 0, own_grad[LAT : 2 * LAT], own_grad[0:LAT])
    keep = jnp.where(core == 0, own_grad[0:LAT], own_grad[LAT : 2 * LAT])
    half_send[...] = give

    def pair_grad_copy():
        return pair_copy(PAIR_GRAD, half_send, half_recv)

    pair_grad_copy().start()

    data_own[...] = data_rows(z)

    pair_grad_copy().wait_recv()
    part_all[place] = (keep + half_recv[...]).astype(BF16)
    own_part = part_all.at[place]
    each(
        chips - 1,
        lambda k: gene_copy(PART, own_part, own_part, 2 * chip_peer(k) + core).start(),
    )

    wait_all(TOTAL, 1, total_recv.at[pl.ds(0, DP - 1)])
    grand_recv[g] = jnp.sum(total_recv[...], axis=0)
    own_grand = grand_recv.at[g]
    each(GENE - 1, lambda k: gene_copy(GRAND, own_grand, own_grand, gene_peer(k)).start())

    def pair_psi_copy():
        return pair_copy(PAIR_PSI, psi_all.at[core], psi_all.at[core])

    def pair_turned_copy():
        return pair_copy(PAIR_TURNED, turned_all.at[core], turned_all.at[core])

    wait_all(PSI, 1, psi_all.at[core, pl.ds(0, chips - 1)])
    pair_psi_copy().start()
    wait_all(TURNED, 1, turned_all.at[core])
    pair_turned_copy().start()

    pair_psi_copy().wait_recv()
    psi_rows = psi_all[...].reshape(BLOCK, WIDTH).astype(BF16)
    stat = data_own[...]
    for o in range(SPAN):
        at = lax.rem(d + o, DP)
        stat = stat - dot(
            psi_rows[:, BLOCK * o : BLOCK * (o + 1)],
            proj_low[pl.ds(pl.multiple_of(BLOCK * at, BLOCK), BLOCK)],
            1,
            0,
        )
    data_own[...] = stat

    wait_all(PART, 1, part_all.at[pl.ds(0, chips - 1)])
    sum_all[core] = jnp.sum(part_all[...].astype(F32), axis=0)

    def pair_sum_copy():
        return pair_copy(PAIR_SUM, sum_all.at[core], sum_all.at[core])

    pair_sum_copy().start()

    wait_all(DATA, 1, data_recv.at[pl.ds(0, DP_Z - 1)])
    stat = data_own[...]
    for k in range(DP_Z - 1):
        stat = stat + data_recv[lax.rem(z + 1 + k, DP_Z)].astype(F32)
    pair_turned_copy().wait_recv()
    for o in range(1, 4):
        at = lax.rem(d + (DP - o), DP)
        stat = stat - dot(
            turned_all[:, o - 1].reshape(BLOCK, BLOCK).astype(BF16),
            proj_low[pl.ds(pl.multiple_of(BLOCK * at, BLOCK), BLOCK)],
            0,
            0,
        )
    data_own[...] = stat * (beta[0:1, 0:1] / (CELLS * DP))
    proj_copy = pltpu.make_async_copy(data_own, proj_out, local_sem.at[0])
    proj_copy.start()

    pair_sum_copy().wait_recv()
    first_ref[0:LAT] = sum_all[0] - mean
    first_ref[LAT : 2 * LAT] = sum_all[1] - 0.5 * (variance - 1.0)
    out_copy = pltpu.make_async_copy(first_ref, latent_out, local_sem.at[1])
    out_copy.start()

    wait_all(GRAND, 1, grand_recv.at[pl.ds(0, GENE - 1)])
    factor = beta[:, 0:128] / (CELLS * DP * GENES * GENE)
    amplitude = jnp.exp(jnp.full((1, 128), kernel_log, F32))
    rest = (0.5 - 0.5 * beta[:, 0:128] * amplitude) / 1024
    total_out[0] = jnp.sum(jnp.sum(grand_recv[...], axis=0) * factor + rest)

    latent_across().wait_send()
    pair_gram_copy().wait_send()
    cell_copy().wait_send()
    pair_latent_copy().wait_send()
    pair_psi_copy().wait_send()
    wait_all(LATENT, 0, lat_all.at[core, pl.ds(0, DP_Z - 1)])
    wait_all(GRAM, 0, gram_recv.at[pl.ds(0, chips - 1)])
    wait_all(GRAD, 0, grad_recv.at[pl.ds(0, DP - 1)])
    wait_all(DATA, 0, data_recv.at[pl.ds(0, DP_Z - 1)])
    wait_all(PSI, 0, psi_all.at[core, pl.ds(0, chips - 1)])
    wait_all(PART, 0, part_all.at[pl.ds(0, chips - 1)])
    wait_all(TURNED, 0, turned_all.at[core])
    pair_turned_copy().wait_send()
    pair_grad_copy().wait_send()
    pair_sum_copy().wait_send()
    wait_all(GRAND, 0, grand_recv.at[pl.ds(0, GENE - 1)])
    wait_all(TOTAL, 0, total_recv.at[pl.ds(0, DP - 1)])
    proj_copy.wait()
    out_copy.wait()


def finish(latent_ref, proj_ref, latent_out, proj_out, latent_held, proj_held, done):
    rows = BLOCK // CLOSING
    cuts = [pl.ds(rows * k, rows) for k in range(CLOSING)]
    pairs = [(proj_ref.at[c], proj_held.at[c], proj_out.at[c]) for c in cuts]
    pairs.append((latent_ref, latent_held, latent_out))
    loads = [
        pltpu.make_async_copy(src, held, done.at[0, k]) for k, (src, held, _) in enumerate(pairs)
    ]
    stores = [
        pltpu.make_async_copy(held, dst, done.at[1, k]) for k, (_, held, dst) in enumerate(pairs)
    ]
    for load in loads:
        load.start()
    for load, store in zip(loads, stores):
        load.wait()
        store.start()
    for store in stores:
        store.wait()


def on_device(
    y_pool,
    cell_index,
    latent_mean,
    latent_logvar,
    inducing,
    length_sq,
    log_var,
    log_beta,
    proj_mean,
    second_moment,
):
    smem = pl.BlockSpec(memory_space=pltpu.SMEM)
    hbm = pl.BlockSpec(memory_space=pl.ANY)
    scratch = [
        pltpu.VMEM((1, CELLS), jnp.int32),
        pltpu.VMEM((LAT, CELLS), F32),
        pltpu.VMEM((LAT, CELLS), F32),
        pltpu.VMEM((LAT, IND), F32),
        pltpu.VMEM((1, LAT), F32),
        pltpu.VMEM((IND // GENE, IND), F32),
        pltpu.VMEM((IND, GENES), F32),
        pltpu.VMEM((IND, GENES), BF16),
        pltpu.VMEM((IND, GENES), BF16),
        pltpu.VMEM((2, CELLS, GENES), BF16),
        pltpu.VMEM((DEPTH, IND), BF16),
        pltpu.VMEM((IND, CELLS), F32),
        pltpu.VMEM((IND, CELLS), BF16),
        pltpu.VMEM((DP_Z * BLOCK, CELLS), BF16),
        pltpu.VMEM((2, DP_Z, DP // DP_Z, LAT, CELLS), F32),
        pltpu.VMEM((GENE, ROWS, WIDTH), F32),
        pltpu.VMEM((GENE // 2, ROWS, WIDTH), F32),
        pltpu.VMEM((GENE // 2, 2 * ROWS, HALF), BF16),
        pltpu.VMEM((GENE // 2, 2 * ROWS, HALF), BF16),
        pltpu.VMEM((DP_Z, BLOCK, GENES), BF16),
        pltpu.VMEM((DP_Z, BLOCK, GENES), BF16),
        pltpu.VMEM((BLOCK, GENES), F32),
        pltpu.VMEM((SPAN, BLOCK, BLOCK), F32),
        pltpu.VMEM((SPAN, BLOCK, BLOCK), F32),
        pltpu.VMEM((2, ROWS, BLOCK), F32),
        pltpu.VMEM((STEPS, PAIRS, DEPTH), BF16),
        pltpu.VMEM((STEPS, 128, PAIRS), BF16),
        pltpu.VMEM((DP, DEPTH, CELLS), BF16),
        pltpu.VMEM((DP, LAT, CELLS), F32),
        pltpu.VMEM((ROWS, WIDTH), F32),
        pltpu.VMEM((STEPS, PAIRS, 128), F32),
        pltpu.VMEM((2 * LAT, CELLS), F32),
        pltpu.VMEM((1, CELLS), F32),
        pltpu.VMEM((DP, 2 * LAT, CELLS), BF16),
        pltpu.VMEM((DP, 2 * LAT, CELLS), BF16),
        pltpu.VMEM((2, GENE // 2, ROWS, WIDTH), F32),
        pltpu.VMEM((2, 3, GENE // 2, ROWS, BLOCK), F32),
        pltpu.VMEM((LAT, CELLS), F32),
        pltpu.VMEM((LAT, CELLS), F32),
        pltpu.VMEM((GENE // 2, LAT, CELLS), BF16),
        pltpu.VMEM((2, LAT, CELLS), F32),
        pltpu.VMEM((DP, 8, 128), F32),
        pltpu.VMEM((GENE, 8, 128), F32),
        pltpu.SemaphoreType.DMA((11,)),
        pltpu.SemaphoreType.DMA((KINDS, 2)),
    ]
    latent, proj, scalar = pl.pallas_call(
        kernel,
        out_shape=(
            jax.ShapeDtypeStruct((2 * LAT, CELLS), F32),
            jax.ShapeDtypeStruct((BLOCK, GENES), F32),
            jax.ShapeDtypeStruct((1,), F32),
        ),
        in_specs=[hbm] * 6 + [smem, smem, hbm, hbm],
        out_specs=(hbm, hbm, smem),
        scratch_shapes=scratch,
        compiler_params=pltpu.CompilerParams(
            collective_id=0, has_side_effects=True, vmem_limit_bytes=56 * 1024 * 1024
        ),
        name="bound_gradients",
    )(
        y_pool,
        cell_index.reshape(1, CELLS),
        latent_mean,
        latent_logvar,
        inducing,
        length_sq.reshape(1, LAT),
        log_var,
        log_beta,
        proj_mean,
        second_moment,
    )
    latent, proj = pl.pallas_call(
        finish,
        out_shape=(
            jax.ShapeDtypeStruct((2 * LAT, CELLS), F32),
            jax.ShapeDtypeStruct((BLOCK, GENES), F32),
        ),
        in_specs=[hbm, hbm],
        out_specs=(hbm, hbm),
        scratch_shapes=[
            pltpu.VMEM((2 * LAT, CELLS), F32),
            pltpu.VMEM((BLOCK, GENES), F32),
            pltpu.SemaphoreType.DMA((2, CLOSING + 1)),
        ],
        name="finish",
    )(latent, proj)
    return (latent.reshape(2, LAT, CELLS), proj, scalar)


def solution(mesh):
    in_specs = (
        P("dp", "gene"),
        P("dp"),
        P(None, "dp"),
        P(None, "dp"),
        P(),
        P(),
        P(),
        P(),
        P(None, "gene"),
        P("gene", None),
    )
    out_specs = (P(None, None, "dp"), P("dp", "gene"), P())
    return jax.shard_map(
        on_device, mesh=mesh, in_specs=in_specs, out_specs=out_specs, check_vma=False
    )
```

```python
import functools

import jax
import jax.numpy as jnp
from jax import lax
from jax.experimental import pallas as pl
from jax.experimental.pallas import tpu as pltpu
from jax.sharding import PartitionSpec as P

F32 = jnp.float32
BF16 = jnp.bfloat16
LOG2E = 1.4426950408889634
MESH = pl.DeviceIdType.MESH

DP = 8
DP_Z = 4
GENE = 16
CELLS = 256
LAT = 32
IND = 1024
GENES = 1024
BLOCK = IND // DP
ROWS = BLOCK // GENE
SPAN = 5
WIDTH = SPAN * BLOCK
STEPS = 4
PAIRS = ROWS * WIDTH // STEPS
DEPTH = 256
HALF = 384
CLOSING = 4
FIRST = 64
(
    ACROSS,
    LATENT,
    PAIR_LATENT,
    PAIR_GRAM,
    GRAM,
    CELL,
    GRAD,
    DATA,
    PSI,
    PAIR_PSI,
    PART,
    TURNED,
    PAIR_TURNED,
    PAIR_GRAD,
    PAIR_SUM,
    TOTAL,
    EARLY,
    OVER,
    KINDS,
) = range(19)
BLOCK_WEIGHT = (1.0, 2.0, 2.0, 2.0, 1.0)


def each(count, body):
    def step(k, carry):
        body(k)
        return carry

    lax.fori_loop(0, count, step, 0)


def every(count, body):
    for k in range(count):
        body(k)


def split_two(value):
    high = value.astype(BF16).astype(F32)
    return high, (value - high).astype(BF16).astype(F32)


def split_three(value):
    high = value.astype(BF16).astype(F32)
    rest = value - high
    mid = rest.astype(BF16).astype(F32)
    return high, mid, (rest - mid).astype(BF16).astype(F32)


def special(rows, width):
    place = lax.broadcasted_iota(jnp.int32, (64, width), 0)
    total = jnp.zeros((64, width), F32)
    for at, row in enumerate(rows):
        total = jnp.where(place == at, jnp.broadcast_to(row, (64, width)), total)
    return total


def point_features(value, extra):
    width = value.shape[1]
    high, low = split_two(value)
    square_high, square_low = split_two(value * value)
    ones = jnp.ones((1, width), F32)
    rows = [ones, ones, ones] + list(extra)
    return jnp.concatenate(
        [high, square_high, low, square_low, high, square_high, special(rows, width)], axis=0
    )


def cell_coefficients(linear, square, constant, extra):
    width = linear.shape[1]
    high, low = split_two(linear)
    square_high, square_low = split_two(square)
    rows = list(split_three(constant)) + [jnp.ones((1, width), F32)] * extra
    return jnp.concatenate(
        [high, square_high, high, square_high, low, square_low, special(rows, width)], axis=0
    )


def moments(table):
    return table[192:193], table[0:32] + table[64:96], table[32:64] + table[96:128]


def dot(left, right, left_dim, right_dim):
    return lax.dot_general(
        left, right, (((left_dim,), (right_dim,)), ((), ())), preferred_element_type=F32
    )


def kernel(
    y_hbm,
    index_hbm,
    mean_hbm,
    logvar_hbm,
    inducing_hbm,
    length_hbm,
    log_var_ref,
    log_beta_ref,
    proj_hbm,
    moment_hbm,
    latent_out,
    proj_out,
    total_out,
    index_ref,
    mean_ref,
    logvar_ref,
    inducing_ref,
    length_ref,
    moment_ref,
    proj_f32,
    proj_low,
    y_ref,
    cell_all,
    point_feat,
    psi_one_ref,
    psi_low_ref,
    psi_side,
    lat_all,
    gram_send,
    gram_pair,
    gram_out,
    gram_recv,
    early_send,
    early_recv,
    early_own,
    over_send,
    over_recv,
    data_send,
    data_recv,
    data_own,
    base_ref,
    norm_ref,
    row_ref,
    pair_feat,
    pair_cols,
    cell_coef,
    inv_width,
    weight_ref,
    psi_acc,
    first_ref,
    trace_ref,
    grad_send,
    grad_recv,
    psi_all,
    turned_all,
    half_send,
    half_recv,
    part_all,
    sum_all,
    total_recv,
    local_sem,
    sems,
):
    d = lax.axis_index("dp")
    g = lax.axis_index("gene")
    z = lax.rem(d, DP_Z)
    half = lax.div(d, DP_Z)
    side = d - z
    across = lax.rem(d + DP_Z, DP)
    core = lax.rem(g, 2)
    place = lax.div(g, 2)
    group = GENE // 2 * core + place
    sibling = g + 1 - 2 * core
    chips = GENE // 2

    def remote(src, dst, axis, send_sem, recv_sem, peer):
        return pltpu.make_async_remote_copy(
            src_ref=src,
            dst_ref=dst,
            send_sem=send_sem,
            recv_sem=recv_sem,
            device_id={axis: peer},
            device_id_type=MESH,
        )

    def dp_peer(k):
        return lax.rem(d + 1 + k, DP)

    def gene_peer(k):
        return lax.rem(g + 1 + k, GENE)

    def chip_peer(k):
        return lax.rem(place + 1 + k, GENE // 2)

    def z_peer(k):
        return side + lax.rem(z + 1 + k, DP_Z)

    def cell_order(k):
        return lax.rem(side + DP_Z * (1 - lax.div(k, DP_Z)), DP) + lax.rem(z + 1 + k, DP_Z)

    def dp_copy(kind, src, dst, peer):
        return remote(src, dst, "dp", sems.at[kind, 0], sems.at[kind, 1], peer)

    def gene_copy(kind, src, dst, peer):
        return remote(src, dst, "gene", sems.at[kind, 0], sems.at[kind, 1], peer)

    def pair_copy(kind, src, dst):
        return gene_copy(kind, src, dst, sibling)

    def wait_all(kind, side_of, buffer):
        pltpu.make_async_copy(buffer, buffer, sems.at[kind, side_of]).wait()

    quarter = IND // 4
    proj_copies = [
        pltpu.make_async_copy(
            proj_hbm.at[pl.ds(quarter * k, quarter)],
            proj_f32.at[pl.ds(quarter * k, quarter)],
            local_sem.at[k],
        )
        for k in range(4)
    ]
    y_copy = pltpu.make_async_copy(y_hbm, y_ref, local_sem.at[4])
    small = [
        (mean_hbm, mean_ref),
        (logvar_hbm, logvar_ref),
        (moment_hbm, moment_ref),
        (inducing_hbm, inducing_ref),
        (index_hbm, index_ref),
        (length_hbm, length_ref),
    ]
    small_copies = [
        pltpu.make_async_copy(src, dst, local_sem.at[5 + k]) for k, (src, dst) in enumerate(small)
    ]
    for copy in small_copies[0:2] + proj_copies + small_copies[2:] + [y_copy]:
        copy.start()

    barrier = pltpu.get_barrier_semaphore()
    every(
        DP - 1,
        lambda k: pl.semaphore_signal(
            barrier, inc=1, device_id={"dp": dp_peer(k)}, device_id_type=MESH
        ),
    )
    every(
        GENE - 1,
        lambda k: pl.semaphore_signal(
            barrier, inc=1, device_id={"gene": gene_peer(k)}, device_id_type=MESH
        ),
    )
    def greet_step(k):
        pl.semaphore_signal(
            barrier,
            inc=1,
            device_id={
                "dp": lax.rem(d + DP - 1 - k // (chips - 1), DP),
                "gene": 2 * chip_peer(k % (chips - 1)) + core,
            },
            device_id_type=MESH,
        )

    every(3 * (chips - 1), greet_step)
    for copy in small_copies[0:2]:
        copy.wait()
    lat_all[core, z, half] = jnp.where(core == 0, mean_ref[...], logvar_ref[...])
    pl.semaphore_wait(barrier, DP + GENE - 2 + 3 * (chips - 1))

    def latent_across():
        mine = lat_all.at[core, z, half]
        return dp_copy(ACROSS, mine, mine, across)

    latent_across().start()

    for k in range(4):
        proj_copies[k].wait()
        proj_low[quarter * k : quarter * (k + 1)] = proj_f32[
            quarter * k : quarter * (k + 1)
        ].astype(BF16)

    for copy in small_copies[2:]:
        copy.wait()
    own_rows = proj_low[pl.ds(pl.multiple_of(BLOCK * d, BLOCK), BLOCK)]
    row_of = lax.broadcasted_iota(jnp.int32, (BLOCK, 64), 0) + BLOCK * d
    col_of = lax.broadcasted_iota(jnp.int32, (BLOCK, 64), 1) + 64 * g
    pick_rows = jnp.where(row_of == col_of, 1.0, 0.0).astype(BF16)
    moment_cols = moment_ref[:, pl.ds(pl.multiple_of(BLOCK * d, BLOCK), BLOCK)].astype(BF16)
    for o in range(SPAN):
        at = lax.rem(d + o, DP)
        start = pl.multiple_of(BLOCK * at, BLOCK)
        gram = dot(own_rows, proj_low[pl.ds(start, BLOCK)], 1, 1)
        moment_rows = dot(pick_rows, moment_ref[:, pl.ds(start, BLOCK)].astype(BF16), 1, 0)
        to_row = lax.broadcasted_iota(jnp.int32, (64, BLOCK), 0) + 64 * g
        to_col = lax.broadcasted_iota(jnp.int32, (64, BLOCK), 1) + BLOCK * at
        to_place = jnp.where(to_row == to_col, 1.0, 0.0).astype(BF16)
        moment_part = moment_rows + dot(moment_cols, to_place, 0, 0)
        block = BLOCK_WEIGHT[o] * (gram + 0.5 * moment_part)
        gram_send[:, :, BLOCK * o : BLOCK * (o + 1)] = block.reshape(GENE, ROWS, BLOCK)

    def pair_gram_copy():
        return pair_copy(PAIR_GRAM, gram_send.at[pl.ds(chips * (1 - core), chips)], gram_pair)

    pair_gram_copy().start()

    eye_cells = lax.broadcasted_iota(jnp.int32, (CELLS, CELLS), 0) == lax.broadcasted_iota(
        jnp.int32, (CELLS, CELLS), 1
    )
    local_index = (index_ref[...] - d * IND).astype(F32)
    index_col = jnp.sum(
        jnp.where(eye_cells, jnp.broadcast_to(local_index, (CELLS, CELLS)), 0.0),
        axis=1,
        keepdims=True,
    )
    row_number = lax.broadcasted_iota(jnp.int32, (CELLS, IND), 1).astype(F32)
    one_hot = jnp.where(row_number == index_col, 1.0, 0.0).astype(BF16)
    y_copy.wait()
    cell_rows = dot(one_hot, y_ref[...], 1, 0)
    cell_all[0] = cell_rows.astype(BF16)

    pair_gram_copy().wait_recv()
    gram_sum = gram_send[pl.ds(chips * core, chips)] + gram_pair[...]
    gram_sum = jnp.concatenate([gram_sum, jnp.zeros((chips, ROWS, 128), F32)], axis=2)
    gram_out[...] = jnp.concatenate(
        [gram_sum[:, :, 0:HALF], gram_sum[:, :, HALF:]], axis=1
    ).astype(BF16)

    def gram_step(k):
        chip = chip_peer(k)
        gene_copy(GRAM, gram_out.at[chip], gram_recv.at[place], 2 * chip + core).start()

    every(chips - 1, gram_step)
    gram_recv[place] = gram_out[place]

    def cell_copy():
        return dp_copy(CELL, cell_all.at[0], cell_all.at[1], across)

    cell_copy().start()
    squares = jnp.sum((cell_rows * cell_rows).reshape(CELLS // 8, 8, GENES), axis=0)
    square_tile = functools.reduce(
        jnp.add, [squares[:, 128 * k : 128 * (k + 1)] for k in range(GENES // 128)]
    )

    latent_across().wait_recv()
    every(
        DP_Z - 1,
        lambda k: dp_copy(LATENT, lat_all.at[core, z], lat_all.at[core, z], z_peer(k)).start(),
    )

    kernel_log = log_var_ref[0]
    eye = lax.broadcasted_iota(jnp.int32, (LAT, LAT), 0) == lax.broadcasted_iota(
        jnp.int32, (LAT, LAT), 1
    )
    length = jnp.sum(
        jnp.where(eye, jnp.broadcast_to(length_ref[...], (LAT, LAT)), 0.0), axis=1, keepdims=True
    )

    def first_coefficients(cell_mean, inverse):
        constant = kernel_log + 0.5 * jnp.sum(
            jnp.log(length * inverse) - cell_mean * cell_mean * inverse, axis=0, keepdims=True
        )
        return cell_coefficients(
            LOG2E * cell_mean * inverse, (-0.5 * LOG2E) * inverse, LOG2E * constant, 0
        ).astype(BF16)

    mean = mean_ref[...]
    variance = jnp.exp(logvar_ref[...])
    inverse = 1.0 / (length + variance)
    point_feat[...] = point_features(inducing_ref[...], []).astype(BF16)
    psi_one_ref[...] = jnp.exp2(dot(point_feat[...], first_coefficients(mean, inverse), 0, 0))
    psi_low_ref[...] = psi_one_ref[...].astype(BF16)
    beta = jnp.exp(jnp.full((1, CELLS), log_beta_ref[0], F32))

    lane = lax.broadcasted_iota(jnp.int32, (BLOCK, BLOCK), 1)
    squared = lax.rem(lane, 2 * LAT) >= LAT
    high_part = lane < 2 * LAT
    ones = jnp.where((lane >= 64) & (lane < 67), 1.0, 0.0)
    half_inv = (-0.5 * LOG2E) / length

    def window(o):
        at = lax.rem(d + o, DP)
        return inducing_ref[:, pl.ds(pl.multiple_of(BLOCK * at, BLOCK), BLOCK)]

    for o in range(SPAN):
        points = window(o)
        norm = jnp.sum(points * points * half_inv, axis=0, keepdims=True)
        base_ref[o] = jnp.concatenate([points] * 4, axis=0).T
        norm_ref[o] = jnp.broadcast_to(norm, (BLOCK, BLOCK)).T
    own_point = base_ref[0, pl.ds(pl.multiple_of(ROWS * group, ROWS), ROWS)]
    own_norm = norm_ref[0, pl.ds(pl.multiple_of(ROWS * group, ROWS), ROWS)]
    row_ref[0] = own_point
    row_ref[1] = own_norm

    def feature_step(i):
        row = row_ref[0, pl.ds(i, 1)]
        row_norm = row_ref[1, pl.ds(i, 1)]
        for o in range(SPAN):
            middle = 0.5 * (base_ref[o] + row)
            value = jnp.where(squared, middle * middle, middle)
            high = value.astype(BF16).astype(F32)
            pair = split_three(norm_ref[o] + row_norm)
            extra = ones
            for k in range(3):
                extra = jnp.where(lane == 67 + k, pair[k], extra)
            offset = pl.multiple_of(lax.rem(i, 2) * WIDTH + BLOCK * o, BLOCK)
            at = pl.ds(offset, BLOCK)
            step = lax.div(i, 2)
            pair_feat[step, at, 0:128] = jnp.where(high_part, high, value - high).astype(BF16)
            pair_feat[step, at, 128:256] = jnp.where(high_part, high, extra).astype(BF16)

    each(ROWS, feature_step)

    cross = dot(proj_low[...], cell_all[0], 1, 1)
    product = psi_one_ref[...] * cross
    sum_0, sum_1, sum_2 = moments(dot(point_feat[...], product.astype(BF16), 1, 0))
    beta_sq = beta * beta
    first_ref[0:LAT] = beta_sq * inverse * (sum_1 - mean * sum_0)
    first_ref[LAT : 2 * LAT] = (
        beta_sq
        * 0.5
        * variance
        * inverse
        * (inverse * (sum_2 - 2.0 * mean * sum_1 + mean * mean * sum_0) - sum_0)
    )

    def early_step(k):
        at = lax.rem(z + 1 + k, DP_Z)
        starts = [pl.multiple_of(BLOCK * (DP_Z * h + at), BLOCK) for h in range(DP // DP_Z)]
        rows = jnp.concatenate([psi_low_ref[pl.ds(start, FIRST)] for start in starts], axis=0)
        rows = dot(rows, cell_all[0], 1, 0).astype(BF16)
        for h in range(DP // DP_Z):
            early_send[at, h] = rows[FIRST * h : FIRST * (h + 1)]

        @pl.when(k < DP_Z - 1)
        def _():
            dp_copy(EARLY, early_send.at[at], early_recv.at[z], z_peer(k)).start()

    each(DP_Z, early_step)

    def latents(kind, at):
        return lat_all[kind, lax.rem(at, DP_Z), lax.div(at, DP_Z)]

    def pair_latent_copy():
        return pair_copy(PAIR_LATENT, lat_all.at[core], lat_all.at[core])

    wait_all(LATENT, 1, lat_all.at[core, pl.ds(0, DP_Z - 1)])
    pair_latent_copy().start()
    wait_all(GRAM, 1, gram_recv.at[pl.ds(0, chips - 1)])
    weight = jnp.sum(gram_recv[...].astype(F32), axis=0)
    weight = jnp.concatenate([weight[0:ROWS], weight[ROWS:, 0 : WIDTH - HALF]], axis=1)
    weight_ref[...] = weight
    base = window(0)
    own_lane = lax.broadcasted_iota(jnp.int32, (LAT, BLOCK), 1) - ROWS * group

    def weight_step(i):
        column = jnp.sum(jnp.where(own_lane == i, base, 0.0), axis=1, keepdims=True)
        row = weight_ref[pl.ds(i, 1)]
        for o in range(SPAN):
            weight_row = row[:, BLOCK * o : BLOCK * (o + 1)]
            middle = 0.5 * (window(o) + column)
            linear = middle * weight_row
            high, low = split_two(linear)
            block = jnp.concatenate(
                [high, middle * linear, low, special(split_two(weight_row), BLOCK)[0:32]], axis=0
            )
            offset = pl.multiple_of(lax.rem(i, 2) * WIDTH + BLOCK * o, BLOCK)
            pair_cols[lax.div(i, 2), :, pl.ds(offset, BLOCK)] = block.astype(BF16)

    each(ROWS, weight_step)
    psi_acc[...] = jnp.zeros_like(psi_acc)
    trace_ref[...] = jnp.zeros_like(trace_ref)

    pair_latent_copy().wait_recv()

    def coefficient_step(at):
        cell_mean = latents(0, at)
        cell_var = jnp.exp(latents(1, at))
        inverse_w = 1.0 / (length + 2.0 * cell_var)
        inv_width[at] = inverse_w
        const = 2.0 * kernel_log + jnp.sum(
            0.5 * jnp.log(length * inverse_w) - cell_mean * cell_mean * inverse_w,
            axis=0,
            keepdims=True,
        )
        block = cell_coefficients(
            (2.0 * LOG2E) * cell_mean * inverse_w,
            (2.0 * LOG2E) * cell_var * inverse_w / length,
            LOG2E * const,
            3,
        )
        cell_coef[at] = block.astype(BF16)

    each(DP, coefficient_step)

    def cell_gradients(at):
        table = jnp.zeros((128, CELLS), F32)
        for s in range(STEPS):
            psi = jnp.exp2(dot(pair_feat[s], cell_coef[at], 1, 0))
            psi_acc[s] += psi[:, 0:128] + psi[:, 128:256]
            table = table + dot(pair_cols[s], psi.astype(BF16), 1, 0)
        mom_0 = table[96:97] + table[97:98]
        mom_1 = table[0:32] + table[64:96]
        mom_2 = table[32:64]
        cell_mean = latents(0, at)
        cell_var = jnp.exp(latents(1, at))
        inverse_w = inv_width[at]
        trace_ref[...] += mom_0
        by_mean = -beta * inverse_w * (mom_1 - cell_mean * mom_0)
        by_logvar = (
            -beta
            * cell_var
            * inverse_w
            * (
                inverse_w * (mom_2 - 2.0 * cell_mean * mom_1 + cell_mean * cell_mean * mom_0)
                - 0.5 * mom_0
            )
        )
        return by_mean, by_logvar

    def cell_step(k):
        at = cell_order(k)
        by_mean, by_logvar = cell_gradients(at)
        grad_send[at, 0:LAT] = by_mean.astype(BF16)
        grad_send[at, LAT : 2 * LAT] = by_logvar.astype(BF16)
        dp_copy(GRAD, grad_send.at[at], grad_recv.at[d], at).start()

    each(DP - 1, cell_step)

    cell_copy().wait_recv()
    side_points = inducing_ref[:, pl.ds(pl.multiple_of(BLOCK * side, BLOCK), BLOCK * DP_Z)]
    across_mean = latents(0, across)
    across_inverse = 1.0 / (length + jnp.exp(latents(1, across)))
    psi_across = jnp.exp2(
        dot(
            point_features(side_points, []).astype(BF16),
            first_coefficients(across_mean, across_inverse),
            0,
            0,
        )
    )
    psi_side[...] = psi_across.astype(BF16)

    def data_rows(at):
        start = pl.multiple_of(BLOCK * (side + at) + FIRST, FIRST)
        near = psi_low_ref[pl.ds(start, BLOCK - FIRST)]
        far = psi_side[pl.ds(pl.multiple_of(BLOCK * at + FIRST, FIRST), BLOCK - FIRST)]
        return dot(near, cell_all[0], 1, 0) + dot(far, cell_all[1], 1, 0)

    def data_step(k):
        at = lax.rem(z + 1 + k, DP_Z)
        data_send[at] = data_rows(at).astype(BF16)

    each(DP_Z - 1, data_step)

    def data_send_rows():
        def send_step(k):
            at = lax.rem(z + 1 + k, DP_Z)
            dp_copy(DATA, data_send.at[at], data_recv.at[z], z_peer(k)).start()

        every(DP_Z - 1, send_step)

    by_mean, by_logvar = cell_gradients(d)
    first_ref[0:LAT] += by_mean
    first_ref[LAT : 2 * LAT] += by_logvar

    grad_recv[d] = jnp.zeros((2 * LAT, CELLS), BF16)
    wait_all(GRAD, 1, grad_recv.at[pl.ds(0, DP - 1)])
    own_grad = first_ref[...]
    for p in range(DP):
        own_grad = own_grad + grad_recv[p].astype(F32)
    first_ref[...] = own_grad
    give = jnp.where(core == 0, own_grad[LAT : 2 * LAT], own_grad[0:LAT])
    keep = jnp.where(core == 0, own_grad[0:LAT], own_grad[LAT : 2 * LAT])
    total_row = sum_0 - 0.5 * trace_ref[...]
    total_row = total_row[:, 0:128] + total_row[:, 128:256]
    total_row = total_row - 0.5 * jnp.sum(square_tile, axis=0, keepdims=True)
    total_row = jnp.concatenate([total_row, jnp.zeros((1, 128), F32)], axis=1)
    total_tile = jnp.broadcast_to(0.125 * total_row, (8, CELLS))
    half_send[0:LAT] = give
    half_send[LAT : LAT + 8] = total_tile

    def pair_grad_copy():
        return pair_copy(PAIR_GRAD, half_send, half_recv)

    pair_grad_copy().start()

    add_lanes = jnp.ones((16, 128), BF16)
    sums = [dot(add_lanes, psi_acc[s].astype(BF16), 1, 1)[0:1] for s in range(STEPS)]
    rows = jnp.concatenate(
        [sums[i // 2][:, WIDTH * (i % 2) : WIDTH * (i % 2 + 1)] for i in range(ROWS)], axis=0
    )
    psi_all[core, place] = rows
    own_psi = psi_all.at[core, place]

    def turned_step(k):
        chip = chip_peer(k)
        for o in range(1, 4):
            pltpu.make_async_remote_copy(
                src_ref=psi_all.at[core, place, :, pl.ds(BLOCK * o, BLOCK)],
                dst_ref=turned_all.at[core, o - 1, place],
                send_sem=sems.at[TURNED, 0],
                recv_sem=sems.at[TURNED, 1],
                device_id={"dp": lax.rem(d + o, DP), "gene": 2 * chip + core},
                device_id_type=MESH,
            ).start()

    every(
        chips - 1,
        lambda k: gene_copy(PSI, own_psi, own_psi, 2 * chip_peer(k) + core).start(),
    )
    every(chips, turned_step)

    data_send_rows()

    pair_grad_copy().wait_recv()
    totals = jnp.sum(total_tile + half_recv[LAT : LAT + 8], axis=0, keepdims=True)
    part_all[place, 0:LAT] = (keep + half_recv[0:LAT]).astype(BF16)
    part_all[place, LAT : LAT + 16] = special(split_three(totals), CELLS)[0:16].astype(BF16)
    own_part = part_all.at[place]
    every(
        chips - 1,
        lambda k: gene_copy(PART, own_part, own_part, 2 * chip_peer(k) + core).start(),
    )

    wait_all(EARLY, 1, early_recv.at[pl.ds(0, DP_Z - 1)])
    early_recv[z] = early_send[z]

    def early_sum(h):
        total = early_recv[0, h].astype(F32)
        for p in range(1, DP_Z):
            total = total + early_recv[p, h].astype(F32)
        return total

    early_own[...] = early_sum(half)
    over_send[...] = early_sum(1 - half).astype(BF16)

    def over_copy():
        return dp_copy(OVER, over_send, over_recv, across)

    over_copy().start()

    data_own[FIRST:BLOCK] = data_rows(z)
    data_own[0:FIRST] = early_own[...]

    def pair_psi_copy():
        return pair_copy(PAIR_PSI, psi_all.at[core], psi_all.at[core])

    def pair_turned_copy():
        return pair_copy(PAIR_TURNED, turned_all.at[core], turned_all.at[core])

    wait_all(PSI, 1, psi_all.at[core, pl.ds(0, chips - 1)])
    pair_psi_copy().start()

    wait_all(PART, 1, part_all.at[pl.ds(0, chips - 1)])
    part_sum = jnp.sum(part_all[...].astype(F32), axis=0)
    sum_all[core] = part_sum[0:LAT]
    total_recv[d] = part_sum[LAT : LAT + 8, 0:128] + part_sum[LAT : LAT + 8, 128:256]
    own_total = total_recv.at[d]

    def pair_sum_copy():
        return pair_copy(PAIR_SUM, sum_all.at[core], sum_all.at[core])

    pair_sum_copy().start()
    every(DP - 1, lambda k: dp_copy(TOTAL, own_total, own_total, dp_peer(k)).start())

    wait_all(TURNED, 1, turned_all.at[core])
    pair_turned_copy().start()

    pair_psi_copy().wait_recv()
    psi_rows = psi_all[...].reshape(BLOCK, WIDTH).astype(BF16)
    stat = data_own[...]
    for o in range(SPAN):
        at = lax.rem(d + o, DP)
        stat = stat - dot(
            psi_rows[:, BLOCK * o : BLOCK * (o + 1)],
            proj_low[pl.ds(pl.multiple_of(BLOCK * at, BLOCK), BLOCK)],
            1,
            0,
        )
    data_own[...] = stat

    wait_all(DATA, 1, data_recv.at[pl.ds(0, DP_Z - 1)])
    over_copy().wait_recv()
    data_own[0:FIRST] += over_recv[...].astype(F32)
    late = data_own[FIRST:BLOCK]
    for k in range(DP_Z - 1):
        late = late + data_recv[lax.rem(z + 1 + k, DP_Z)].astype(F32)
    data_own[FIRST:BLOCK] = late
    stat = data_own[...]
    pair_turned_copy().wait_recv()
    for o in range(1, 4):
        at = lax.rem(d + (DP - o), DP)
        stat = stat - dot(
            turned_all[:, o - 1].reshape(BLOCK, BLOCK).astype(BF16),
            proj_low[pl.ds(pl.multiple_of(BLOCK * at, BLOCK), BLOCK)],
            0,
            0,
        )
    data_own[...] = stat * (beta[0:1, 0:1] / (CELLS * DP))
    proj_copy = pltpu.make_async_copy(data_own, proj_out, local_sem.at[0])
    proj_copy.start()

    pair_sum_copy().wait_recv()
    first_ref[0:LAT] = sum_all[0] - mean
    first_ref[LAT : 2 * LAT] = sum_all[1] - 0.5 * (variance - 1.0)
    out_copy = pltpu.make_async_copy(first_ref, latent_out, local_sem.at[1])
    out_copy.start()

    wait_all(TOTAL, 1, total_recv.at[pl.ds(0, DP - 1)])
    factor = beta[:, 0:128] / (CELLS * DP * GENES * GENE)
    amplitude = jnp.exp(jnp.full((1, 128), kernel_log, F32))
    rest = (0.5 - 0.5 * beta[:, 0:128] * amplitude) / 1024
    total_out[0] = jnp.sum(jnp.sum(total_recv[...], axis=0) * factor + rest)

    latent_across().wait_send()
    pair_gram_copy().wait_send()
    cell_copy().wait_send()
    pair_latent_copy().wait_send()
    pair_psi_copy().wait_send()
    wait_all(LATENT, 0, lat_all.at[core, pl.ds(0, DP_Z - 1)])
    wait_all(GRAM, 0, gram_recv.at[pl.ds(0, chips - 1)])
    wait_all(GRAD, 0, grad_recv.at[pl.ds(0, DP - 1)])
    over_copy().wait_send()
    wait_all(EARLY, 0, early_recv.at[pl.ds(0, DP_Z - 1)])
    wait_all(DATA, 0, data_recv.at[pl.ds(0, DP_Z - 1)])
    wait_all(PSI, 0, psi_all.at[core, pl.ds(0, chips - 1)])
    wait_all(PART, 0, part_all.at[pl.ds(0, chips - 1)])
    wait_all(TURNED, 0, turned_all.at[core])
    pair_turned_copy().wait_send()
    pair_grad_copy().wait_send()
    pair_sum_copy().wait_send()
    wait_all(TOTAL, 0, total_recv.at[pl.ds(0, DP - 1)])
    proj_copy.wait()
    out_copy.wait()


def finish(latent_ref, proj_ref, latent_out, proj_out, latent_held, proj_held, done):
    rows = BLOCK // CLOSING
    cuts = [pl.ds(rows * k, rows) for k in range(CLOSING)]
    pairs = [(proj_ref.at[c], proj_held.at[c], proj_out.at[c]) for c in cuts]
    pairs.append((latent_ref, latent_held, latent_out))
    loads = [
        pltpu.make_async_copy(src, held, done.at[0, k]) for k, (src, held, _) in enumerate(pairs)
    ]
    stores = [
        pltpu.make_async_copy(held, dst, done.at[1, k]) for k, (_, held, dst) in enumerate(pairs)
    ]
    for load in loads:
        load.start()
    for load, store in zip(loads, stores):
        load.wait()
        store.start()
    for store in stores:
        store.wait()


def on_device(
    y_pool,
    cell_index,
    latent_mean,
    latent_logvar,
    inducing,
    length_sq,
    log_var,
    log_beta,
    proj_mean,
    second_moment,
):
    smem = pl.BlockSpec(memory_space=pltpu.SMEM)
    hbm = pl.BlockSpec(memory_space=pl.ANY)
    scratch = [
        pltpu.VMEM((1, CELLS), jnp.int32),
        pltpu.VMEM((LAT, CELLS), F32),
        pltpu.VMEM((LAT, CELLS), F32),
        pltpu.VMEM((LAT, IND), F32),
        pltpu.VMEM((1, LAT), F32),
        pltpu.VMEM((IND // GENE, IND), F32),
        pltpu.VMEM((IND, GENES), F32),
        pltpu.VMEM((IND, GENES), BF16),
        pltpu.VMEM((IND, GENES), BF16),
        pltpu.VMEM((2, CELLS, GENES), BF16),
        pltpu.VMEM((DEPTH, IND), BF16),
        pltpu.VMEM((IND, CELLS), F32),
        pltpu.VMEM((IND, CELLS), BF16),
        pltpu.VMEM((DP_Z * BLOCK, CELLS), BF16),
        pltpu.VMEM((2, DP_Z, DP // DP_Z, LAT, CELLS), F32),
        pltpu.VMEM((GENE, ROWS, WIDTH), F32),
        pltpu.VMEM((GENE // 2, ROWS, WIDTH), F32),
        pltpu.VMEM((GENE // 2, 2 * ROWS, HALF), BF16),
        pltpu.VMEM((GENE // 2, 2 * ROWS, HALF), BF16),
        pltpu.VMEM((DP_Z, DP // DP_Z, FIRST, GENES), BF16),
        pltpu.VMEM((DP_Z, DP // DP_Z, FIRST, GENES), BF16),
        pltpu.VMEM((FIRST, GENES), F32),
        pltpu.VMEM((FIRST, GENES), BF16),
        pltpu.VMEM((FIRST, GENES), BF16),
        pltpu.VMEM((DP_Z, BLOCK - FIRST, GENES), BF16),
        pltpu.VMEM((DP_Z, BLOCK - FIRST, GENES), BF16),
        pltpu.VMEM((BLOCK, GENES), F32),
        pltpu.VMEM((SPAN, BLOCK, BLOCK), F32),
        pltpu.VMEM((SPAN, BLOCK, BLOCK), F32),
        pltpu.VMEM((2, ROWS, BLOCK), F32),
        pltpu.VMEM((STEPS, PAIRS, DEPTH), BF16),
        pltpu.VMEM((STEPS, 128, PAIRS), BF16),
        pltpu.VMEM((DP, DEPTH, CELLS), BF16),
        pltpu.VMEM((DP, LAT, CELLS), F32),
        pltpu.VMEM((ROWS, WIDTH), F32),
        pltpu.VMEM((STEPS, PAIRS, 128), F32),
        pltpu.VMEM((2 * LAT, CELLS), F32),
        pltpu.VMEM((1, CELLS), F32),
        pltpu.VMEM((DP, 2 * LAT, CELLS), BF16),
        pltpu.VMEM((DP, 2 * LAT, CELLS), BF16),
        pltpu.VMEM((2, GENE // 2, ROWS, WIDTH), F32),
        pltpu.VMEM((2, 3, GENE // 2, ROWS, BLOCK), F32),
        pltpu.VMEM((LAT + 8, CELLS), F32),
        pltpu.VMEM((LAT + 8, CELLS), F32),
        pltpu.VMEM((GENE // 2, LAT + 16, CELLS), BF16),
        pltpu.VMEM((2, LAT, CELLS), F32),
        pltpu.VMEM((DP, 8, 128), F32),
        pltpu.SemaphoreType.DMA((11,)),
        pltpu.SemaphoreType.DMA((KINDS, 2)),
    ]
    latent, proj, scalar = pl.pallas_call(
        kernel,
        out_shape=(
            jax.ShapeDtypeStruct((2 * LAT, CELLS), F32),
            jax.ShapeDtypeStruct((BLOCK, GENES), F32),
            jax.ShapeDtypeStruct((1,), F32),
        ),
        in_specs=[hbm] * 6 + [smem, smem, hbm, hbm],
        out_specs=(hbm, hbm, smem),
        scratch_shapes=scratch,
        compiler_params=pltpu.CompilerParams(
            collective_id=0, has_side_effects=True, vmem_limit_bytes=56 * 1024 * 1024
        ),
        name="bound_gradients",
    )(
        y_pool,
        cell_index.reshape(1, CELLS),
        latent_mean,
        latent_logvar,
        inducing,
        length_sq.reshape(1, LAT),
        log_var,
        log_beta,
        proj_mean,
        second_moment,
    )
    latent, proj = pl.pallas_call(
        finish,
        out_shape=(
            jax.ShapeDtypeStruct((2 * LAT, CELLS), F32),
            jax.ShapeDtypeStruct((BLOCK, GENES), F32),
        ),
        in_specs=[hbm, hbm],
        out_specs=(hbm, hbm),
        scratch_shapes=[
            pltpu.VMEM((2 * LAT, CELLS), F32),
            pltpu.VMEM((BLOCK, GENES), F32),
            pltpu.SemaphoreType.DMA((2, CLOSING + 1)),
        ],
        name="finish",
    )(latent, proj)
    return (latent.reshape(2, LAT, CELLS), proj, scalar)


def solution(mesh):
    in_specs = (
        P("dp", "gene"),
        P("dp"),
        P(None, "dp"),
        P(None, "dp"),
        P(),
        P(),
        P(),
        P(),
        P(None, "gene"),
        P("gene", None),
    )
    out_specs = (P(None, None, "dp"), P("dp", "gene"), P())
    return jax.shard_map(
        on_device, mesh=mesh, in_specs=in_specs, out_specs=out_specs, check_vma=False
    )
```

```python
import functools

import jax
import jax.numpy as jnp
from jax import lax
from jax.experimental import pallas as pl
from jax.experimental.pallas import tpu as pltpu
from jax.sharding import PartitionSpec as P

F32 = jnp.float32
BF16 = jnp.bfloat16
LOG2E = 1.4426950408889634
MESH = pl.DeviceIdType.MESH

DP = 8
DP_Z = 4
GENE = 16
CELLS = 256
LAT = 32
IND = 1024
GENES = 1024
BLOCK = IND // DP
ROWS = BLOCK // GENE
SPAN = 5
WIDTH = SPAN * BLOCK
STEPS = 4
SHARE = ROWS // STEPS
PAIRS = SHARE * WIDTH
DEPTH = 256
HALF = 384
CLOSING = 4
FIRST = 64
(
    LATENT,
    PAIR_LATENT,
    PAIR_GRAM,
    GRAM,
    CELL,
    GRAD,
    DATA,
    PSI,
    PAIR_PSI,
    PART,
    TURNED,
    PAIR_TURNED,
    PAIR_GRAD,
    PAIR_SUM,
    TOTAL,
    EARLY,
    OVER,
    KINDS,
) = range(18)
BLOCK_WEIGHT = (1.0, 2.0, 2.0, 2.0, 1.0)


def each(count, body):
    def step(k, carry):
        body(k)
        return carry

    lax.fori_loop(0, count, step, 0)


def every(count, body):
    for k in range(count):
        body(k)


def split_two(value):
    high = value.astype(BF16).astype(F32)
    return high, (value - high).astype(BF16).astype(F32)


def split_three(value):
    high = value.astype(BF16).astype(F32)
    rest = value - high
    mid = rest.astype(BF16).astype(F32)
    return high, mid, (rest - mid).astype(BF16).astype(F32)


def special(rows, width):
    place = lax.broadcasted_iota(jnp.int32, (64, width), 0)
    total = jnp.zeros((64, width), F32)
    for at, row in enumerate(rows):
        total = jnp.where(place == at, jnp.broadcast_to(row, (64, width)), total)
    return total


def point_features(value, extra):
    width = value.shape[1]
    high, low = split_two(value)
    square_high, square_low = split_two(value * value)
    ones = jnp.ones((1, width), F32)
    rows = [ones, ones, ones] + list(extra)
    return jnp.concatenate(
        [high, square_high, low, square_low, high, square_high, special(rows, width)], axis=0
    )


def cell_coefficients(linear, square, constant, extra):
    width = linear.shape[1]
    high, low = split_two(linear)
    square_high, square_low = split_two(square)
    rows = list(split_three(constant)) + [jnp.ones((1, width), F32)] * extra
    return jnp.concatenate(
        [high, square_high, high, square_high, low, square_low, special(rows, width)], axis=0
    )


def moments(table):
    return table[192:193], table[0:32] + table[64:96], table[32:64] + table[96:128]


def dot(left, right, left_dim, right_dim):
    return lax.dot_general(
        left, right, (((left_dim,), (right_dim,)), ((), ())), preferred_element_type=F32
    )


def kernel(
    y_hbm,
    index_hbm,
    mean_hbm,
    logvar_hbm,
    inducing_hbm,
    length_hbm,
    log_var_ref,
    log_beta_ref,
    proj_hbm,
    moment_hbm,
    latent_out,
    proj_out,
    total_out,
    index_ref,
    mean_ref,
    logvar_ref,
    inducing_ref,
    length_ref,
    moment_ref,
    proj_f32,
    proj_low,
    y_ref,
    cell_all,
    point_feat,
    psi_one_ref,
    psi_low_ref,
    psi_side,
    lat_all,
    gram_send,
    gram_pair,
    gram_out,
    gram_recv,
    early_send,
    early_recv,
    early_own,
    over_send,
    over_recv,
    data_send,
    data_recv,
    data_own,
    base_ref,
    norm_ref,
    own_norm_ref,
    pair_feat,
    pair_cols,
    cell_coef,
    inv_width,
    psi_acc,
    first_ref,
    trace_ref,
    grad_send,
    grad_recv,
    psi_all,
    turned_all,
    half_send,
    half_recv,
    part_all,
    sum_all,
    total_recv,
    local_sem,
    sems,
):
    d = lax.axis_index("dp")
    g = lax.axis_index("gene")
    z = lax.rem(d, DP_Z)
    half = lax.div(d, DP_Z)
    side = d - z
    across = lax.rem(d + DP_Z, DP)
    core = lax.rem(g, 2)
    place = lax.div(g, 2)
    group = GENE // 2 * core + place
    sibling = g + 1 - 2 * core
    chips = GENE // 2

    def remote(src, dst, axis, send_sem, recv_sem, peer):
        return pltpu.make_async_remote_copy(
            src_ref=src,
            dst_ref=dst,
            send_sem=send_sem,
            recv_sem=recv_sem,
            device_id={axis: peer},
            device_id_type=MESH,
        )

    def dp_peer(k):
        return lax.rem(d + 1 + k, DP)

    def gene_peer(k):
        return lax.rem(g + 1 + k, GENE)

    def chip_peer(k):
        return lax.rem(place + 1 + k, GENE // 2)

    def z_peer(k):
        return side + lax.rem(z + 1 + k, DP_Z)

    def cell_order(k):
        return lax.rem(side + DP_Z * (1 - lax.div(k, DP_Z)), DP) + lax.rem(z + 1 + k, DP_Z)

    def dp_copy(kind, src, dst, peer):
        return remote(src, dst, "dp", sems.at[kind, 0], sems.at[kind, 1], peer)

    def gene_copy(kind, src, dst, peer):
        return remote(src, dst, "gene", sems.at[kind, 0], sems.at[kind, 1], peer)

    def pair_copy(kind, src, dst):
        return gene_copy(kind, src, dst, sibling)

    def wait_all(kind, side_of, buffer):
        pltpu.make_async_copy(buffer, buffer, sems.at[kind, side_of]).wait()

    quarter = IND // 4
    proj_copies = [
        pltpu.make_async_copy(
            proj_hbm.at[pl.ds(quarter * k, quarter)],
            proj_f32.at[pl.ds(quarter * k, quarter)],
            local_sem.at[k],
        )
        for k in range(4)
    ]
    y_copy = pltpu.make_async_copy(y_hbm, y_ref, local_sem.at[4])
    small = [
        (mean_hbm, mean_ref),
        (logvar_hbm, logvar_ref),
        (moment_hbm, moment_ref),
        (inducing_hbm, inducing_ref),
        (index_hbm, index_ref),
        (length_hbm, length_ref),
    ]
    small_copies = [
        pltpu.make_async_copy(src, dst, local_sem.at[5 + k]) for k, (src, dst) in enumerate(small)
    ]
    for copy in small_copies[0:2] + proj_copies + small_copies[2:] + [y_copy]:
        copy.start()

    barrier = pltpu.get_barrier_semaphore()
    every(
        DP - 1,
        lambda k: pl.semaphore_signal(
            barrier, inc=1, device_id={"dp": dp_peer(k)}, device_id_type=MESH
        ),
    )
    every(
        GENE - 1,
        lambda k: pl.semaphore_signal(
            barrier, inc=1, device_id={"gene": gene_peer(k)}, device_id_type=MESH
        ),
    )
    def greet_step(k):
        pl.semaphore_signal(
            barrier,
            inc=1,
            device_id={
                "dp": lax.rem(d + DP - 1 - k // (chips - 1), DP),
                "gene": 2 * chip_peer(k % (chips - 1)) + core,
            },
            device_id_type=MESH,
        )

    every(3 * (chips - 1), greet_step)
    for copy in small_copies[0:2]:
        copy.wait()
    lat_all[core, d] = jnp.where(core == 0, mean_ref[...], logvar_ref[...])
    pl.semaphore_wait(barrier, DP + GENE - 2 + 3 * (chips - 1))

    own_latent = lat_all.at[core, d]
    every(DP - 1, lambda k: dp_copy(LATENT, own_latent, own_latent, dp_peer(k)).start())

    for k in range(4):
        proj_copies[k].wait()
        proj_low[quarter * k : quarter * (k + 1)] = proj_f32[
            quarter * k : quarter * (k + 1)
        ].astype(BF16)

    for copy in small_copies[2:]:
        copy.wait()
    own_rows = proj_low[pl.ds(pl.multiple_of(BLOCK * d, BLOCK), BLOCK)]
    row_of = lax.broadcasted_iota(jnp.int32, (BLOCK, 64), 0) + BLOCK * d
    col_of = lax.broadcasted_iota(jnp.int32, (BLOCK, 64), 1) + 64 * g
    pick_rows = jnp.where(row_of == col_of, 1.0, 0.0).astype(BF16)
    moment_cols = moment_ref[:, pl.ds(pl.multiple_of(BLOCK * d, BLOCK), BLOCK)].astype(BF16)
    for o in range(SPAN):
        at = lax.rem(d + o, DP)
        start = pl.multiple_of(BLOCK * at, BLOCK)
        gram = dot(own_rows, proj_low[pl.ds(start, BLOCK)], 1, 1)
        moment_rows = dot(pick_rows, moment_ref[:, pl.ds(start, BLOCK)].astype(BF16), 1, 0)
        to_row = lax.broadcasted_iota(jnp.int32, (64, BLOCK), 0) + 64 * g
        to_col = lax.broadcasted_iota(jnp.int32, (64, BLOCK), 1) + BLOCK * at
        to_place = jnp.where(to_row == to_col, 1.0, 0.0).astype(BF16)
        moment_part = moment_rows + dot(moment_cols, to_place, 0, 0)
        block = BLOCK_WEIGHT[o] * (gram + 0.5 * moment_part)
        gram_send[:, :, BLOCK * o : BLOCK * (o + 1)] = block.reshape(GENE, ROWS, BLOCK)

    def pair_gram_copy():
        return pair_copy(PAIR_GRAM, gram_send.at[pl.ds(chips * (1 - core), chips)], gram_pair)

    pair_gram_copy().start()

    eye_cells = lax.broadcasted_iota(jnp.int32, (CELLS, CELLS), 0) == lax.broadcasted_iota(
        jnp.int32, (CELLS, CELLS), 1
    )
    local_index = (index_ref[...] - d * IND).astype(F32)
    index_col = jnp.sum(
        jnp.where(eye_cells, jnp.broadcast_to(local_index, (CELLS, CELLS)), 0.0),
        axis=1,
        keepdims=True,
    )
    row_number = lax.broadcasted_iota(jnp.int32, (CELLS, IND), 1).astype(F32)
    one_hot = jnp.where(row_number == index_col, 1.0, 0.0).astype(BF16)
    y_copy.wait()
    cell_rows = dot(one_hot, y_ref[...], 1, 0)
    cell_all[0] = cell_rows.astype(BF16)

    pair_gram_copy().wait_recv()
    gram_sum = gram_send[pl.ds(chips * core, chips)] + gram_pair[...]
    gram_sum = jnp.concatenate([gram_sum, jnp.zeros((chips, ROWS, 128), F32)], axis=2)
    gram_out[...] = jnp.concatenate(
        [gram_sum[:, :, 0:HALF], gram_sum[:, :, HALF:]], axis=1
    ).astype(BF16)

    def gram_step(k):
        chip = chip_peer(k)
        gene_copy(GRAM, gram_out.at[chip], gram_recv.at[place], 2 * chip + core).start()

    every(chips - 1, gram_step)
    gram_recv[place] = gram_out[place]

    def cell_copy():
        return dp_copy(CELL, cell_all.at[0], cell_all.at[1], across)

    cell_copy().start()
    squares = jnp.sum((cell_rows * cell_rows).reshape(CELLS // 8, 8, GENES), axis=0)
    square_tile = functools.reduce(
        jnp.add, [squares[:, 128 * k : 128 * (k + 1)] for k in range(GENES // 128)]
    )

    kernel_log = log_var_ref[0]
    eye = lax.broadcasted_iota(jnp.int32, (LAT, LAT), 0) == lax.broadcasted_iota(
        jnp.int32, (LAT, LAT), 1
    )
    length = jnp.sum(
        jnp.where(eye, jnp.broadcast_to(length_ref[...], (LAT, LAT)), 0.0), axis=1, keepdims=True
    )

    def first_coefficients(cell_mean, inverse):
        constant = kernel_log + 0.5 * jnp.sum(
            jnp.log(length * inverse) - cell_mean * cell_mean * inverse, axis=0, keepdims=True
        )
        return cell_coefficients(
            LOG2E * cell_mean * inverse, (-0.5 * LOG2E) * inverse, LOG2E * constant, 0
        ).astype(BF16)

    mean = mean_ref[...]
    variance = jnp.exp(logvar_ref[...])
    inverse = 1.0 / (length + variance)
    point_feat[...] = point_features(inducing_ref[...], []).astype(BF16)
    psi_one_ref[...] = jnp.exp2(dot(point_feat[...], first_coefficients(mean, inverse), 0, 0))
    psi_low_ref[...] = psi_one_ref[...].astype(BF16)
    beta = jnp.exp(jnp.full((1, CELLS), log_beta_ref[0], F32))

    def early_step(k):
        at = lax.rem(z + 1 + k, DP_Z)
        starts = [pl.multiple_of(BLOCK * (DP_Z * h + at), BLOCK) for h in range(DP // DP_Z)]
        rows = jnp.concatenate([psi_low_ref[pl.ds(start, FIRST)] for start in starts], axis=0)
        rows = dot(rows, cell_all[0], 1, 0).astype(BF16)
        for h in range(DP // DP_Z):
            early_send[at, h] = rows[FIRST * h : FIRST * (h + 1)]

        @pl.when(k < DP_Z - 1)
        def _():
            dp_copy(EARLY, early_send.at[at], early_recv.at[z], z_peer(k)).start()

    each(DP_Z, early_step)

    lane = lax.broadcasted_iota(jnp.int32, (BLOCK, BLOCK), 1)
    squared = lax.rem(lane, 2 * LAT) >= LAT
    high_part = lane < 2 * LAT
    half_inv = (-0.5 * LOG2E) / length

    def window(o):
        at = lax.rem(d + o, DP)
        return inducing_ref[:, pl.ds(pl.multiple_of(BLOCK * at, BLOCK), BLOCK)]

    def in_lanes(start, parts, rest):
        place = lax.broadcasted_iota(jnp.int32, rest.shape, 1)
        for k, part in enumerate(parts):
            rest = jnp.where(place == start + k, part, rest)
        return rest

    for o in range(SPAN):
        points = window(o)
        norm = jnp.sum(points * points * half_inv, axis=0, keepdims=True)
        base_ref[o] = 0.5 * jnp.concatenate([points] * 4, axis=0).T
        norm = jnp.broadcast_to(norm, (BLOCK, BLOCK)).T
        ones = jnp.where((lane >= 64) & (lane < 67), 1.0, 0.0)
        norm_ref[o] = in_lanes(67, split_three(norm), ones)
        if o == 0:
            own_norm_ref[...] = norm
    own = pl.ds(pl.multiple_of(ROWS * group, ROWS), ROWS)
    point_rows = base_ref[0, own]
    norm_rows = in_lanes(70, split_three(own_norm_ref[own]), jnp.zeros((ROWS, BLOCK), F32))

    def feature_step(i):
        for o in range(SPAN):
            middle = base_ref[o] + point_rows[i : i + 1]
            value = jnp.where(squared, middle * middle, middle)
            high = value.astype(BF16).astype(F32)
            extra = norm_ref[o] + norm_rows[i : i + 1]
            start = WIDTH * (i % SHARE) + BLOCK * o
            at = slice(start, start + BLOCK)
            pair_feat[i // SHARE, at, 0:128] = jnp.where(high_part, high, value - high).astype(BF16)
            pair_feat[i // SHARE, at, 128:256] = jnp.where(high_part, high, extra).astype(BF16)

    every(ROWS, feature_step)

    def latents(kind, at):
        return lat_all[kind, at]

    def pair_latent_copy():
        return pair_copy(PAIR_LATENT, lat_all.at[core], lat_all.at[core])

    wait_all(LATENT, 1, lat_all.at[core, pl.ds(0, DP - 1)])
    pair_latent_copy().start()

    cross = dot(proj_low[...], cell_all[0], 1, 1)
    product = psi_one_ref[...] * cross
    sum_0, sum_1, sum_2 = moments(dot(point_feat[...], product.astype(BF16), 1, 0))
    beta_sq = beta * beta
    first_ref[0:LAT] = beta_sq * inverse * (sum_1 - mean * sum_0)
    first_ref[LAT : 2 * LAT] = (
        beta_sq
        * 0.5
        * variance
        * inverse
        * (inverse * (sum_2 - 2.0 * mean * sum_1 + mean * mean * sum_0) - sum_0)
    )

    wait_all(GRAM, 1, gram_recv.at[pl.ds(0, chips - 1)])
    weight = jnp.sum(gram_recv[...].astype(F32), axis=0)
    weight = jnp.concatenate([weight[0:ROWS], weight[ROWS:, 0 : WIDTH - HALF]], axis=1)
    base = window(0)
    own_lane = lax.broadcasted_iota(jnp.int32, (LAT, BLOCK), 1) - ROWS * group
    first_rows = lax.broadcasted_iota(jnp.int32, (LAT, BLOCK), 0)

    def weight_step(i):
        column = jnp.sum(jnp.where(own_lane == i, base, 0.0), axis=1, keepdims=True)
        for o in range(SPAN):
            weight_row = weight[i : i + 1, BLOCK * o : BLOCK * (o + 1)]
            middle = 0.5 * (window(o) + column)
            linear = middle * weight_row
            high, low = split_two(linear)
            weight_high, weight_low = split_two(weight_row)
            rest = jnp.where(first_rows == 0, weight_high, 0.0)
            rest = jnp.where(first_rows == 1, weight_low, rest)
            block = jnp.concatenate([high, middle * linear, low, rest], axis=0)
            start = WIDTH * (i % SHARE) + BLOCK * o
            pair_cols[i // SHARE, :, start : start + BLOCK] = block.astype(BF16)

    every(ROWS, weight_step)
    psi_acc[...] = jnp.zeros_like(psi_acc)
    trace_ref[...] = jnp.zeros_like(trace_ref)

    pair_latent_copy().wait_recv()

    def coefficient_step(at):
        cell_mean = latents(0, at)
        cell_var = jnp.exp(latents(1, at))
        inverse_w = 1.0 / (length + 2.0 * cell_var)
        inv_width[at] = inverse_w
        const = 2.0 * kernel_log + jnp.sum(
            0.5 * jnp.log(length * inverse_w) - cell_mean * cell_mean * inverse_w,
            axis=0,
            keepdims=True,
        )
        block = cell_coefficients(
            (2.0 * LOG2E) * cell_mean * inverse_w,
            (2.0 * LOG2E) * cell_var * inverse_w / length,
            LOG2E * const,
            6,
        )
        cell_coef[at] = block.astype(BF16)

    each(DP, coefficient_step)

    def cell_gradients(at):
        table = jnp.zeros((128, CELLS), F32)
        for s in range(STEPS):
            psi = jnp.exp2(dot(pair_feat[s], cell_coef[at], 1, 0))
            psi_acc[s] += psi[:, 0:128] + psi[:, 128:256]
            table = table + dot(pair_cols[s], psi.astype(BF16), 1, 0)
        mom_0 = table[96:97] + table[97:98]
        mom_1 = table[0:32] + table[64:96]
        mom_2 = table[32:64]
        cell_mean = latents(0, at)
        cell_var = jnp.exp(latents(1, at))
        inverse_w = inv_width[at]
        trace_ref[...] += mom_0
        by_mean = -beta * inverse_w * (mom_1 - cell_mean * mom_0)
        by_logvar = (
            -beta
            * cell_var
            * inverse_w
            * (
                inverse_w * (mom_2 - 2.0 * cell_mean * mom_1 + cell_mean * cell_mean * mom_0)
                - 0.5 * mom_0
            )
        )
        return by_mean, by_logvar

    def cell_step(k):
        at = cell_order(k)
        by_mean, by_logvar = cell_gradients(at)
        grad_send[at, 0:LAT] = by_mean.astype(BF16)
        grad_send[at, LAT : 2 * LAT] = by_logvar.astype(BF16)
        dp_copy(GRAD, grad_send.at[at], grad_recv.at[d], at).start()

    each(DP - 1, cell_step)

    cell_copy().wait_recv()
    side_points = inducing_ref[:, pl.ds(pl.multiple_of(BLOCK * side, BLOCK), BLOCK * DP_Z)]
    across_mean = latents(0, across)
    across_inverse = 1.0 / (length + jnp.exp(latents(1, across)))
    psi_across = jnp.exp2(
        dot(
            point_features(side_points, []).astype(BF16),
            first_coefficients(across_mean, across_inverse),
            0,
            0,
        )
    )
    psi_side[...] = psi_across.astype(BF16)

    def data_rows(at):
        start = pl.multiple_of(BLOCK * (side + at) + FIRST, FIRST)
        near = psi_low_ref[pl.ds(start, BLOCK - FIRST)]
        far = psi_side[pl.ds(pl.multiple_of(BLOCK * at + FIRST, FIRST), BLOCK - FIRST)]
        return dot(near, cell_all[0], 1, 0) + dot(far, cell_all[1], 1, 0)

    def data_step(k):
        at = lax.rem(z + 1 + k, DP_Z)
        data_send[at] = data_rows(at).astype(BF16)

    each(DP_Z - 1, data_step)

    def data_send_rows():
        def send_step(k):
            at = lax.rem(z + 1 + k, DP_Z)
            dp_copy(DATA, data_send.at[at], data_recv.at[z], z_peer(k)).start()

        every(DP_Z - 1, send_step)

    by_mean, by_logvar = cell_gradients(d)
    first_ref[0:LAT] += by_mean
    first_ref[LAT : 2 * LAT] += by_logvar

    grad_recv[d] = jnp.zeros((2 * LAT, CELLS), BF16)
    wait_all(GRAD, 1, grad_recv.at[pl.ds(0, DP - 1)])
    own_grad = first_ref[...]
    for p in range(DP):
        own_grad = own_grad + grad_recv[p].astype(F32)
    first_ref[...] = own_grad
    give = jnp.where(core == 0, own_grad[LAT : 2 * LAT], own_grad[0:LAT])
    keep = jnp.where(core == 0, own_grad[0:LAT], own_grad[LAT : 2 * LAT])
    total_row = sum_0 - 0.5 * trace_ref[...]
    total_row = total_row[:, 0:128] + total_row[:, 128:256]
    total_row = total_row - 0.5 * jnp.sum(square_tile, axis=0, keepdims=True)
    total_row = jnp.concatenate([total_row, jnp.zeros((1, 128), F32)], axis=1)
    total_tile = jnp.broadcast_to(0.125 * total_row, (8, CELLS))
    half_send[0:LAT] = give
    half_send[LAT : LAT + 8] = total_tile

    def pair_grad_copy():
        return pair_copy(PAIR_GRAD, half_send, half_recv)

    pair_grad_copy().start()

    add_lanes = jnp.ones((16, 128), BF16)
    sums = [dot(add_lanes, psi_acc[s].astype(BF16), 1, 1)[0:1] for s in range(STEPS)]
    rows = jnp.concatenate(
        [
            sums[i // SHARE][:, WIDTH * (i % SHARE) : WIDTH * (i % SHARE + 1)]
            for i in range(ROWS)
        ],
        axis=0,
    )
    psi_all[core, place] = rows
    own_psi = psi_all.at[core, place]

    def turned_step(k):
        chip = chip_peer(k)
        for o in range(1, 4):
            pltpu.make_async_remote_copy(
                src_ref=psi_all.at[core, place, :, pl.ds(BLOCK * o, BLOCK)],
                dst_ref=turned_all.at[core, o - 1, place],
                send_sem=sems.at[TURNED, 0],
                recv_sem=sems.at[TURNED, 1],
                device_id={"dp": lax.rem(d + o, DP), "gene": 2 * chip + core},
                device_id_type=MESH,
            ).start()

    every(
        chips - 1,
        lambda k: gene_copy(PSI, own_psi, own_psi, 2 * chip_peer(k) + core).start(),
    )
    every(chips, turned_step)

    data_send_rows()

    pair_grad_copy().wait_recv()
    totals = jnp.sum(total_tile + half_recv[LAT : LAT + 8], axis=0, keepdims=True)
    part_all[place, 0:LAT] = (keep + half_recv[0:LAT]).astype(BF16)
    part_all[place, LAT : LAT + 16] = special(split_three(totals), CELLS)[0:16].astype(BF16)
    own_part = part_all.at[place]
    every(
        chips - 1,
        lambda k: gene_copy(PART, own_part, own_part, 2 * chip_peer(k) + core).start(),
    )

    wait_all(EARLY, 1, early_recv.at[pl.ds(0, DP_Z - 1)])
    early_recv[z] = early_send[z]

    def early_sum(h):
        total = early_recv[0, h].astype(F32)
        for p in range(1, DP_Z):
            total = total + early_recv[p, h].astype(F32)
        return total

    early_own[...] = early_sum(half)
    over_send[...] = early_sum(1 - half).astype(BF16)

    def over_copy():
        return dp_copy(OVER, over_send, over_recv, across)

    over_copy().start()

    data_own[FIRST:BLOCK] = data_rows(z)
    data_own[0:FIRST] = early_own[...]

    def pair_psi_copy():
        return pair_copy(PAIR_PSI, psi_all.at[core], psi_all.at[core])

    def pair_turned_copy():
        return pair_copy(PAIR_TURNED, turned_all.at[core], turned_all.at[core])

    wait_all(PSI, 1, psi_all.at[core, pl.ds(0, chips - 1)])
    pair_psi_copy().start()

    wait_all(PART, 1, part_all.at[pl.ds(0, chips - 1)])
    part_sum = jnp.sum(part_all[...].astype(F32), axis=0)
    sum_all[core] = part_sum[0:LAT]
    total_recv[d] = part_sum[LAT : LAT + 8, 0:128] + part_sum[LAT : LAT + 8, 128:256]
    own_total = total_recv.at[d]

    def pair_sum_copy():
        return pair_copy(PAIR_SUM, sum_all.at[core], sum_all.at[core])

    pair_sum_copy().start()
    every(DP - 1, lambda k: dp_copy(TOTAL, own_total, own_total, dp_peer(k)).start())

    wait_all(TURNED, 1, turned_all.at[core])
    pair_turned_copy().start()

    pair_psi_copy().wait_recv()
    psi_rows = psi_all[...].reshape(BLOCK, WIDTH).astype(BF16)
    stat = data_own[...]
    for o in range(SPAN):
        at = lax.rem(d + o, DP)
        stat = stat - dot(
            psi_rows[:, BLOCK * o : BLOCK * (o + 1)],
            proj_low[pl.ds(pl.multiple_of(BLOCK * at, BLOCK), BLOCK)],
            1,
            0,
        )
    data_own[...] = stat

    wait_all(DATA, 1, data_recv.at[pl.ds(0, DP_Z - 1)])
    over_copy().wait_recv()
    data_own[0:FIRST] += over_recv[...].astype(F32)
    late = data_own[FIRST:BLOCK]
    for k in range(DP_Z - 1):
        late = late + data_recv[lax.rem(z + 1 + k, DP_Z)].astype(F32)
    data_own[FIRST:BLOCK] = late
    stat = data_own[...]
    pair_turned_copy().wait_recv()
    for o in range(1, 4):
        at = lax.rem(d + (DP - o), DP)
        stat = stat - dot(
            turned_all[:, o - 1].reshape(BLOCK, BLOCK).astype(BF16),
            proj_low[pl.ds(pl.multiple_of(BLOCK * at, BLOCK), BLOCK)],
            0,
            0,
        )
    data_own[...] = stat * (beta[0:1, 0:1] / (CELLS * DP))
    proj_copy = pltpu.make_async_copy(data_own, proj_out, local_sem.at[0])
    proj_copy.start()

    pair_sum_copy().wait_recv()
    first_ref[0:LAT] = sum_all[0] - mean
    first_ref[LAT : 2 * LAT] = sum_all[1] - 0.5 * (variance - 1.0)
    out_copy = pltpu.make_async_copy(first_ref, latent_out, local_sem.at[1])
    out_copy.start()

    wait_all(TOTAL, 1, total_recv.at[pl.ds(0, DP - 1)])
    factor = beta[:, 0:128] / (CELLS * DP * GENES * GENE)
    amplitude = jnp.exp(jnp.full((1, 128), kernel_log, F32))
    rest = (0.5 - 0.5 * beta[:, 0:128] * amplitude) / 1024
    total_out[0] = jnp.sum(jnp.sum(total_recv[...], axis=0) * factor + rest)

    pair_gram_copy().wait_send()
    cell_copy().wait_send()
    pair_latent_copy().wait_send()
    pair_psi_copy().wait_send()
    wait_all(LATENT, 0, lat_all.at[core, pl.ds(0, DP - 1)])
    wait_all(GRAM, 0, gram_recv.at[pl.ds(0, chips - 1)])
    wait_all(GRAD, 0, grad_recv.at[pl.ds(0, DP - 1)])
    over_copy().wait_send()
    wait_all(EARLY, 0, early_recv.at[pl.ds(0, DP_Z - 1)])
    wait_all(DATA, 0, data_recv.at[pl.ds(0, DP_Z - 1)])
    wait_all(PSI, 0, psi_all.at[core, pl.ds(0, chips - 1)])
    wait_all(PART, 0, part_all.at[pl.ds(0, chips - 1)])
    wait_all(TURNED, 0, turned_all.at[core])
    pair_turned_copy().wait_send()
    pair_grad_copy().wait_send()
    pair_sum_copy().wait_send()
    wait_all(TOTAL, 0, total_recv.at[pl.ds(0, DP - 1)])
    proj_copy.wait()
    out_copy.wait()


def finish(latent_ref, proj_ref, latent_out, proj_out, latent_held, proj_held, done):
    rows = BLOCK // CLOSING
    cuts = [pl.ds(rows * k, rows) for k in range(CLOSING)]
    pairs = [(proj_ref.at[c], proj_held.at[c], proj_out.at[c]) for c in cuts]
    pairs.append((latent_ref, latent_held, latent_out))
    loads = [
        pltpu.make_async_copy(src, held, done.at[0, k]) for k, (src, held, _) in enumerate(pairs)
    ]
    stores = [
        pltpu.make_async_copy(held, dst, done.at[1, k]) for k, (_, held, dst) in enumerate(pairs)
    ]
    for load in loads:
        load.start()
    for load, store in zip(loads, stores):
        load.wait()
        store.start()
    for store in stores:
        store.wait()


def on_device(
    y_pool,
    cell_index,
    latent_mean,
    latent_logvar,
    inducing,
    length_sq,
    log_var,
    log_beta,
    proj_mean,
    second_moment,
):
    smem = pl.BlockSpec(memory_space=pltpu.SMEM)
    hbm = pl.BlockSpec(memory_space=pl.ANY)
    scratch = [
        pltpu.VMEM((1, CELLS), jnp.int32),
        pltpu.VMEM((LAT, CELLS), F32),
        pltpu.VMEM((LAT, CELLS), F32),
        pltpu.VMEM((LAT, IND), F32),
        pltpu.VMEM((1, LAT), F32),
        pltpu.VMEM((IND // GENE, IND), F32),
        pltpu.VMEM((IND, GENES), F32),
        pltpu.VMEM((IND, GENES), BF16),
        pltpu.VMEM((IND, GENES), BF16),
        pltpu.VMEM((2, CELLS, GENES), BF16),
        pltpu.VMEM((DEPTH, IND), BF16),
        pltpu.VMEM((IND, CELLS), F32),
        pltpu.VMEM((IND, CELLS), BF16),
        pltpu.VMEM((DP_Z * BLOCK, CELLS), BF16),
        pltpu.VMEM((2, DP, LAT, CELLS), F32),
        pltpu.VMEM((GENE, ROWS, WIDTH), F32),
        pltpu.VMEM((GENE // 2, ROWS, WIDTH), F32),
        pltpu.VMEM((GENE // 2, 2 * ROWS, HALF), BF16),
        pltpu.VMEM((GENE // 2, 2 * ROWS, HALF), BF16),
        pltpu.VMEM((DP_Z, DP // DP_Z, FIRST, GENES), BF16),
        pltpu.VMEM((DP_Z, DP // DP_Z, FIRST, GENES), BF16),
        pltpu.VMEM((FIRST, GENES), F32),
        pltpu.VMEM((FIRST, GENES), BF16),
        pltpu.VMEM((FIRST, GENES), BF16),
        pltpu.VMEM((DP_Z, BLOCK - FIRST, GENES), BF16),
        pltpu.VMEM((DP_Z, BLOCK - FIRST, GENES), BF16),
        pltpu.VMEM((BLOCK, GENES), F32),
        pltpu.VMEM((SPAN, BLOCK, BLOCK), F32),
        pltpu.VMEM((SPAN, BLOCK, BLOCK), F32),
        pltpu.VMEM((BLOCK, BLOCK), F32),
        pltpu.VMEM((STEPS, PAIRS, DEPTH), BF16),
        pltpu.VMEM((STEPS, 128, PAIRS), BF16),
        pltpu.VMEM((DP, DEPTH, CELLS), BF16),
        pltpu.VMEM((DP, LAT, CELLS), F32),
        pltpu.VMEM((STEPS, PAIRS, 128), F32),
        pltpu.VMEM((2 * LAT, CELLS), F32),
        pltpu.VMEM((1, CELLS), F32),
        pltpu.VMEM((DP, 2 * LAT, CELLS), BF16),
        pltpu.VMEM((DP, 2 * LAT, CELLS), BF16),
        pltpu.VMEM((2, GENE // 2, ROWS, WIDTH), F32),
        pltpu.VMEM((2, 3, GENE // 2, ROWS, BLOCK), F32),
        pltpu.VMEM((LAT + 8, CELLS), F32),
        pltpu.VMEM((LAT + 8, CELLS), F32),
        pltpu.VMEM((GENE // 2, LAT + 16, CELLS), BF16),
        pltpu.VMEM((2, LAT, CELLS), F32),
        pltpu.VMEM((DP, 8, 128), F32),
        pltpu.SemaphoreType.DMA((11,)),
        pltpu.SemaphoreType.DMA((KINDS, 2)),
    ]
    latent, proj, scalar = pl.pallas_call(
        kernel,
        out_shape=(
            jax.ShapeDtypeStruct((2 * LAT, CELLS), F32),
            jax.ShapeDtypeStruct((BLOCK, GENES), F32),
            jax.ShapeDtypeStruct((1,), F32),
        ),
        in_specs=[hbm] * 6 + [smem, smem, hbm, hbm],
        out_specs=(hbm, hbm, smem),
        scratch_shapes=scratch,
        compiler_params=pltpu.CompilerParams(
            collective_id=0, has_side_effects=True, vmem_limit_bytes=56 * 1024 * 1024
        ),
        name="bound_gradients",
    )(
        y_pool,
        cell_index.reshape(1, CELLS),
        latent_mean,
        latent_logvar,
        inducing,
        length_sq.reshape(1, LAT),
        log_var,
        log_beta,
        proj_mean,
        second_moment,
    )
    latent, proj = pl.pallas_call(
        finish,
        out_shape=(
            jax.ShapeDtypeStruct((2 * LAT, CELLS), F32),
            jax.ShapeDtypeStruct((BLOCK, GENES), F32),
        ),
        in_specs=[hbm, hbm],
        out_specs=(hbm, hbm),
        scratch_shapes=[
            pltpu.VMEM((2 * LAT, CELLS), F32),
            pltpu.VMEM((BLOCK, GENES), F32),
            pltpu.SemaphoreType.DMA((2, CLOSING + 1)),
        ],
        name="finish",
    )(latent, proj)
    return (latent.reshape(2, LAT, CELLS), proj, scalar)


def solution(mesh):
    in_specs = (
        P("dp", "gene"),
        P("dp"),
        P(None, "dp"),
        P(None, "dp"),
        P(),
        P(),
        P(),
        P(),
        P(None, "gene"),
        P("gene", None),
    )
    out_specs = (P(None, None, "dp"), P("dp", "gene"), P())
    return jax.shard_map(
        on_device, mesh=mesh, in_specs=in_specs, out_specs=out_specs, check_vma=False
    )
```

```python
import functools

import jax
import jax.numpy as jnp
from jax import lax
from jax.experimental import pallas as pl
from jax.experimental.pallas import tpu as pltpu
from jax.sharding import PartitionSpec as P

F32 = jnp.float32
BF16 = jnp.bfloat16
LOG2E = 1.4426950408889634
MESH = pl.DeviceIdType.MESH

DP = 8
DP_Z = 4
GENE = 16
CELLS = 256
LAT = 32
IND = 1024
GENES = 1024
BLOCK = IND // DP
ROWS = BLOCK // GENE
SPAN = 5
WIDTH = SPAN * BLOCK
STEPS = 4
SHARE = ROWS // STEPS
PAIRS = SHARE * WIDTH
DEPTH = 256
HALF = 384
CLOSING = 4
FIRST = 64
(
    LATENT,
    PAIR_LATENT,
    PAIR_GRAM,
    GRAM,
    CELL,
    GRAD,
    DATA,
    PSI,
    PAIR_PSI,
    PART,
    TURNED,
    PAIR_TURNED,
    PAIR_GRAD,
    PAIR_SUM,
    TOTAL,
    EARLY,
    OVER,
    KINDS,
) = range(18)
BLOCK_WEIGHT = (1.0, 2.0, 2.0, 2.0, 1.0)


def each(count, body):
    def step(k, carry):
        body(k)
        return carry

    lax.fori_loop(0, count, step, 0)


def every(count, body):
    for k in range(count):
        body(k)


def split_two(value):
    high = value.astype(BF16).astype(F32)
    return high, (value - high).astype(BF16).astype(F32)


def split_three(value):
    high = value.astype(BF16).astype(F32)
    rest = value - high
    mid = rest.astype(BF16).astype(F32)
    return high, mid, (rest - mid).astype(BF16).astype(F32)


def special(rows, width):
    place = lax.broadcasted_iota(jnp.int32, (64, width), 0)
    total = jnp.zeros((64, width), F32)
    for at, row in enumerate(rows):
        total = jnp.where(place == at, jnp.broadcast_to(row, (64, width)), total)
    return total


def point_features(value, extra):
    width = value.shape[1]
    high, low = split_two(value)
    square_high, square_low = split_two(value * value)
    ones = jnp.ones((1, width), F32)
    rows = [ones, ones, ones] + list(extra)
    return jnp.concatenate(
        [high, square_high, low, square_low, high, square_high, special(rows, width)], axis=0
    )


def cell_coefficients(linear, square, constant, extra):
    width = linear.shape[1]
    high, low = split_two(linear)
    square_high, square_low = split_two(square)
    rows = list(split_three(constant)) + [jnp.ones((1, width), F32)] * extra
    return jnp.concatenate(
        [high, square_high, high, square_high, low, square_low, special(rows, width)], axis=0
    )


def moments(table):
    return table[192:193], table[0:32] + table[64:96], table[32:64] + table[96:128]


def dot(left, right, left_dim, right_dim):
    return lax.dot_general(
        left, right, (((left_dim,), (right_dim,)), ((), ())), preferred_element_type=F32
    )


def kernel(
    y_hbm,
    index_hbm,
    mean_hbm,
    logvar_hbm,
    inducing_hbm,
    length_hbm,
    log_var_ref,
    log_beta_ref,
    proj_hbm,
    moment_hbm,
    latent_out,
    proj_out,
    total_out,
    index_ref,
    mean_ref,
    logvar_ref,
    inducing_ref,
    length_ref,
    moment_ref,
    proj_f32,
    proj_low,
    y_ref,
    cell_all,
    point_feat,
    psi_one_ref,
    psi_low_ref,
    psi_side,
    lat_all,
    gram_send,
    gram_pair,
    gram_out,
    gram_recv,
    early_send,
    early_recv,
    early_own,
    over_send,
    over_recv,
    data_send,
    data_recv,
    data_own,
    base_ref,
    norm_ref,
    own_norm_ref,
    pair_feat,
    pair_cols,
    cell_coef,
    inv_width,
    psi_acc,
    first_ref,
    trace_ref,
    grad_send,
    grad_recv,
    psi_all,
    turned_all,
    half_send,
    half_recv,
    part_all,
    sum_all,
    total_recv,
    local_sem,
    sems,
):
    d = lax.axis_index("dp")
    g = lax.axis_index("gene")
    z = lax.rem(d, DP_Z)
    half = lax.div(d, DP_Z)
    side = d - z
    across = lax.rem(d + DP_Z, DP)
    core = lax.rem(g, 2)
    place = lax.div(g, 2)
    group = GENE // 2 * core + place
    sibling = g + 1 - 2 * core
    chips = GENE // 2

    def remote(src, dst, axis, send_sem, recv_sem, peer):
        return pltpu.make_async_remote_copy(
            src_ref=src,
            dst_ref=dst,
            send_sem=send_sem,
            recv_sem=recv_sem,
            device_id={axis: peer},
            device_id_type=MESH,
        )

    def dp_peer(k):
        return lax.rem(d + 1 + k, DP)

    def gene_peer(k):
        return lax.rem(g + 1 + k, GENE)

    def chip_peer(k):
        return lax.rem(place + 1 + k, GENE // 2)

    def z_peer(k):
        return side + lax.rem(z + 1 + k, DP_Z)

    def cell_order(k):
        far = 1 - lax.div(DP - 2 - k, DP_Z)
        return lax.rem(side + DP_Z * far, DP) + lax.rem(z + 1 + k + far, DP_Z)

    def dp_copy(kind, src, dst, peer):
        return remote(src, dst, "dp", sems.at[kind, 0], sems.at[kind, 1], peer)

    def gene_copy(kind, src, dst, peer):
        return remote(src, dst, "gene", sems.at[kind, 0], sems.at[kind, 1], peer)

    def pair_copy(kind, src, dst):
        return gene_copy(kind, src, dst, sibling)

    def wait_all(kind, side_of, buffer):
        pltpu.make_async_copy(buffer, buffer, sems.at[kind, side_of]).wait()

    quarter = IND // 4
    proj_copies = [
        pltpu.make_async_copy(
            proj_hbm.at[pl.ds(quarter * k, quarter)],
            proj_f32.at[pl.ds(quarter * k, quarter)],
            local_sem.at[k],
        )
        for k in range(4)
    ]
    y_copy = pltpu.make_async_copy(y_hbm, y_ref, local_sem.at[4])
    small = [
        (mean_hbm, mean_ref),
        (logvar_hbm, logvar_ref),
        (moment_hbm, moment_ref),
        (inducing_hbm, inducing_ref),
        (index_hbm, index_ref),
        (length_hbm, length_ref),
    ]
    small_copies = [
        pltpu.make_async_copy(src, dst, local_sem.at[5 + k]) for k, (src, dst) in enumerate(small)
    ]
    for copy in small_copies[0:2] + proj_copies + small_copies[2:] + [y_copy]:
        copy.start()

    barrier = pltpu.get_barrier_semaphore()
    every(
        DP - 1,
        lambda k: pl.semaphore_signal(
            barrier, inc=1, device_id={"dp": dp_peer(k)}, device_id_type=MESH
        ),
    )
    every(
        GENE - 1,
        lambda k: pl.semaphore_signal(
            barrier, inc=1, device_id={"gene": gene_peer(k)}, device_id_type=MESH
        ),
    )
    def greet_step(k):
        pl.semaphore_signal(
            barrier,
            inc=1,
            device_id={
                "dp": lax.rem(d + DP - 1 - k // (chips - 1), DP),
                "gene": 2 * chip_peer(k % (chips - 1)) + core,
            },
            device_id_type=MESH,
        )

    every(3 * (chips - 1), greet_step)
    for copy in small_copies[0:2]:
        copy.wait()
    lat_all[core, d] = jnp.where(core == 0, mean_ref[...], logvar_ref[...])
    pl.semaphore_wait(barrier, DP + GENE - 2 + 3 * (chips - 1))

    own_latent = lat_all.at[core, d]
    every(DP - 1, lambda k: dp_copy(LATENT, own_latent, own_latent, dp_peer(k)).start())

    for k in range(4):
        proj_copies[k].wait()
        proj_low[quarter * k : quarter * (k + 1)] = proj_f32[
            quarter * k : quarter * (k + 1)
        ].astype(BF16)

    for copy in small_copies[2:]:
        copy.wait()
    own_rows = proj_low[pl.ds(pl.multiple_of(BLOCK * d, BLOCK), BLOCK)]
    row_of = lax.broadcasted_iota(jnp.int32, (BLOCK, 64), 0) + BLOCK * d
    col_of = lax.broadcasted_iota(jnp.int32, (BLOCK, 64), 1) + 64 * g
    pick_rows = jnp.where(row_of == col_of, 1.0, 0.0).astype(BF16)
    moment_cols = moment_ref[:, pl.ds(pl.multiple_of(BLOCK * d, BLOCK), BLOCK)].astype(BF16)
    for o in range(SPAN):
        at = lax.rem(d + o, DP)
        start = pl.multiple_of(BLOCK * at, BLOCK)
        gram = dot(own_rows, proj_low[pl.ds(start, BLOCK)], 1, 1)
        moment_rows = dot(pick_rows, moment_ref[:, pl.ds(start, BLOCK)].astype(BF16), 1, 0)
        to_row = lax.broadcasted_iota(jnp.int32, (64, BLOCK), 0) + 64 * g
        to_col = lax.broadcasted_iota(jnp.int32, (64, BLOCK), 1) + BLOCK * at
        to_place = jnp.where(to_row == to_col, 1.0, 0.0).astype(BF16)
        moment_part = moment_rows + dot(moment_cols, to_place, 0, 0)
        block = BLOCK_WEIGHT[o] * (gram + 0.5 * moment_part)
        gram_send[:, :, BLOCK * o : BLOCK * (o + 1)] = block.reshape(GENE, ROWS, BLOCK)

    def pair_gram_copy():
        return pair_copy(PAIR_GRAM, gram_send.at[pl.ds(chips * (1 - core), chips)], gram_pair)

    pair_gram_copy().start()

    eye_cells = lax.broadcasted_iota(jnp.int32, (CELLS, CELLS), 0) == lax.broadcasted_iota(
        jnp.int32, (CELLS, CELLS), 1
    )
    local_index = (index_ref[...] - d * IND).astype(F32)
    index_col = jnp.sum(
        jnp.where(eye_cells, jnp.broadcast_to(local_index, (CELLS, CELLS)), 0.0),
        axis=1,
        keepdims=True,
    )
    row_number = lax.broadcasted_iota(jnp.int32, (CELLS, IND), 1).astype(F32)
    one_hot = jnp.where(row_number == index_col, 1.0, 0.0).astype(BF16)
    y_copy.wait()
    cell_rows = dot(one_hot, y_ref[...], 1, 0)
    cell_all[0] = cell_rows.astype(BF16)

    pair_gram_copy().wait_recv()
    gram_sum = gram_send[pl.ds(chips * core, chips)] + gram_pair[...]
    gram_sum = jnp.concatenate([gram_sum, jnp.zeros((chips, ROWS, 128), F32)], axis=2)
    gram_out[...] = jnp.concatenate(
        [gram_sum[:, :, 0:HALF], gram_sum[:, :, HALF:]], axis=1
    ).astype(BF16)

    def gram_step(k):
        chip = chip_peer(k)
        gene_copy(GRAM, gram_out.at[chip], gram_recv.at[place], 2 * chip + core).start()

    every(chips - 1, gram_step)
    gram_recv[place] = gram_out[place]

    def cell_copy():
        return dp_copy(CELL, cell_all.at[0], cell_all.at[1], across)

    cell_copy().start()
    squares = jnp.sum((cell_rows * cell_rows).reshape(CELLS // 8, 8, GENES), axis=0)
    square_tile = functools.reduce(
        jnp.add, [squares[:, 128 * k : 128 * (k + 1)] for k in range(GENES // 128)]
    )

    kernel_log = log_var_ref[0]
    eye = lax.broadcasted_iota(jnp.int32, (LAT, LAT), 0) == lax.broadcasted_iota(
        jnp.int32, (LAT, LAT), 1
    )
    length = jnp.sum(
        jnp.where(eye, jnp.broadcast_to(length_ref[...], (LAT, LAT)), 0.0), axis=1, keepdims=True
    )

    def first_coefficients(cell_mean, inverse):
        constant = kernel_log + 0.5 * jnp.sum(
            jnp.log(length * inverse) - cell_mean * cell_mean * inverse, axis=0, keepdims=True
        )
        return cell_coefficients(
            LOG2E * cell_mean * inverse, (-0.5 * LOG2E) * inverse, LOG2E * constant, 0
        ).astype(BF16)

    mean = mean_ref[...]
    variance = jnp.exp(logvar_ref[...])
    inverse = 1.0 / (length + variance)
    point_feat[...] = point_features(inducing_ref[...], []).astype(BF16)
    psi_one_ref[...] = jnp.exp2(dot(point_feat[...], first_coefficients(mean, inverse), 0, 0))
    psi_low_ref[...] = psi_one_ref[...].astype(BF16)
    beta = jnp.exp(jnp.full((1, CELLS), log_beta_ref[0], F32))

    def early_step(k):
        at = lax.rem(z + 1 + k, DP_Z)
        starts = [pl.multiple_of(BLOCK * (DP_Z * h + at), BLOCK) for h in range(DP // DP_Z)]
        rows = jnp.concatenate([psi_low_ref[pl.ds(start, FIRST)] for start in starts], axis=0)
        rows = dot(rows, cell_all[0], 1, 0).astype(BF16)
        for h in range(DP // DP_Z):
            early_send[at, h] = rows[FIRST * h : FIRST * (h + 1)]

        @pl.when(k < DP_Z - 1)
        def _():
            dp_copy(EARLY, early_send.at[at], early_recv.at[z], z_peer(k)).start()

    each(DP_Z, early_step)

    lane = lax.broadcasted_iota(jnp.int32, (BLOCK, BLOCK), 1)
    squared = lax.rem(lane, 2 * LAT) >= LAT
    high_part = lane < 2 * LAT
    half_inv = (-0.5 * LOG2E) / length

    def window(o):
        at = lax.rem(d + o, DP)
        return inducing_ref[:, pl.ds(pl.multiple_of(BLOCK * at, BLOCK), BLOCK)]

    def in_lanes(start, parts, rest):
        place = lax.broadcasted_iota(jnp.int32, rest.shape, 1)
        for k, part in enumerate(parts):
            rest = jnp.where(place == start + k, part, rest)
        return rest

    for o in range(SPAN):
        points = window(o)
        norm = jnp.sum(points * points * half_inv, axis=0, keepdims=True)
        base_ref[o] = 0.5 * jnp.concatenate([points] * 4, axis=0).T
        norm = jnp.broadcast_to(norm, (BLOCK, BLOCK)).T
        ones = jnp.where((lane >= 64) & (lane < 67), 1.0, 0.0)
        norm_ref[o] = in_lanes(67, split_three(norm), ones)
        if o == 0:
            own_norm_ref[...] = norm
    own = pl.ds(pl.multiple_of(ROWS * group, ROWS), ROWS)
    point_rows = base_ref[0, own]
    norm_rows = in_lanes(70, split_three(own_norm_ref[own]), jnp.zeros((ROWS, BLOCK), F32))

    def feature_step(i):
        for o in range(SPAN):
            middle = base_ref[o] + point_rows[i : i + 1]
            value = jnp.where(squared, middle * middle, middle)
            high = value.astype(BF16).astype(F32)
            extra = norm_ref[o] + norm_rows[i : i + 1]
            start = WIDTH * (i % SHARE) + BLOCK * o
            at = slice(start, start + BLOCK)
            pair_feat[i // SHARE, at, 0:128] = jnp.where(high_part, high, value - high).astype(BF16)
            pair_feat[i // SHARE, at, 128:256] = jnp.where(high_part, high, extra).astype(BF16)

    every(ROWS, feature_step)

    def latents(kind, at):
        return lat_all[kind, at]

    def pair_latent_copy():
        return pair_copy(PAIR_LATENT, lat_all.at[core], lat_all.at[core])

    wait_all(LATENT, 1, lat_all.at[core, pl.ds(0, DP - 1)])
    pair_latent_copy().start()

    cross = dot(proj_low[...], cell_all[0], 1, 1)
    product = psi_one_ref[...] * cross
    sum_0, sum_1, sum_2 = moments(dot(point_feat[...], product.astype(BF16), 1, 0))
    beta_sq = beta * beta
    first_ref[0:LAT] = beta_sq * inverse * (sum_1 - mean * sum_0)
    first_ref[LAT : 2 * LAT] = (
        beta_sq
        * 0.5
        * variance
        * inverse
        * (inverse * (sum_2 - 2.0 * mean * sum_1 + mean * mean * sum_0) - sum_0)
    )

    pair_latent_copy().wait_recv()

    def coefficient_step(at):
        cell_mean = latents(0, at)
        cell_var = jnp.exp(latents(1, at))
        inverse_w = 1.0 / (length + 2.0 * cell_var)
        inv_width[at] = inverse_w
        const = 2.0 * kernel_log + jnp.sum(
            0.5 * jnp.log(length * inverse_w) - cell_mean * cell_mean * inverse_w,
            axis=0,
            keepdims=True,
        )
        block = cell_coefficients(
            (2.0 * LOG2E) * cell_mean * inverse_w,
            (2.0 * LOG2E) * cell_var * inverse_w / length,
            LOG2E * const,
            6,
        )
        cell_coef[at] = block.astype(BF16)

    each(DP, coefficient_step)

    wait_all(GRAM, 1, gram_recv.at[pl.ds(0, chips - 1)])
    weight = jnp.sum(gram_recv[...].astype(F32), axis=0)
    weight = jnp.concatenate([weight[0:ROWS], weight[ROWS:, 0 : WIDTH - HALF]], axis=1)
    base = window(0)
    own_lane = lax.broadcasted_iota(jnp.int32, (LAT, BLOCK), 1) - ROWS * group
    first_rows = lax.broadcasted_iota(jnp.int32, (LAT, BLOCK), 0)

    def weight_step(i):
        column = jnp.sum(jnp.where(own_lane == i, base, 0.0), axis=1, keepdims=True)
        for o in range(SPAN):
            weight_row = weight[i : i + 1, BLOCK * o : BLOCK * (o + 1)]
            middle = 0.5 * (window(o) + column)
            linear = middle * weight_row
            high, low = split_two(linear)
            weight_high, weight_low = split_two(weight_row)
            rest = jnp.where(first_rows == 0, weight_high, 0.0)
            rest = jnp.where(first_rows == 1, weight_low, rest)
            block = jnp.concatenate([high, middle * linear, low, rest], axis=0)
            start = WIDTH * (i % SHARE) + BLOCK * o
            pair_cols[i // SHARE, :, start : start + BLOCK] = block.astype(BF16)

    every(ROWS, weight_step)
    psi_acc[...] = jnp.zeros_like(psi_acc)
    trace_ref[...] = jnp.zeros_like(trace_ref)

    def cell_gradients(at):
        table = jnp.zeros((128, CELLS), F32)
        for s in range(STEPS):
            psi = jnp.exp2(dot(pair_feat[s], cell_coef[at], 1, 0))
            psi_acc[s] += psi[:, 0:128] + psi[:, 128:256]
            table = table + dot(pair_cols[s], psi.astype(BF16), 1, 0)
        mom_0 = table[96:97] + table[97:98]
        mom_1 = table[0:32] + table[64:96]
        mom_2 = table[32:64]
        cell_mean = latents(0, at)
        cell_var = jnp.exp(latents(1, at))
        inverse_w = inv_width[at]
        trace_ref[...] += mom_0
        by_mean = -beta * inverse_w * (mom_1 - cell_mean * mom_0)
        by_logvar = (
            -beta
            * cell_var
            * inverse_w
            * (
                inverse_w * (mom_2 - 2.0 * cell_mean * mom_1 + cell_mean * cell_mean * mom_0)
                - 0.5 * mom_0
            )
        )
        return by_mean, by_logvar

    def cell_step(k):
        at = cell_order(k)
        by_mean, by_logvar = cell_gradients(at)
        grad_send[at, 0:LAT] = by_mean.astype(BF16)
        grad_send[at, LAT : 2 * LAT] = by_logvar.astype(BF16)
        dp_copy(GRAD, grad_send.at[at], grad_recv.at[d], at).start()

    each(DP - 1, cell_step)

    cell_copy().wait_recv()
    side_points = inducing_ref[:, pl.ds(pl.multiple_of(BLOCK * side, BLOCK), BLOCK * DP_Z)]
    across_mean = latents(0, across)
    across_inverse = 1.0 / (length + jnp.exp(latents(1, across)))
    psi_across = jnp.exp2(
        dot(
            point_features(side_points, []).astype(BF16),
            first_coefficients(across_mean, across_inverse),
            0,
            0,
        )
    )
    psi_side[...] = psi_across.astype(BF16)

    def data_rows(at):
        start = pl.multiple_of(BLOCK * (side + at) + FIRST, FIRST)
        near = psi_low_ref[pl.ds(start, BLOCK - FIRST)]
        far = psi_side[pl.ds(pl.multiple_of(BLOCK * at + FIRST, FIRST), BLOCK - FIRST)]
        return dot(near, cell_all[0], 1, 0) + dot(far, cell_all[1], 1, 0)

    def data_step(k):
        at = lax.rem(z + 1 + k, DP_Z)
        data_send[at] = data_rows(at).astype(BF16)

    each(DP_Z - 1, data_step)

    def data_send_rows():
        def send_step(k):
            at = lax.rem(z + 1 + k, DP_Z)
            dp_copy(DATA, data_send.at[at], data_recv.at[z], z_peer(k)).start()

        every(DP_Z - 1, send_step)

    by_mean, by_logvar = cell_gradients(d)
    first_ref[0:LAT] += by_mean
    first_ref[LAT : 2 * LAT] += by_logvar

    grad_recv[d] = jnp.zeros((2 * LAT, CELLS), BF16)
    wait_all(GRAD, 1, grad_recv.at[pl.ds(0, DP - 1)])
    own_grad = first_ref[...]
    for p in range(DP):
        own_grad = own_grad + grad_recv[p].astype(F32)
    first_ref[...] = own_grad
    give = jnp.where(core == 0, own_grad[LAT : 2 * LAT], own_grad[0:LAT])
    keep = jnp.where(core == 0, own_grad[0:LAT], own_grad[LAT : 2 * LAT])
    total_row = sum_0 - 0.5 * trace_ref[...]
    total_row = total_row[:, 0:128] + total_row[:, 128:256]
    total_row = total_row - 0.5 * jnp.sum(square_tile, axis=0, keepdims=True)
    total_row = jnp.concatenate([total_row, jnp.zeros((1, 128), F32)], axis=1)
    total_tile = jnp.broadcast_to(0.125 * total_row, (8, CELLS))
    half_send[0:LAT] = give
    half_send[LAT : LAT + 8] = total_tile

    def pair_grad_copy():
        return pair_copy(PAIR_GRAD, half_send, half_recv)

    pair_grad_copy().start()

    add_lanes = jnp.ones((16, 128), BF16)
    sums = [dot(add_lanes, psi_acc[s].astype(BF16), 1, 1)[0:1] for s in range(STEPS)]
    rows = jnp.concatenate(
        [
            sums[i // SHARE][:, WIDTH * (i % SHARE) : WIDTH * (i % SHARE + 1)]
            for i in range(ROWS)
        ],
        axis=0,
    )
    psi_all[core, place] = rows
    own_psi = psi_all.at[core, place]

    def turned_step(k):
        chip = chip_peer(k)
        for o in range(1, 4):
            pltpu.make_async_remote_copy(
                src_ref=psi_all.at[core, place, :, pl.ds(BLOCK * o, BLOCK)],
                dst_ref=turned_all.at[core, o - 1, place],
                send_sem=sems.at[TURNED, 0],
                recv_sem=sems.at[TURNED, 1],
                device_id={"dp": lax.rem(d + o, DP), "gene": 2 * chip + core},
                device_id_type=MESH,
            ).start()

    every(
        chips - 1,
        lambda k: gene_copy(PSI, own_psi, own_psi, 2 * chip_peer(k) + core).start(),
    )
    every(chips, turned_step)

    data_send_rows()

    pair_grad_copy().wait_recv()
    totals = jnp.sum(total_tile + half_recv[LAT : LAT + 8], axis=0, keepdims=True)
    part_all[place, 0:LAT] = (keep + half_recv[0:LAT]).astype(BF16)
    part_all[place, LAT : LAT + 16] = special(split_three(totals), CELLS)[0:16].astype(BF16)
    own_part = part_all.at[place]
    every(
        chips - 1,
        lambda k: gene_copy(PART, own_part, own_part, 2 * chip_peer(k) + core).start(),
    )

    wait_all(EARLY, 1, early_recv.at[pl.ds(0, DP_Z - 1)])
    early_recv[z] = early_send[z]

    def early_sum(h):
        total = early_recv[0, h].astype(F32)
        for p in range(1, DP_Z):
            total = total + early_recv[p, h].astype(F32)
        return total

    early_own[...] = early_sum(half)
    over_send[...] = early_sum(1 - half).astype(BF16)

    def over_copy():
        return dp_copy(OVER, over_send, over_recv, across)

    over_copy().start()

    data_own[FIRST:BLOCK] = data_rows(z)
    data_own[0:FIRST] = early_own[...]

    def pair_psi_copy():
        return pair_copy(PAIR_PSI, psi_all.at[core], psi_all.at[core])

    def pair_turned_copy():
        return pair_copy(PAIR_TURNED, turned_all.at[core], turned_all.at[core])

    wait_all(PSI, 1, psi_all.at[core, pl.ds(0, chips - 1)])
    pair_psi_copy().start()

    wait_all(PART, 1, part_all.at[pl.ds(0, chips - 1)])
    part_sum = jnp.sum(part_all[...].astype(F32), axis=0)
    sum_all[core] = part_sum[0:LAT]
    total_recv[d] = part_sum[LAT : LAT + 8, 0:128] + part_sum[LAT : LAT + 8, 128:256]
    own_total = total_recv.at[d]

    def pair_sum_copy():
        return pair_copy(PAIR_SUM, sum_all.at[core], sum_all.at[core])

    pair_sum_copy().start()
    every(DP - 1, lambda k: dp_copy(TOTAL, own_total, own_total, dp_peer(k)).start())

    wait_all(TURNED, 1, turned_all.at[core])
    pair_turned_copy().start()

    pair_psi_copy().wait_recv()
    psi_rows = psi_all[...].reshape(BLOCK, WIDTH).astype(BF16)
    stat = data_own[...]
    for o in range(SPAN):
        at = lax.rem(d + o, DP)
        stat = stat - dot(
            psi_rows[:, BLOCK * o : BLOCK * (o + 1)],
            proj_low[pl.ds(pl.multiple_of(BLOCK * at, BLOCK), BLOCK)],
            1,
            0,
        )
    data_own[...] = stat

    wait_all(DATA, 1, data_recv.at[pl.ds(0, DP_Z - 1)])
    over_copy().wait_recv()
    data_own[0:FIRST] += over_recv[...].astype(F32)
    late = data_own[FIRST:BLOCK]
    for k in range(DP_Z - 1):
        late = late + data_recv[lax.rem(z + 1 + k, DP_Z)].astype(F32)
    data_own[FIRST:BLOCK] = late
    stat = data_own[...]
    pair_turned_copy().wait_recv()
    for o in range(1, 4):
        at = lax.rem(d + (DP - o), DP)
        stat = stat - dot(
            turned_all[:, o - 1].reshape(BLOCK, BLOCK).astype(BF16),
            proj_low[pl.ds(pl.multiple_of(BLOCK * at, BLOCK), BLOCK)],
            0,
            0,
        )
    data_own[...] = stat * (beta[0:1, 0:1] / (CELLS * DP))
    proj_copy = pltpu.make_async_copy(data_own, proj_out, local_sem.at[0])
    proj_copy.start()

    pair_sum_copy().wait_recv()
    first_ref[0:LAT] = sum_all[0] - mean
    first_ref[LAT : 2 * LAT] = sum_all[1] - 0.5 * (variance - 1.0)
    out_copy = pltpu.make_async_copy(first_ref, latent_out, local_sem.at[1])
    out_copy.start()

    wait_all(TOTAL, 1, total_recv.at[pl.ds(0, DP - 1)])
    factor = beta[:, 0:128] / (CELLS * DP * GENES * GENE)
    amplitude = jnp.exp(jnp.full((1, 128), kernel_log, F32))
    rest = (0.5 - 0.5 * beta[:, 0:128] * amplitude) / 1024
    total_out[0] = jnp.sum(jnp.sum(total_recv[...], axis=0) * factor + rest)

    pair_gram_copy().wait_send()
    cell_copy().wait_send()
    pair_latent_copy().wait_send()
    pair_psi_copy().wait_send()
    wait_all(LATENT, 0, lat_all.at[core, pl.ds(0, DP - 1)])
    wait_all(GRAM, 0, gram_recv.at[pl.ds(0, chips - 1)])
    wait_all(GRAD, 0, grad_recv.at[pl.ds(0, DP - 1)])
    over_copy().wait_send()
    wait_all(EARLY, 0, early_recv.at[pl.ds(0, DP_Z - 1)])
    wait_all(DATA, 0, data_recv.at[pl.ds(0, DP_Z - 1)])
    wait_all(PSI, 0, psi_all.at[core, pl.ds(0, chips - 1)])
    wait_all(PART, 0, part_all.at[pl.ds(0, chips - 1)])
    wait_all(TURNED, 0, turned_all.at[core])
    pair_turned_copy().wait_send()
    pair_grad_copy().wait_send()
    pair_sum_copy().wait_send()
    wait_all(TOTAL, 0, total_recv.at[pl.ds(0, DP - 1)])
    proj_copy.wait()
    out_copy.wait()


def finish(latent_ref, proj_ref, latent_out, proj_out, latent_held, proj_held, done):
    rows = BLOCK // CLOSING
    cuts = [pl.ds(rows * k, rows) for k in range(CLOSING)]
    pairs = [(proj_ref.at[c], proj_held.at[c], proj_out.at[c]) for c in cuts]
    pairs.append((latent_ref, latent_held, latent_out))
    loads = [
        pltpu.make_async_copy(src, held, done.at[0, k]) for k, (src, held, _) in enumerate(pairs)
    ]
    stores = [
        pltpu.make_async_copy(held, dst, done.at[1, k]) for k, (_, held, dst) in enumerate(pairs)
    ]
    for load in loads:
        load.start()
    for load, store in zip(loads, stores):
        load.wait()
        store.start()
    for store in stores:
        store.wait()


def on_device(
    y_pool,
    cell_index,
    latent_mean,
    latent_logvar,
    inducing,
    length_sq,
    log_var,
    log_beta,
    proj_mean,
    second_moment,
):
    smem = pl.BlockSpec(memory_space=pltpu.SMEM)
    hbm = pl.BlockSpec(memory_space=pl.ANY)
    scratch = [
        pltpu.VMEM((1, CELLS), jnp.int32),
        pltpu.VMEM((LAT, CELLS), F32),
        pltpu.VMEM((LAT, CELLS), F32),
        pltpu.VMEM((LAT, IND), F32),
        pltpu.VMEM((1, LAT), F32),
        pltpu.VMEM((IND // GENE, IND), F32),
        pltpu.VMEM((IND, GENES), F32),
        pltpu.VMEM((IND, GENES), BF16),
        pltpu.VMEM((IND, GENES), BF16),
        pltpu.VMEM((2, CELLS, GENES), BF16),
        pltpu.VMEM((DEPTH, IND), BF16),
        pltpu.VMEM((IND, CELLS), F32),
        pltpu.VMEM((IND, CELLS), BF16),
        pltpu.VMEM((DP_Z * BLOCK, CELLS), BF16),
        pltpu.VMEM((2, DP, LAT, CELLS), F32),
        pltpu.VMEM((GENE, ROWS, WIDTH), F32),
        pltpu.VMEM((GENE // 2, ROWS, WIDTH), F32),
        pltpu.VMEM((GENE // 2, 2 * ROWS, HALF), BF16),
        pltpu.VMEM((GENE // 2, 2 * ROWS, HALF), BF16),
        pltpu.VMEM((DP_Z, DP // DP_Z, FIRST, GENES), BF16),
        pltpu.VMEM((DP_Z, DP // DP_Z, FIRST, GENES), BF16),
        pltpu.VMEM((FIRST, GENES), F32),
        pltpu.VMEM((FIRST, GENES), BF16),
        pltpu.VMEM((FIRST, GENES), BF16),
        pltpu.VMEM((DP_Z, BLOCK - FIRST, GENES), BF16),
        pltpu.VMEM((DP_Z, BLOCK - FIRST, GENES), BF16),
        pltpu.VMEM((BLOCK, GENES), F32),
        pltpu.VMEM((SPAN, BLOCK, BLOCK), F32),
        pltpu.VMEM((SPAN, BLOCK, BLOCK), F32),
        pltpu.VMEM((BLOCK, BLOCK), F32),
        pltpu.VMEM((STEPS, PAIRS, DEPTH), BF16),
        pltpu.VMEM((STEPS, 128, PAIRS), BF16),
        pltpu.VMEM((DP, DEPTH, CELLS), BF16),
        pltpu.VMEM((DP, LAT, CELLS), F32),
        pltpu.VMEM((STEPS, PAIRS, 128), F32),
        pltpu.VMEM((2 * LAT, CELLS), F32),
        pltpu.VMEM((1, CELLS), F32),
        pltpu.VMEM((DP, 2 * LAT, CELLS), BF16),
        pltpu.VMEM((DP, 2 * LAT, CELLS), BF16),
        pltpu.VMEM((2, GENE // 2, ROWS, WIDTH), F32),
        pltpu.VMEM((2, 3, GENE // 2, ROWS, BLOCK), F32),
        pltpu.VMEM((LAT + 8, CELLS), F32),
        pltpu.VMEM((LAT + 8, CELLS), F32),
        pltpu.VMEM((GENE // 2, LAT + 16, CELLS), BF16),
        pltpu.VMEM((2, LAT, CELLS), F32),
        pltpu.VMEM((DP, 8, 128), F32),
        pltpu.SemaphoreType.DMA((11,)),
        pltpu.SemaphoreType.DMA((KINDS, 2)),
    ]
    latent, proj, scalar = pl.pallas_call(
        kernel,
        out_shape=(
            jax.ShapeDtypeStruct((2 * LAT, CELLS), F32),
            jax.ShapeDtypeStruct((BLOCK, GENES), F32),
            jax.ShapeDtypeStruct((1,), F32),
        ),
        in_specs=[hbm] * 6 + [smem, smem, hbm, hbm],
        out_specs=(hbm, hbm, smem),
        scratch_shapes=scratch,
        compiler_params=pltpu.CompilerParams(
            collective_id=0, has_side_effects=True, vmem_limit_bytes=56 * 1024 * 1024
        ),
        name="bound_gradients",
    )(
        y_pool,
        cell_index.reshape(1, CELLS),
        latent_mean,
        latent_logvar,
        inducing,
        length_sq.reshape(1, LAT),
        log_var,
        log_beta,
        proj_mean,
        second_moment,
    )
    latent, proj = pl.pallas_call(
        finish,
        out_shape=(
            jax.ShapeDtypeStruct((2 * LAT, CELLS), F32),
            jax.ShapeDtypeStruct((BLOCK, GENES), F32),
        ),
        in_specs=[hbm, hbm],
        out_specs=(hbm, hbm),
        scratch_shapes=[
            pltpu.VMEM((2 * LAT, CELLS), F32),
            pltpu.VMEM((BLOCK, GENES), F32),
            pltpu.SemaphoreType.DMA((2, CLOSING + 1)),
        ],
        name="finish",
    )(latent, proj)
    return (latent.reshape(2, LAT, CELLS), proj, scalar)


def solution(mesh):
    in_specs = (
        P("dp", "gene"),
        P("dp"),
        P(None, "dp"),
        P(None, "dp"),
        P(),
        P(),
        P(),
        P(),
        P(None, "gene"),
        P("gene", None),
    )
    out_specs = (P(None, None, "dp"), P("dp", "gene"), P())
    return jax.shard_map(
        on_device, mesh=mesh, in_specs=in_specs, out_specs=out_specs, check_vma=False
    )
```

```python
import functools

import jax
import jax.numpy as jnp
from jax import lax
from jax.experimental import pallas as pl
from jax.experimental.pallas import tpu as pltpu
from jax.sharding import PartitionSpec as P

F32 = jnp.float32
BF16 = jnp.bfloat16
LOG2E = 1.4426950408889634
MESH = pl.DeviceIdType.MESH

DP = 8
DP_Z = 4
GENE = 16
CELLS = 256
LAT = 32
IND = 1024
GENES = 1024
BLOCK = IND // DP
ROWS = BLOCK // GENE
SPAN = 5
WIDTH = SPAN * BLOCK
STEPS = 4
SHARE = ROWS // STEPS
PAIRS = SHARE * WIDTH
DEPTH = 256
HALF = 384
CLOSING = 4
FIRST = 64
(
    LATENT,
    PAIR_LATENT,
    PAIR_GRAM,
    GRAM,
    CELL,
    GRAD,
    DATA,
    PSI,
    PAIR_PSI,
    PART,
    TURNED,
    PAIR_TURNED,
    PAIR_GRAD,
    PAIR_SUM,
    TOTAL,
    EARLY,
    OVER,
    KINDS,
) = range(18)
BLOCK_WEIGHT = (1.0, 2.0, 2.0, 2.0, 1.0)


def each(count, body):
    def step(k, carry):
        body(k)
        return carry

    lax.fori_loop(0, count, step, 0)


def every(count, body):
    for k in range(count):
        body(k)


def split_two(value):
    high = value.astype(BF16).astype(F32)
    return high, (value - high).astype(BF16).astype(F32)


def split_three(value):
    high = value.astype(BF16).astype(F32)
    rest = value - high
    mid = rest.astype(BF16).astype(F32)
    return high, mid, (rest - mid).astype(BF16).astype(F32)


def special(rows, width):
    place = lax.broadcasted_iota(jnp.int32, (64, width), 0)
    total = jnp.zeros((64, width), F32)
    for at, row in enumerate(rows):
        total = jnp.where(place == at, jnp.broadcast_to(row, (64, width)), total)
    return total


def point_features(value, extra):
    width = value.shape[1]
    high, low = split_two(value)
    square_high, square_low = split_two(value * value)
    ones = jnp.ones((1, width), F32)
    rows = [ones, ones, ones] + list(extra)
    return jnp.concatenate(
        [high, square_high, low, square_low, high, square_high, special(rows, width)], axis=0
    )


def cell_coefficients(linear, square, constant, extra):
    width = linear.shape[1]
    high, low = split_two(linear)
    square_high, square_low = split_two(square)
    rows = list(split_three(constant)) + [jnp.ones((1, width), F32)] * extra
    return jnp.concatenate(
        [high, square_high, high, square_high, low, square_low, special(rows, width)], axis=0
    )


def moments(table):
    return table[192:193], table[0:32] + table[64:96], table[32:64] + table[96:128]


def dot(left, right, left_dim, right_dim):
    return lax.dot_general(
        left, right, (((left_dim,), (right_dim,)), ((), ())), preferred_element_type=F32
    )


def kernel(
    y_hbm,
    index_hbm,
    mean_hbm,
    logvar_hbm,
    inducing_hbm,
    length_hbm,
    log_var_ref,
    log_beta_ref,
    proj_hbm,
    moment_hbm,
    latent_out,
    proj_out,
    total_out,
    index_ref,
    mean_ref,
    logvar_ref,
    inducing_ref,
    length_ref,
    moment_ref,
    proj_f32,
    proj_low,
    y_ref,
    cell_all,
    point_feat,
    psi_one_ref,
    psi_low_ref,
    psi_side,
    lat_all,
    gram_send,
    gram_pair,
    gram_out,
    gram_recv,
    early_send,
    early_recv,
    early_own,
    over_send,
    over_recv,
    data_send,
    data_recv,
    data_own,
    base_ref,
    norm_ref,
    own_norm_ref,
    pair_feat,
    pair_cols,
    cell_coef,
    inv_width,
    psi_acc,
    first_ref,
    trace_ref,
    grad_send,
    grad_recv,
    psi_all,
    turned_all,
    half_send,
    half_recv,
    part_all,
    sum_all,
    total_recv,
    local_sem,
    sems,
):
    d = lax.axis_index("dp")
    g = lax.axis_index("gene")
    z = lax.rem(d, DP_Z)
    half = lax.div(d, DP_Z)
    side = d - z
    across = lax.rem(d + DP_Z, DP)
    core = lax.rem(g, 2)
    place = lax.div(g, 2)
    group = GENE // 2 * core + place
    sibling = g + 1 - 2 * core
    chips = GENE // 2

    def remote(src, dst, axis, send_sem, recv_sem, peer):
        return pltpu.make_async_remote_copy(
            src_ref=src,
            dst_ref=dst,
            send_sem=send_sem,
            recv_sem=recv_sem,
            device_id={axis: peer},
            device_id_type=MESH,
        )

    def dp_peer(k):
        return lax.rem(d + 1 + k, DP)

    def gene_peer(k):
        return lax.rem(g + 1 + k, GENE)

    def chip_peer(k):
        return lax.rem(place + 1 + k, GENE // 2)

    def z_peer(k):
        return side + lax.rem(z + 1 + k, DP_Z)

    def cell_order(k):
        far = 1 - lax.div(DP - 2 - k, DP_Z)
        return lax.rem(side + DP_Z * far, DP) + lax.rem(z + 1 + k + far, DP_Z)

    def dp_copy(kind, src, dst, peer):
        return remote(src, dst, "dp", sems.at[kind, 0], sems.at[kind, 1], peer)

    def gene_copy(kind, src, dst, peer):
        return remote(src, dst, "gene", sems.at[kind, 0], sems.at[kind, 1], peer)

    def pair_copy(kind, src, dst):
        return gene_copy(kind, src, dst, sibling)

    def wait_all(kind, side_of, buffer):
        pltpu.make_async_copy(buffer, buffer, sems.at[kind, side_of]).wait()

    quarter = IND // 4
    proj_copies = [
        pltpu.make_async_copy(
            proj_hbm.at[pl.ds(quarter * k, quarter)],
            proj_f32.at[pl.ds(quarter * k, quarter)],
            local_sem.at[k],
        )
        for k in range(4)
    ]
    y_copy = pltpu.make_async_copy(y_hbm, y_ref, local_sem.at[4])
    small = [
        (mean_hbm, mean_ref),
        (logvar_hbm, logvar_ref),
        (moment_hbm, moment_ref),
        (inducing_hbm, inducing_ref),
        (index_hbm, index_ref),
        (length_hbm, length_ref),
    ]
    small_copies = [
        pltpu.make_async_copy(src, dst, local_sem.at[5 + k]) for k, (src, dst) in enumerate(small)
    ]
    for copy in small_copies[0:2] + proj_copies + small_copies[2:] + [y_copy]:
        copy.start()

    barrier = pltpu.get_barrier_semaphore()
    every(
        DP - 1,
        lambda k: pl.semaphore_signal(
            barrier, inc=1, device_id={"dp": dp_peer(k)}, device_id_type=MESH
        ),
    )
    every(
        GENE - 1,
        lambda k: pl.semaphore_signal(
            barrier, inc=1, device_id={"gene": gene_peer(k)}, device_id_type=MESH
        ),
    )
    def greet_step(k):
        pl.semaphore_signal(
            barrier,
            inc=1,
            device_id={
                "dp": lax.rem(d + DP - 1 - k // (chips - 1), DP),
                "gene": 2 * chip_peer(k % (chips - 1)) + core,
            },
            device_id_type=MESH,
        )

    every(3 * (chips - 1), greet_step)
    for copy in small_copies[0:2]:
        copy.wait()
    lat_all[core, d] = jnp.where(core == 0, mean_ref[...], logvar_ref[...])
    pl.semaphore_wait(barrier, DP + GENE - 2 + 3 * (chips - 1))

    own_latent = lat_all.at[core, d]
    every(DP - 1, lambda k: dp_copy(LATENT, own_latent, own_latent, dp_peer(k)).start())

    for k in range(4):
        proj_copies[k].wait()
        proj_low[quarter * k : quarter * (k + 1)] = proj_f32[
            quarter * k : quarter * (k + 1)
        ].astype(BF16)

    for copy in small_copies[2:]:
        copy.wait()
    own_rows = proj_low[pl.ds(pl.multiple_of(BLOCK * d, BLOCK), BLOCK)]
    row_of = lax.broadcasted_iota(jnp.int32, (BLOCK, 64), 0) + BLOCK * d
    col_of = lax.broadcasted_iota(jnp.int32, (BLOCK, 64), 1) + 64 * g
    pick_rows = jnp.where(row_of == col_of, 1.0, 0.0).astype(BF16)
    moment_cols = moment_ref[:, pl.ds(pl.multiple_of(BLOCK * d, BLOCK), BLOCK)].astype(BF16)
    for o in range(SPAN):
        at = lax.rem(d + o, DP)
        start = pl.multiple_of(BLOCK * at, BLOCK)
        gram = dot(own_rows, proj_low[pl.ds(start, BLOCK)], 1, 1)
        moment_rows = dot(pick_rows, moment_ref[:, pl.ds(start, BLOCK)].astype(BF16), 1, 0)
        to_row = lax.broadcasted_iota(jnp.int32, (64, BLOCK), 0) + 64 * g
        to_col = lax.broadcasted_iota(jnp.int32, (64, BLOCK), 1) + BLOCK * at
        to_place = jnp.where(to_row == to_col, 1.0, 0.0).astype(BF16)
        moment_part = moment_rows + dot(moment_cols, to_place, 0, 0)
        block = BLOCK_WEIGHT[o] * (gram + 0.5 * moment_part)
        gram_send[:, :, BLOCK * o : BLOCK * (o + 1)] = block.reshape(GENE, ROWS, BLOCK)

    def pair_gram_copy():
        return pair_copy(PAIR_GRAM, gram_send.at[pl.ds(chips * (1 - core), chips)], gram_pair)

    pair_gram_copy().start()

    eye_cells = lax.broadcasted_iota(jnp.int32, (CELLS, CELLS), 0) == lax.broadcasted_iota(
        jnp.int32, (CELLS, CELLS), 1
    )
    local_index = (index_ref[...] - d * IND).astype(F32)
    index_col = jnp.sum(
        jnp.where(eye_cells, jnp.broadcast_to(local_index, (CELLS, CELLS)), 0.0),
        axis=1,
        keepdims=True,
    )
    row_number = lax.broadcasted_iota(jnp.int32, (CELLS, IND), 1).astype(F32)
    one_hot = jnp.where(row_number == index_col, 1.0, 0.0).astype(BF16)
    y_copy.wait()
    cell_rows = dot(one_hot, y_ref[...], 1, 0)
    cell_all[0] = cell_rows.astype(BF16)

    pair_gram_copy().wait_recv()
    gram_sum = gram_send[pl.ds(chips * core, chips)] + gram_pair[...]
    gram_sum = jnp.concatenate([gram_sum, jnp.zeros((chips, ROWS, 128), F32)], axis=2)
    gram_out[...] = jnp.concatenate(
        [gram_sum[:, :, 0:HALF], gram_sum[:, :, HALF:]], axis=1
    ).astype(BF16)

    def gram_step(k):
        chip = chip_peer(k)
        gene_copy(GRAM, gram_out.at[chip], gram_recv.at[place], 2 * chip + core).start()

    every(chips - 1, gram_step)
    gram_recv[place] = gram_out[place]

    def cell_copy():
        return dp_copy(CELL, cell_all.at[0], cell_all.at[1], across)

    cell_copy().start()
    squares = jnp.sum((cell_rows * cell_rows).reshape(CELLS // 8, 8, GENES), axis=0)
    square_tile = functools.reduce(
        jnp.add, [squares[:, 128 * k : 128 * (k + 1)] for k in range(GENES // 128)]
    )

    kernel_log = log_var_ref[0]
    eye = lax.broadcasted_iota(jnp.int32, (LAT, LAT), 0) == lax.broadcasted_iota(
        jnp.int32, (LAT, LAT), 1
    )
    length = jnp.sum(
        jnp.where(eye, jnp.broadcast_to(length_ref[...], (LAT, LAT)), 0.0), axis=1, keepdims=True
    )

    def first_coefficients(cell_mean, inverse):
        constant = kernel_log + 0.5 * jnp.sum(
            jnp.log(length * inverse) - cell_mean * cell_mean * inverse, axis=0, keepdims=True
        )
        return cell_coefficients(
            LOG2E * cell_mean * inverse, (-0.5 * LOG2E) * inverse, LOG2E * constant, 0
        ).astype(BF16)

    mean = mean_ref[...]
    variance = jnp.exp(logvar_ref[...])
    inverse = 1.0 / (length + variance)
    point_feat[...] = point_features(inducing_ref[...], []).astype(BF16)
    psi_one_ref[...] = jnp.exp2(dot(point_feat[...], first_coefficients(mean, inverse), 0, 0))
    psi_low_ref[...] = psi_one_ref[...].astype(BF16)
    beta = jnp.exp(jnp.full((1, CELLS), log_beta_ref[0], F32))

    def early_step(k):
        at = lax.rem(z + 1 + k, DP_Z)
        starts = [pl.multiple_of(BLOCK * (DP_Z * h + at), BLOCK) for h in range(DP // DP_Z)]
        rows = jnp.concatenate([psi_low_ref[pl.ds(start, FIRST)] for start in starts], axis=0)
        rows = dot(rows, cell_all[0], 1, 0).astype(BF16)
        for h in range(DP // DP_Z):
            early_send[at, h] = rows[FIRST * h : FIRST * (h + 1)]

        @pl.when(k < DP_Z - 1)
        def _():
            dp_copy(EARLY, early_send.at[at], early_recv.at[z], z_peer(k)).start()

    each(DP_Z, early_step)

    lane = lax.broadcasted_iota(jnp.int32, (BLOCK, BLOCK), 1)
    squared = lax.rem(lane, 2 * LAT) >= LAT
    high_part = lane < 2 * LAT
    half_inv = (-0.5 * LOG2E) / length

    def window(o):
        at = lax.rem(d + o, DP)
        return inducing_ref[:, pl.ds(pl.multiple_of(BLOCK * at, BLOCK), BLOCK)]

    def in_lanes(start, parts, rest):
        place = lax.broadcasted_iota(jnp.int32, rest.shape, 1)
        for k, part in enumerate(parts):
            rest = jnp.where(place == start + k, part, rest)
        return rest

    for o in range(SPAN):
        points = window(o)
        norm = jnp.sum(points * points * half_inv, axis=0, keepdims=True)
        base_ref[o] = 0.5 * jnp.concatenate([points] * 4, axis=0).T
        norm = jnp.broadcast_to(norm, (BLOCK, BLOCK)).T
        ones = jnp.where((lane >= 64) & (lane < 67), 1.0, 0.0)
        norm_ref[o] = in_lanes(67, split_three(norm), ones)
        if o == 0:
            own_norm_ref[...] = norm
    own = pl.ds(pl.multiple_of(ROWS * group, ROWS), ROWS)
    point_rows = base_ref[0, own]
    norm_rows = in_lanes(70, split_three(own_norm_ref[own]), jnp.zeros((ROWS, BLOCK), F32))

    def feature_step(i):
        for o in range(SPAN):
            middle = base_ref[o] + point_rows[i : i + 1]
            value = jnp.where(squared, middle * middle, middle)
            high = value.astype(BF16).astype(F32)
            extra = norm_ref[o] + norm_rows[i : i + 1]
            start = WIDTH * (i % SHARE) + BLOCK * o
            at = slice(start, start + BLOCK)
            pair_feat[i // SHARE, at, 0:128] = jnp.where(high_part, high, value - high).astype(BF16)
            pair_feat[i // SHARE, at, 128:256] = jnp.where(high_part, high, extra).astype(BF16)

    every(ROWS, feature_step)

    def latents(kind, at):
        return lat_all[kind, at]

    def pair_latent_copy():
        return pair_copy(PAIR_LATENT, lat_all.at[core], lat_all.at[core])

    wait_all(LATENT, 1, lat_all.at[core, pl.ds(0, DP - 1)])
    pair_latent_copy().start()

    cross = dot(proj_low[...], cell_all[0], 1, 1)
    product = psi_one_ref[...] * cross
    sum_0, sum_1, sum_2 = moments(dot(point_feat[...], product.astype(BF16), 1, 0))
    beta_sq = beta * beta
    first_ref[0:LAT] = beta_sq * inverse * (sum_1 - mean * sum_0)
    first_ref[LAT : 2 * LAT] = (
        beta_sq
        * 0.5
        * variance
        * inverse
        * (inverse * (sum_2 - 2.0 * mean * sum_1 + mean * mean * sum_0) - sum_0)
    )

    pair_latent_copy().wait_recv()

    def coefficient_step(at):
        cell_mean = latents(0, at)
        cell_var = jnp.exp(latents(1, at))
        inverse_w = 1.0 / (length + 2.0 * cell_var)
        inv_width[at] = inverse_w
        const = 2.0 * kernel_log + jnp.sum(
            0.5 * jnp.log(length * inverse_w) - cell_mean * cell_mean * inverse_w,
            axis=0,
            keepdims=True,
        )
        block = cell_coefficients(
            (2.0 * LOG2E) * cell_mean * inverse_w,
            (2.0 * LOG2E) * cell_var * inverse_w / length,
            LOG2E * const,
            6,
        )
        cell_coef[at] = block.astype(BF16)

    each(DP, coefficient_step)

    wait_all(GRAM, 1, gram_recv.at[pl.ds(0, chips - 1)])
    weight = jnp.sum(gram_recv[...].astype(F32), axis=0)
    weight = jnp.concatenate([weight[0:ROWS], weight[ROWS:, 0 : WIDTH - HALF]], axis=1)
    base = window(0)
    own_lane = lax.broadcasted_iota(jnp.int32, (LAT, BLOCK), 1) - ROWS * group
    first_rows = lax.broadcasted_iota(jnp.int32, (LAT, BLOCK), 0)

    def weight_step(i):
        column = jnp.sum(jnp.where(own_lane == i, base, 0.0), axis=1, keepdims=True)
        for o in range(SPAN):
            weight_row = weight[i : i + 1, BLOCK * o : BLOCK * (o + 1)]
            middle = 0.5 * (window(o) + column)
            linear = middle * weight_row
            high, low = split_two(linear)
            weight_high, weight_low = split_two(weight_row)
            rest = jnp.where(first_rows == 0, weight_high, 0.0)
            rest = jnp.where(first_rows == 1, weight_low, rest)
            block = jnp.concatenate([high, middle * linear, low, rest], axis=0)
            start = WIDTH * (i % SHARE) + BLOCK * o
            pair_cols[i // SHARE, :, start : start + BLOCK] = block.astype(BF16)

    every(ROWS, weight_step)
    psi_acc[...] = jnp.zeros_like(psi_acc)
    trace_ref[...] = jnp.zeros_like(trace_ref)

    def cell_gradients(at):
        table = jnp.zeros((128, CELLS), F32)
        for s in range(STEPS):
            psi = jnp.exp2(dot(pair_feat[s], cell_coef[at], 1, 0))
            psi_acc[s] += psi[:, 0:128] + psi[:, 128:256]
            table = table + dot(pair_cols[s], psi.astype(BF16), 1, 0)
        mom_0 = table[96:97] + table[97:98]
        mom_1 = table[0:32] + table[64:96]
        mom_2 = table[32:64]
        cell_mean = latents(0, at)
        cell_var = jnp.exp(latents(1, at))
        inverse_w = inv_width[at]
        trace_ref[...] += mom_0
        by_mean = -beta * inverse_w * (mom_1 - cell_mean * mom_0)
        by_logvar = (
            -beta
            * cell_var
            * inverse_w
            * (
                inverse_w * (mom_2 - 2.0 * cell_mean * mom_1 + cell_mean * cell_mean * mom_0)
                - 0.5 * mom_0
            )
        )
        return by_mean, by_logvar

    def cell_step(k):
        at = cell_order(k)
        by_mean, by_logvar = cell_gradients(at)
        grad_send[at, 0:LAT] = by_mean.astype(BF16)
        grad_send[at, LAT : 2 * LAT] = by_logvar.astype(BF16)
        dp_copy(GRAD, grad_send.at[at], grad_recv.at[d], at).start()

    each(DP - 1, cell_step)

    cell_copy().wait_recv()
    side_points = inducing_ref[:, pl.ds(pl.multiple_of(BLOCK * side, BLOCK), BLOCK * DP_Z)]
    across_mean = latents(0, across)
    across_inverse = 1.0 / (length + jnp.exp(latents(1, across)))
    psi_across = jnp.exp2(
        dot(
            point_features(side_points, []).astype(BF16),
            first_coefficients(across_mean, across_inverse),
            0,
            0,
        )
    )
    psi_side[...] = psi_across.astype(BF16)

    def data_rows(at):
        start = pl.multiple_of(BLOCK * (side + at) + FIRST, FIRST)
        near = psi_low_ref[pl.ds(start, BLOCK - FIRST)]
        far = psi_side[pl.ds(pl.multiple_of(BLOCK * at + FIRST, FIRST), BLOCK - FIRST)]
        return dot(near, cell_all[0], 1, 0) + dot(far, cell_all[1], 1, 0)

    def data_step(k):
        at = lax.rem(z + 1 + k, DP_Z)
        data_send[at] = data_rows(at).astype(BF16)

    each(DP_Z - 1, data_step)

    def data_send_rows():
        def send_step(k):
            at = lax.rem(z + 1 + k, DP_Z)
            dp_copy(DATA, data_send.at[at], data_recv.at[z], z_peer(k)).start()

        every(DP_Z - 1, send_step)

    data_send_rows()

    by_mean, by_logvar = cell_gradients(d)
    first_ref[0:LAT] += by_mean
    first_ref[LAT : 2 * LAT] += by_logvar

    grad_recv[d] = jnp.zeros((2 * LAT, CELLS), BF16)
    wait_all(GRAD, 1, grad_recv.at[pl.ds(0, DP - 1)])
    own_grad = first_ref[...]
    for p in range(DP):
        own_grad = own_grad + grad_recv[p].astype(F32)
    first_ref[...] = own_grad
    give = jnp.where(core == 0, own_grad[LAT : 2 * LAT], own_grad[0:LAT])
    keep = jnp.where(core == 0, own_grad[0:LAT], own_grad[LAT : 2 * LAT])
    total_row = sum_0 - 0.5 * trace_ref[...]
    total_row = total_row[:, 0:128] + total_row[:, 128:256]
    total_row = total_row - 0.5 * jnp.sum(square_tile, axis=0, keepdims=True)
    total_row = jnp.concatenate([total_row, jnp.zeros((1, 128), F32)], axis=1)
    total_tile = jnp.broadcast_to(0.125 * total_row, (8, CELLS))
    half_send[0:LAT] = give
    half_send[LAT : LAT + 8] = total_tile

    def pair_grad_copy():
        return pair_copy(PAIR_GRAD, half_send, half_recv)

    pair_grad_copy().start()

    add_lanes = jnp.ones((16, 128), BF16)
    sums = [dot(add_lanes, psi_acc[s].astype(BF16), 1, 1)[0:1] for s in range(STEPS)]
    rows = jnp.concatenate(
        [
            sums[i // SHARE][:, WIDTH * (i % SHARE) : WIDTH * (i % SHARE + 1)]
            for i in range(ROWS)
        ],
        axis=0,
    )
    psi_all[core, place] = rows
    own_psi = psi_all.at[core, place]

    def turned_step(k):
        chip = chip_peer(k)
        for o in range(1, 4):
            pltpu.make_async_remote_copy(
                src_ref=psi_all.at[core, place, :, pl.ds(BLOCK * o, BLOCK)],
                dst_ref=turned_all.at[core, o - 1, place],
                send_sem=sems.at[TURNED, 0],
                recv_sem=sems.at[TURNED, 1],
                device_id={"dp": lax.rem(d + o, DP), "gene": 2 * chip + core},
                device_id_type=MESH,
            ).start()

    every(
        chips - 1,
        lambda k: gene_copy(PSI, own_psi, own_psi, 2 * chip_peer(k) + core).start(),
    )
    every(chips, turned_step)

    pair_grad_copy().wait_recv()
    totals = jnp.sum(total_tile + half_recv[LAT : LAT + 8], axis=0, keepdims=True)
    part_all[place, 0:LAT] = (keep + half_recv[0:LAT]).astype(BF16)
    part_all[place, LAT : LAT + 16] = special(split_three(totals), CELLS)[0:16].astype(BF16)
    own_part = part_all.at[place]
    every(
        chips - 1,
        lambda k: gene_copy(PART, own_part, own_part, 2 * chip_peer(k) + core).start(),
    )

    wait_all(EARLY, 1, early_recv.at[pl.ds(0, DP_Z - 1)])
    early_recv[z] = early_send[z]

    def early_sum(h):
        total = early_recv[0, h].astype(F32)
        for p in range(1, DP_Z):
            total = total + early_recv[p, h].astype(F32)
        return total

    early_own[...] = early_sum(half)
    over_send[...] = early_sum(1 - half).astype(BF16)

    def over_copy():
        return dp_copy(OVER, over_send, over_recv, across)

    over_copy().start()

    data_own[FIRST:BLOCK] = data_rows(z)
    data_own[0:FIRST] = early_own[...]

    def pair_psi_copy():
        return pair_copy(PAIR_PSI, psi_all.at[core], psi_all.at[core])

    def pair_turned_copy():
        return pair_copy(PAIR_TURNED, turned_all.at[core], turned_all.at[core])

    wait_all(PSI, 1, psi_all.at[core, pl.ds(0, chips - 1)])
    pair_psi_copy().start()

    wait_all(PART, 1, part_all.at[pl.ds(0, chips - 1)])
    part_sum = jnp.sum(part_all[...].astype(F32), axis=0)
    sum_all[core] = part_sum[0:LAT]
    total_recv[d] = part_sum[LAT : LAT + 8, 0:128] + part_sum[LAT : LAT + 8, 128:256]
    own_total = total_recv.at[d]

    def pair_sum_copy():
        return pair_copy(PAIR_SUM, sum_all.at[core], sum_all.at[core])

    pair_sum_copy().start()
    every(DP - 1, lambda k: dp_copy(TOTAL, own_total, own_total, dp_peer(k)).start())

    wait_all(TURNED, 1, turned_all.at[core])
    pair_turned_copy().start()

    pair_psi_copy().wait_recv()
    psi_rows = psi_all[...].reshape(BLOCK, WIDTH).astype(BF16)
    stat = data_own[...]
    for o in range(SPAN):
        at = lax.rem(d + o, DP)
        stat = stat - dot(
            psi_rows[:, BLOCK * o : BLOCK * (o + 1)],
            proj_low[pl.ds(pl.multiple_of(BLOCK * at, BLOCK), BLOCK)],
            1,
            0,
        )
    data_own[...] = stat

    wait_all(DATA, 1, data_recv.at[pl.ds(0, DP_Z - 1)])
    over_copy().wait_recv()
    data_own[0:FIRST] += over_recv[...].astype(F32)
    late = data_own[FIRST:BLOCK]
    for k in range(DP_Z - 1):
        late = late + data_recv[lax.rem(z + 1 + k, DP_Z)].astype(F32)
    data_own[FIRST:BLOCK] = late
    stat = data_own[...]
    pair_turned_copy().wait_recv()
    for o in range(1, 4):
        at = lax.rem(d + (DP - o), DP)
        stat = stat - dot(
            turned_all[:, o - 1].reshape(BLOCK, BLOCK).astype(BF16),
            proj_low[pl.ds(pl.multiple_of(BLOCK * at, BLOCK), BLOCK)],
            0,
            0,
        )
    data_own[...] = stat * (beta[0:1, 0:1] / (CELLS * DP))
    proj_copy = pltpu.make_async_copy(data_own, proj_out, local_sem.at[0])
    proj_copy.start()

    pair_sum_copy().wait_recv()
    first_ref[0:LAT] = sum_all[0] - mean
    first_ref[LAT : 2 * LAT] = sum_all[1] - 0.5 * (variance - 1.0)
    out_copy = pltpu.make_async_copy(first_ref, latent_out, local_sem.at[1])
    out_copy.start()

    wait_all(TOTAL, 1, total_recv.at[pl.ds(0, DP - 1)])
    factor = beta[:, 0:128] / (CELLS * DP * GENES * GENE)
    amplitude = jnp.exp(jnp.full((1, 128), kernel_log, F32))
    rest = (0.5 - 0.5 * beta[:, 0:128] * amplitude) / 1024
    total_out[0] = jnp.sum(jnp.sum(total_recv[...], axis=0) * factor + rest)

    pair_gram_copy().wait_send()
    cell_copy().wait_send()
    pair_latent_copy().wait_send()
    pair_psi_copy().wait_send()
    wait_all(LATENT, 0, lat_all.at[core, pl.ds(0, DP - 1)])
    wait_all(GRAM, 0, gram_recv.at[pl.ds(0, chips - 1)])
    wait_all(GRAD, 0, grad_recv.at[pl.ds(0, DP - 1)])
    over_copy().wait_send()
    wait_all(EARLY, 0, early_recv.at[pl.ds(0, DP_Z - 1)])
    wait_all(DATA, 0, data_recv.at[pl.ds(0, DP_Z - 1)])
    wait_all(PSI, 0, psi_all.at[core, pl.ds(0, chips - 1)])
    wait_all(PART, 0, part_all.at[pl.ds(0, chips - 1)])
    wait_all(TURNED, 0, turned_all.at[core])
    pair_turned_copy().wait_send()
    pair_grad_copy().wait_send()
    pair_sum_copy().wait_send()
    wait_all(TOTAL, 0, total_recv.at[pl.ds(0, DP - 1)])
    proj_copy.wait()
    out_copy.wait()


def finish(latent_ref, proj_ref, latent_out, proj_out, latent_held, proj_held, done):
    rows = BLOCK // CLOSING
    cuts = [pl.ds(rows * k, rows) for k in range(CLOSING)]
    pairs = [(proj_ref.at[c], proj_held.at[c], proj_out.at[c]) for c in cuts]
    pairs.append((latent_ref, latent_held, latent_out))
    loads = [
        pltpu.make_async_copy(src, held, done.at[0, k]) for k, (src, held, _) in enumerate(pairs)
    ]
    stores = [
        pltpu.make_async_copy(held, dst, done.at[1, k]) for k, (_, held, dst) in enumerate(pairs)
    ]
    for load in loads:
        load.start()
    for load, store in zip(loads, stores):
        load.wait()
        store.start()
    for store in stores:
        store.wait()


def on_device(
    y_pool,
    cell_index,
    latent_mean,
    latent_logvar,
    inducing,
    length_sq,
    log_var,
    log_beta,
    proj_mean,
    second_moment,
):
    smem = pl.BlockSpec(memory_space=pltpu.SMEM)
    hbm = pl.BlockSpec(memory_space=pl.ANY)
    scratch = [
        pltpu.VMEM((1, CELLS), jnp.int32),
        pltpu.VMEM((LAT, CELLS), F32),
        pltpu.VMEM((LAT, CELLS), F32),
        pltpu.VMEM((LAT, IND), F32),
        pltpu.VMEM((1, LAT), F32),
        pltpu.VMEM((IND // GENE, IND), F32),
        pltpu.VMEM((IND, GENES), F32),
        pltpu.VMEM((IND, GENES), BF16),
        pltpu.VMEM((IND, GENES), BF16),
        pltpu.VMEM((2, CELLS, GENES), BF16),
        pltpu.VMEM((DEPTH, IND), BF16),
        pltpu.VMEM((IND, CELLS), F32),
        pltpu.VMEM((IND, CELLS), BF16),
        pltpu.VMEM((DP_Z * BLOCK, CELLS), BF16),
        pltpu.VMEM((2, DP, LAT, CELLS), F32),
        pltpu.VMEM((GENE, ROWS, WIDTH), F32),
        pltpu.VMEM((GENE // 2, ROWS, WIDTH), F32),
        pltpu.VMEM((GENE // 2, 2 * ROWS, HALF), BF16),
        pltpu.VMEM((GENE // 2, 2 * ROWS, HALF), BF16),
        pltpu.VMEM((DP_Z, DP // DP_Z, FIRST, GENES), BF16),
        pltpu.VMEM((DP_Z, DP // DP_Z, FIRST, GENES), BF16),
        pltpu.VMEM((FIRST, GENES), F32),
        pltpu.VMEM((FIRST, GENES), BF16),
        pltpu.VMEM((FIRST, GENES), BF16),
        pltpu.VMEM((DP_Z, BLOCK - FIRST, GENES), BF16),
        pltpu.VMEM((DP_Z, BLOCK - FIRST, GENES), BF16),
        pltpu.VMEM((BLOCK, GENES), F32),
        pltpu.VMEM((SPAN, BLOCK, BLOCK), F32),
        pltpu.VMEM((SPAN, BLOCK, BLOCK), F32),
        pltpu.VMEM((BLOCK, BLOCK), F32),
        pltpu.VMEM((STEPS, PAIRS, DEPTH), BF16),
        pltpu.VMEM((STEPS, 128, PAIRS), BF16),
        pltpu.VMEM((DP, DEPTH, CELLS), BF16),
        pltpu.VMEM((DP, LAT, CELLS), F32),
        pltpu.VMEM((STEPS, PAIRS, 128), F32),
        pltpu.VMEM((2 * LAT, CELLS), F32),
        pltpu.VMEM((1, CELLS), F32),
        pltpu.VMEM((DP, 2 * LAT, CELLS), BF16),
        pltpu.VMEM((DP, 2 * LAT, CELLS), BF16),
        pltpu.VMEM((2, GENE // 2, ROWS, WIDTH), F32),
        pltpu.VMEM((2, 3, GENE // 2, ROWS, BLOCK), F32),
        pltpu.VMEM((LAT + 8, CELLS), F32),
        pltpu.VMEM((LAT + 8, CELLS), F32),
        pltpu.VMEM((GENE // 2, LAT + 16, CELLS), BF16),
        pltpu.VMEM((2, LAT, CELLS), F32),
        pltpu.VMEM((DP, 8, 128), F32),
        pltpu.SemaphoreType.DMA((11,)),
        pltpu.SemaphoreType.DMA((KINDS, 2)),
    ]
    latent, proj, scalar = pl.pallas_call(
        kernel,
        out_shape=(
            jax.ShapeDtypeStruct((2 * LAT, CELLS), F32),
            jax.ShapeDtypeStruct((BLOCK, GENES), F32),
            jax.ShapeDtypeStruct((1,), F32),
        ),
        in_specs=[hbm] * 6 + [smem, smem, hbm, hbm],
        out_specs=(hbm, hbm, smem),
        scratch_shapes=scratch,
        compiler_params=pltpu.CompilerParams(
            collective_id=0, has_side_effects=True, vmem_limit_bytes=56 * 1024 * 1024
        ),
        name="bound_gradients",
    )(
        y_pool,
        cell_index.reshape(1, CELLS),
        latent_mean,
        latent_logvar,
        inducing,
        length_sq.reshape(1, LAT),
        log_var,
        log_beta,
        proj_mean,
        second_moment,
    )
    latent, proj = pl.pallas_call(
        finish,
        out_shape=(
            jax.ShapeDtypeStruct((2 * LAT, CELLS), F32),
            jax.ShapeDtypeStruct((BLOCK, GENES), F32),
        ),
        in_specs=[hbm, hbm],
        out_specs=(hbm, hbm),
        scratch_shapes=[
            pltpu.VMEM((2 * LAT, CELLS), F32),
            pltpu.VMEM((BLOCK, GENES), F32),
            pltpu.SemaphoreType.DMA((2, CLOSING + 1)),
        ],
        name="finish",
    )(latent, proj)
    return (latent.reshape(2, LAT, CELLS), proj, scalar)


def solution(mesh):
    in_specs = (
        P("dp", "gene"),
        P("dp"),
        P(None, "dp"),
        P(None, "dp"),
        P(),
        P(),
        P(),
        P(),
        P(None, "gene"),
        P("gene", None),
    )
    out_specs = (P(None, None, "dp"), P("dp", "gene"), P())
    return jax.shard_map(
        on_device, mesh=mesh, in_specs=in_specs, out_specs=out_specs, check_vma=False
    )
```
